32 devices in a mesh: pipe: 2 (over y), dp: 16 (over z, x, core).
Axes of the slice: x: 2, y: 2, z: 4, core: 2. Of those that a mesh axis runs over, the one named last changes fastest.
Arguments:
- embeds: bfloat16 [2, 16384, 512], P('pipe', 'dp'), may hold values from -6 to 6
- lengths: int32 [2, 64], P('pipe', 'dp'), may hold values from 5 to 200, as said below
- attn_in: bfloat16 [2, 512, 1536], P('pipe'), may hold values from -0.25 to 0.25
- attn_out: bfloat16 [2, 512, 512], P('pipe'), may hold values from -1 to 1
- cross_a: bfloat16 [2, 512, 512], P('pipe'), may hold values from -0.25 to 0.25
- cross_b: bfloat16 [2, 512, 512], P('pipe'), may hold values from -0.5 to 0.5
- ffn_up: bfloat16 [2, 512, 2048], P('pipe'), may hold values from -0.25 to 0.25
- ffn_down: bfloat16 [2, 2048, 512], P('pipe'), may hold values from -0.125 to 0.125
- norm_gains: float32 [2, 3, 512], P('pipe'), may hold values from 0.5 to 1.5
- norm_biases: float32 [2, 3, 512], P('pipe'), may hold values from -2 to 2
- cotangent: bfloat16 [16384, 512], P('dp'), may hold values from -6 to 6
Outputs:
- states: float32 [2, 16384, 512], P('pipe', 'dp')
- input_grads: float32 [2, 16384, 512], P('pipe', 'dp')
- grad_attn_in: float32 [2, 512, 1536], P('pipe')
- grad_attn_out: float32 [2, 512, 512], P('pipe')
- grad_cross_a: float32 [2, 512, 512], P('pipe')
- grad_cross_b: float32 [2, 512, 512], P('pipe')
- grad_ffn_up: float32 [2, 512, 2048], P('pipe')
- grad_ffn_down: float32 [2, 2048, 512], P('pipe')
- grad_gains: float32 [2, 3, 512], P('pipe')
- grad_biases: float32 [2, 3, 512], P('pipe')
The draws below stay inside these ranges and needn't reach their ends.
Inputs may be any that keep to these rules, and one draw needn't show every extreme that they name: Row 0 holds source lengths and row 1 target lengths; in each row some pair has length exactly 200.
All inputs are finite; a program needn't handle non-finite values.
Results may differ from the reference program's by a relative error of at most 0.024.
Values may be sent and summed in bfloat16 or wider, within the bound.
No kernel may reach another device: no remote copies, remote signals or barrier semaphores. Data moves between devices by JAX's collectives and lax.ppermute only.
A program may use at most 256 MiB of HBM per device.

```python
import jax
import jax.numpy as jnp
from jax import lax

D = 512
HEADS = 8
FF = 2048
HEAD_DIM = 64
SLOT = 256
MAXLEN = 200
MINLEN = 5
PAIRS = 64
TOKENS = 16384


def draw_lengths(key, part):
    key = jax.random.fold_in(key, 7)
    key_values, key_longest, key_shortest = jax.random.split(key, 3)
    values = jax.random.randint(key_values, (2, PAIRS), MINLEN, MAXLEN + 1)
    longest = jax.random.randint(key_longest, (2, 1), 0, PAIRS)
    shortest = jax.random.randint(key_shortest, (2, 1), 0, PAIRS)
    places = jnp.arange(PAIRS)[None, :]
    values = jnp.where(places == shortest, MINLEN, values)
    values = jnp.where(places == longest, MAXLEN, values)
    return values.astype(jnp.int32)


def levels(stream_key, shape, cuts, least, top_value):
    factor_of, own = 1.0, jax.random.fold_in(stream_key, 6)
    for dim, shards_of in cuts:
        draws = jnp.exp(jax.random.uniform(jax.random.fold_in(own, dim), (shards_of,), jnp.float32, least / len(cuts), top_value / len(cuts)))
        factor_of = factor_of * jnp.repeat(draws, shape[dim] // shards_of).reshape([-1 if axis == dim else 1 for axis in range(len(shape))])
    return factor_of


def scatter_about(key, dims, scale, most, shards=(), kind=jnp.bfloat16):
    loudness = levels(key, dims, shards, -0.22, 0.18) if shards else 1.0
    drawn = jax.random.normal(key, dims, jnp.float32) * scale * loudness
    return jnp.minimum(jnp.maximum(drawn, -most), most).astype(kind)


def setup_inputs(seed: int = 0) -> dict:
    key_of = jax.random.split(jax.random.key(seed), 12)
    embeds = scatter_about(key_of[0], (2, TOKENS, D), 1.0, 6.0, ((0, 2), (1, 16)))
    lengths = draw_lengths(jax.random.fold_in(key_of[11], 71), 0)
    attn_in = scatter_about(key_of[2], (2, D, 3 * D), D ** -0.5, 0.25, ((0, 2),))
    attn_out = scatter_about(key_of[3], (2, D, D), (D // 16) ** -0.5, 1.0, ((0, 2),))
    cross_a = scatter_about(key_of[4], (2, D, D), D ** -0.5, 0.25, ((0, 2),))
    cross_b = scatter_about(key_of[5], (2, D, D), (D // 4) ** -0.5, 0.5, ((0, 2),))
    ffn_up = scatter_about(key_of[6], (2, D, FF), D ** -0.5, 0.25, ((0, 2),))
    ffn_down = scatter_about(key_of[7], (2, FF, D), FF ** -0.5, 0.125, ((0, 2),))
    norm_gains = jnp.clip(1.0 + 0.1 * jax.random.normal(key_of[8], (2, 3, D), jnp.float32), 0.5, 1.5)
    norm_biases = scatter_about(key_of[9], (2, 3, D), 0.3, 2.0, ((0, 2),), jnp.float32)
    cotangent = scatter_about(key_of[10], (TOKENS, D), 1.0, 6.0, ((0, 16),))
    return dict(embeds=embeds, lengths=lengths, attn_in=attn_in, attn_out=attn_out, cross_a=cross_a, cross_b=cross_b, ffn_up=ffn_up, ffn_down=ffn_down, norm_gains=norm_gains, norm_biases=norm_biases, cotangent=cotangent)


@jax.custom_vjp
def low(v):
    return lax.optimization_barrier(v.astype(jnp.bfloat16)).astype(jnp.float32)

@jax.custom_vjp
def low_back(v):
    return v

def low_keep(v):
    return (low(v), None)

def low_pass(kept, grad):
    return (grad,)

def back_keep(v):
    return (v, None)

def back_low(kept, grad):
    return (low(grad),)
low.defvjp(low_keep, low_pass)
low_back.defvjp(back_keep, back_low)
NORM_EPSILON = 1e-05

def norm_rows(values, norm_gain, norm_bias):
    center = values - lax.optimization_barrier(jnp.mean(values, axis=-1, keepdims=True))
    spread = lax.optimization_barrier(jnp.mean(center * center, axis=-1, keepdims=True))
    return center * lax.rsqrt(spread + NORM_EPSILON) * norm_gain + norm_bias

def matmul(factor_a, factor_b):
    return jnp.dot(factor_a, factor_b, precision=lax.Precision.HIGHEST)

def attend(query_rows, key_rows, value_rows, key_valid):
    count = query_rows.shape[0]
    query_heads = query_rows.reshape(count, HEADS, HEAD_DIM)
    key_heads = key_rows.reshape(count, HEADS, HEAD_DIM)
    value_heads = value_rows.reshape(count, HEADS, HEAD_DIM)
    raw = low_back(jnp.einsum('qhd,khd->hqk', query_heads, key_heads, precision=lax.Precision.HIGHEST))
    scores = jnp.where(key_valid[None, None, :], raw * HEAD_DIM ** (-0.5), -1e+30)
    attn_probs = low(jax.nn.softmax(scores, axis=-1))
    mixed_out = jnp.einsum('hqk,khd->qhd', attn_probs, value_heads, precision=lax.Precision.HIGHEST)
    return mixed_out.reshape(count, HEADS * HEAD_DIM)

def self_block(stream, in_weight, out_weight, norm_gain, norm_bias, key_valid):
    projected = low(low_back(matmul(low(stream), in_weight)))
    query_rows, key_rows, value_rows = jnp.split(projected, 3, axis=-1)
    mixed_out = low(low_back(attend(query_rows, key_rows, value_rows, key_valid)))
    return norm_rows(stream + low_back(matmul(mixed_out, out_weight)), norm_gain, norm_bias)

def feed_block(stream, up_weight, down_weight, norm_gain, norm_bias):
    hidden = low_back(matmul(low(stream), up_weight))
    active = low(jax.nn.gelu(hidden, approximate=True))
    return norm_rows(stream + low_back(matmul(active, down_weight)), norm_gain, norm_bias)

def pair_forward(source, target, source_len, target_len, weights):
    in_weight, out_weight, cross_first, cross_second, up_weight, down_weight, gain_table, bias_table = weights
    places = jnp.arange(SLOT, dtype=jnp.int32)
    source_valid = places < source_len
    target_valid = places < target_len
    first_norm = self_block(source, in_weight[0], out_weight[0], gain_table[0, 0], bias_table[0, 0], source_valid)
    second_norm = feed_block(first_norm, up_weight[0], down_weight[0], gain_table[0, 1], bias_table[0, 1])
    memory = norm_rows(second_norm, gain_table[0, 2], bias_table[0, 2])
    memory_low = low(memory)
    mem_keys = low(low_back(matmul(memory_low, cross_first[0])))
    mem_values = low(low_back(matmul(memory_low, cross_second[0])))
    dec_first = self_block(target, in_weight[1], out_weight[1], gain_table[1, 0], bias_table[1, 0], target_valid)
    queries = low(low_back(matmul(low(dec_first), cross_first[1])))
    cross_out = low(low_back(attend(queries, mem_keys, mem_values, source_valid)))
    dec_second = norm_rows(dec_first + low_back(matmul(cross_out, cross_second[1])), gain_table[1, 1], bias_table[1, 1])
    dec_third = feed_block(dec_second, up_weight[1], down_weight[1], gain_table[1, 2], bias_table[1, 2])
    source_mask = source_valid[:, None].astype(memory.dtype)
    target_mask = target_valid[:, None].astype(memory.dtype)
    return (memory * source_mask, dec_third * target_mask)

def reference(embeds, lengths, attn_in, attn_out, cross_a, cross_b, ffn_up, ffn_down, norm_gains, norm_biases, cotangent):
    weights = tuple((array.astype(jnp.float32) for array in (attn_in, attn_out, cross_a, cross_b, ffn_up, ffn_down, norm_gains, norm_biases)))
    inputs = embeds.astype(jnp.float32).reshape(2, PAIRS, SLOT, D)
    cotan_pairs = cotangent.astype(jnp.float32).reshape(PAIRS, SLOT, D)

    def advance(totals, pair_item):
        source, target, source_len, target_len, cotan_pair = pair_item

        def forward_pair(source_rows, target_rows, weight_set):
            return pair_forward(source_rows, target_rows, source_len, target_len, weight_set)
        outputs, pullback = jax.vjp(forward_pair, source, target, weights)
        grad_source, grad_target, grad_weights = pullback((jnp.zeros_like(outputs[0]), cotan_pair))
        totals = jax.tree.map(jnp.add, totals, grad_weights)
        return (totals, (outputs[0], outputs[1], grad_source, grad_target))
    zero_totals = jax.tree.map(jnp.zeros_like, weights)
    totals, gathered = lax.scan(advance, zero_totals, (inputs[0], inputs[1], lengths[0], lengths[1], cotan_pairs))
    memory_all, decoded_all, source_grads, target_grads = gathered
    states = jnp.stack([memory_all.reshape(TOKENS, D), decoded_all.reshape(TOKENS, D)])
    input_grads = jnp.stack([source_grads.reshape(TOKENS, D), target_grads.reshape(TOKENS, D)])
    return (states, input_grads, totals[0], totals[1], totals[2], totals[3], totals[4], totals[5], totals[6], totals[7])
```

```python
import functools

import jax
import jax.numpy as jnp
from jax import lax
from jax.experimental import pallas as pl
from jax.experimental.pallas import tpu as pltpu
from jax.sharding import PartitionSpec as P

HEADS = 8
D = 512
FF = 2048
SLOT = 256
PR = 208
GP = 2
GR = GP * PR
TALL = 512
ALL = 896
NORM_EPSILON = 1e-05
BF = jnp.bfloat16
F32 = jnp.float32
CORE_C = 0.7978845608028654
CUBE_C = 0.044715


def dot(a, b):
    return lax.dot_general(a, b, (((1,), (0,)), ((), ())), preferred_element_type=F32)


def dot_t(a, b):
    return lax.dot_general(a, b, (((1,), (1,)), ((), ())), preferred_element_type=F32)


def dot_l(a, b):
    return lax.dot_general(a, b, (((0,), (0,)), ((), ())), preferred_element_type=F32)


def rows_at(start, size, step=16):
    return pl.ds(pl.multiple_of(start, step), size)


def loop(n, body):
    def run(i, carry):
        body(i)
        return carry

    lax.fori_loop(0, n, run, 0)


def gelu(u):
    return 0.5 * u * (1.0 + jnp.tanh(CORE_C * (u + CUBE_C * u * u * u)))


def gelu_slope(u):
    square = u * u
    bent = jnp.tanh(CORE_C * u * (1.0 + CUBE_C * square))
    return 0.5 * (1.0 + bent) + 0.5 * u * (1.0 - bent * bent) * (
        CORE_C * (1.0 + 3.0 * CUBE_C * square)
    )


def norm_of(summed):
    center = summed - jnp.mean(summed, axis=-1, keepdims=True)
    spread = jnp.mean(center * center, axis=-1, keepdims=True)
    scale = lax.rsqrt(spread + NORM_EPSILON)
    return center * scale, scale


def norm_back(grad, unit, scale, gain):
    lifted = grad * gain
    first = jnp.mean(lifted, axis=-1, keepdims=True)
    second = jnp.mean(lifted * unit, axis=-1, keepdims=True)
    return scale * (lifted - first - unit * second)


def fold8(values):
    return jnp.sum(values.reshape(-1, 8, values.shape[-1]), axis=0)


class Moves:
    def __init__(self, sems):
        self.sems = sems
        self.used = 0
        self.open = []

    def start(self, source, target):
        copy = pltpu.make_async_copy(source, target, self.sems.at[self.used])
        self.used += 1
        copy.start()
        self.open.append(copy)
        return copy

    def wait(self, *copies):
        for copy in copies:
            copy.wait()
            self.open.remove(copy)

    def finish(self):
        for copy in self.open:
            copy.wait()
        self.open = []


def lane_masks():
    lane = lax.broadcasted_iota(jnp.int32, (1, 128), 1)
    low = jnp.where(lane < 64, 1.0, 0.0).astype(BF)
    high = jnp.where(lane < 64, 0.0, 1.0).astype(BF)
    return low, high


def both_heads(rows, low, high):
    return jnp.concatenate([rows * low, rows * high], axis=0)


def merged_heads(stacked):
    lane = lax.broadcasted_iota(jnp.int32, (PR, 128), 1)
    return jnp.where(lane < 64, stacked[:PR], stacked[SLOT : SLOT + PR])


def probs_of(keys, queries, length):
    raw = dot_t(keys, queries)
    place = lax.broadcasted_iota(jnp.int32, raw.shape, 0)
    raw = jnp.where(place < length, raw, -1e30)
    top = jnp.max(raw, axis=0, keepdims=True)
    terms = jnp.exp(raw - top)
    total = jnp.sum(terms, axis=0, keepdims=True)
    return terms * (1.0 / total)


def attend_forward(length_of, q_ref, q_off, k_ref, k_off, v_ref, v_off, out_ref):
    low, high = lane_masks()
    low_q, high_q = low * 0.125, high * 0.125

    def pair(p):
        length = length_of(p)
        base = rows_at(p * PR, PR)
        wide = rows_at(p * PR, SLOT)
        for hp in range(4):
            at = hp * 128
            queries = both_heads(q_ref[wide, q_off + at : q_off + at + 128], low_q, high_q)
            keys = k_ref[base, k_off + at : k_off + at + 128]
            values = v_ref[base, v_off + at : v_off + at + 128]
            probs = probs_of(keys, queries, length).astype(BF)
            out_ref[base, at : at + 128] = merged_heads(dot_l(probs, values)).astype(BF)

    loop(GP, pair)


def attend_backward(
    length_of, q_ref, q_off, k_ref, k_off, v_ref, v_off, g_ref,
    dq_ref, dq_off, dk_ref, dk_off, dv_ref, dv_off,
):
    low, high = lane_masks()
    low_q, high_q = low * 0.125, high * 0.125

    def pair(p):
        length = length_of(p)
        base = rows_at(p * PR, PR)
        wide = rows_at(p * PR, SLOT)
        row = lax.broadcasted_iota(jnp.int32, (SLOT, 128), 0)
        for hp in range(4):
            at = hp * 128
            queries = both_heads(q_ref[wide, q_off + at : q_off + at + 128], low_q, high_q)
            keys = k_ref[base, k_off + at : k_off + at + 128]
            values = v_ref[base, v_off + at : v_off + at + 128]
            grads = jnp.where(row < PR, g_ref[wide, at : at + 128].astype(F32), 0.0).astype(BF)
            grads = both_heads(grads, low, high)
            probs = probs_of(keys, queries, length)
            grad_probs = dot_t(values, grads)
            mean = jnp.sum(probs * grad_probs, axis=0, keepdims=True)
            grad_raw = (probs * (grad_probs - mean)).astype(BF)
            dv_ref[base, dv_off + at : dv_off + at + 128] = dot(probs.astype(BF), grads).astype(BF)
            dk_ref[base, dk_off + at : dk_off + at + 128] = dot(grad_raw, queries).astype(BF)
            dq = merged_heads(dot_l(grad_raw, keys)) * 0.125
            dq_ref[base, dq_off + at : dq_off + at + 128] = dq.astype(BF)

    loop(GP, pair)


def zero_rows(ref, start):
    ref[start:, :] = jnp.zeros((ref.shape[0] - start, ref.shape[1]), ref.dtype)


def feed_forward(w_up, w_down, h_ref, hb_ref, hid_ref, act_ref):
    hb_ref[...] = h_ref[...].astype(BF)

    def column(n):
        cols = rows_at(n * 512, 512, 512)
        hidden = dot(hb_ref[...], w_up[:, cols])
        hid_ref[:, cols] = hidden.astype(BF)
        act_ref[:, cols] = gelu(hidden).astype(BF)

    loop(FF // 512, column)
    return h_ref[...] + dot(act_ref[...], w_down[...])


def feed_back(w_up, w_down, ds_ref, bg_ref, hid_ref, dhid_ref):
    def column(n):
        cols = rows_at(n * 512, 512, 512)
        grad_act = dot_t(bg_ref[...], w_down[cols, :])
        dhid_ref[:, cols] = (grad_act * gelu_slope(hid_ref[:, cols].astype(F32))).astype(BF)

    loop(FF // 512, column)
    return ds_ref[...] + dot_t(dhid_ref[...], w_up[...])


def feed_weight_grads(hb_ref, dhid_ref, act_ref, bg_ref, out_ref):
    def column(n):
        cols = rows_at(n * 512, 512, 512)
        out_ref[rows_at(n * 512, 512, 512), :] = dot_l(hb_ref[...], dhid_ref[:, cols]).astype(BF)
        out_ref[rows_at(FF + n * 512, 512, 512), :] = dot_l(act_ref[:, cols], bg_ref[...]).astype(BF)

    loop(FF // 512, column)


def count_norm(gb, index, grad, unit):
    gb[8 * index : 8 * index + 8, :] += fold8(grad * unit)
    gb[24 + 8 * index : 32 + 8 * index, :] += fold8(grad)


def forward_body(group, r):
    moves = Moves(r.sems)
    is_encoder = r.role[0] == 0
    first = group * GP
    got_x = moves.start(r.x_in.at[first * SLOT : (first + GP) * SLOT, :], r.x)
    got_in = moves.start(r.w_in, r.win)
    got_out = moves.start(r.w_out, r.wout)
    got_up = moves.start(r.w_up, r.wup)
    got_down = moves.start(r.w_down, r.wdown)
    zero_rows(r.qkv, GR)
    moves.wait(got_x)
    for p in range(GP):
        r.xp[p * PR : (p + 1) * PR, :] = r.x[p * SLOT : p * SLOT + PR, :]
    moves.wait(got_in)

    def column(n):
        cols = rows_at(n * 512, 512, 512)
        r.qkv[0:GR, cols] = dot(r.xp[...], r.win[:, cols]).astype(BF)

    loop(3, column)
    moves.start(r.xp, r.xp_out)
    moves.start(r.qkv.at[0:GR, :], r.qkv_out)
    attend_forward(lambda p: r.lengths[first + p], r.qkv, 0, r.qkv, 512, r.qkv, 1024, r.mix)
    moves.start(r.mix, r.mix_out)
    moves.wait(got_out)
    unit, scale = norm_of(r.xp[...].astype(F32) + dot(r.mix[...], r.wout[...]))
    r.unit0[...] = unit.astype(BF)
    r.sc0[...] = scale
    r.h[...] = unit * r.gains[0:1, :] + r.biases[0:1, :]
    moves.start(r.unit0, r.unit0_out)
    moves.start(r.sc0, r.sc0_out)
    moves.start(r.h, r.h_out)
    moves.wait(got_up, got_down)
    first_used = moves.used

    @pl.when(is_encoder)
    def _():
        own = Moves(r.sems)
        own.used = first_used
        summed = feed_forward(r.wup, r.wdown, r.h, r.hb, r.hid, r.act)
        unit, scale = norm_of(summed)
        r.unit1[...] = unit.astype(BF)
        r.sc1[...] = scale
        unit, scale = norm_of(unit * r.gains[1:2, :] + r.biases[1:2, :])
        r.unit2[...] = unit.astype(BF)
        r.sc2[...] = scale
        memory = unit * r.gains[2:3, :] + r.biases[2:3, :]
        r.mem[...] = memory.astype(BF)
        r.state[...] = memory
        row = lax.broadcasted_iota(jnp.int32, (16, D), 0)
        place = lax.broadcasted_iota(jnp.int32, (PR, D), 0)
        for p in range(GP):
            length = r.lengths[first + p]
            last = r.mem[(p + 1) * PR - 16 : (p + 1) * PR, :].astype(F32)
            r.mem[(p + 1) * PR - 16 : (p + 1) * PR, :] = jnp.where(
                row < 8, last, length.astype(F32)
            ).astype(BF)
            r.states[p * SLOT : p * SLOT + PR, :] = jnp.where(
                place < length, r.state[p * PR : (p + 1) * PR, :], 0.0
            )
            r.states[p * SLOT + PR : (p + 1) * SLOT, :] = jnp.zeros((SLOT - PR, D), F32)
        own.start(r.mem, r.mem_out)
        for name in ("hb", "hid", "act", "unit1", "sc1", "unit2", "sc2"):
            own.start(getattr(r, name), getattr(r, name + "_out"))
        own.start(r.states, r.states_out.at[first * SLOT : (first + GP) * SLOT, :])
        own.finish()

    moves.finish()


def decode_body(group, r):
    first = group * GP

    @pl.when(r.role[0] == 1)
    def _():
        moves = Moves(r.sems)
        core = r.role[1]
        got_h = moves.start(r.h_in, r.h)
        got_q = moves.start(r.wq_in, r.wq)
        got_mem = moves.start(r.mem_in, r.mem)
        got_mine = moves.start(r.mine_in, r.wkv.at[pl.ds(pl.multiple_of(core * D, D), D), :])
        got_other = moves.start(r.other_in, r.wkv.at[pl.ds(pl.multiple_of((1 - core) * D, D), D), :])
        got_o = moves.start(r.wo_in, r.wo)
        got_up = moves.start(r.w_up, r.wup)
        got_down = moves.start(r.w_down, r.wdown)
        got_cot = moves.start(r.cot_in.at[first * SLOT : (first + GP) * SLOT, :], r.cot)
        zero_rows(r.q, GR)
        zero_rows(r.gm, GR)
        r.gb[...] = jnp.zeros_like(r.gb)
        moves.wait(got_h, got_q)
        r.fb[...] = r.h[...].astype(BF)
        r.q[0:GR, :] = dot(r.fb[...], r.wq[...]).astype(BF)
        moves.start(r.fb, r.fb_out)
        moves.wait(got_mem, got_mine, got_other)
        r.k[...] = dot(r.mem[...], r.wkv[0:D, :]).astype(BF)
        r.v[...] = dot(r.mem[...], r.wkv[D : 2 * D, :]).astype(BF)

        def length_of(p):
            last = r.mem[rows_at(p * PR + PR - 16, 16), :].astype(F32)
            return last[15:16, :].astype(jnp.int32)

        attend_forward(length_of, r.q, 0, r.k, 0, r.v, 0, r.mix)
        moves.start(r.mix, r.mix_out)
        moves.wait(got_o)
        unit, scale = norm_of(r.h[...] + dot(r.mix[...], r.wo[...]))
        r.unit1[...] = unit.astype(BF)
        r.sc1[...] = scale
        r.h[...] = unit * r.gains[1:2, :] + r.biases[1:2, :]
        moves.wait(got_up, got_down, got_cot)
        for p in range(GP):
            place = lax.broadcasted_iota(jnp.int32, (PR, 1), 0)
            valid = jnp.where(place < r.lengths[first + p], 1.0, 0.0)
            r.valid[p * PR : (p + 1) * PR, :] = valid
            r.ds[p * PR : (p + 1) * PR, :] = r.cot[p * SLOT : p * SLOT + PR, :].astype(F32) * valid
        summed = feed_forward(r.wup, r.wdown, r.h, r.hb, r.hid, r.act)
        moves.start(r.hb, r.hb_out)
        moves.start(r.act, r.act_out)
        unit, scale = norm_of(summed)
        grad = r.ds[...]
        r.h[...] = (unit * r.gains[2:3, :] + r.biases[2:3, :]) * r.valid[...]
        count_norm(r.gb, 2, grad, unit)
        grad_sum = norm_back(grad, unit, scale, r.gains[2:3, :])
        r.bg2[...] = grad_sum.astype(BF)
        r.ds[...] = grad_sum
        moves.start(r.bg2, r.bg2_out)
        for p in range(GP):
            r.states[p * SLOT : p * SLOT + PR, :] = r.h[p * PR : (p + 1) * PR, :]
            r.states[p * SLOT + PR : (p + 1) * SLOT, :] = jnp.zeros((SLOT - PR, D), F32)
        moves.start(r.states, r.states_out.at[first * SLOT : (first + GP) * SLOT, :])
        grad = feed_back(r.wup, r.wdown, r.ds, r.bg2, r.hid, r.dhid)
        moves.start(r.dhid, r.dhid_out)
        unit = r.unit1[...].astype(F32)
        count_norm(r.gb, 1, grad, unit)
        grad_sum = norm_back(grad, unit, r.sc1[...], r.gains[1:2, :])
        r.bg1[...] = grad_sum.astype(BF)
        r.h[...] = grad_sum
        moves.start(r.bg1, r.bg1_out)
        moves.start(r.gb, r.gb_out)
        r.gm[0:GR, :] = dot_t(r.bg1[...], r.wo[...]).astype(BF)
        attend_backward(length_of, r.q, 0, r.k, 0, r.v, 0, r.gm, r.dq, 0, r.dk, 0, r.dv, 0)
        moves.start(r.dq, r.dq_out)
        moves.start(r.dk, r.dk_out)
        moves.start(r.dv, r.dv_out)
        r.gmem[...] = (
            dot_t(r.dk[...], r.wkv[0:D, :]) + dot_t(r.dv[...], r.wkv[D : 2 * D, :])
        ).astype(BF)
        moves.start(r.gmem, r.gmem_out)
        r.ds[...] = r.h[...] + dot_t(r.dq[...], r.wq[...])
        moves.start(r.ds, r.dh_out)
        moves.finish()


def self_back_part(r, moves, got, first):
    zero_rows(r.gm, GR)
    zero_rows(r.qkv, GR)
    moves.wait(*got[:-1])
    grad = r.dh[...]
    unit = r.unit0[...].astype(F32)
    count_norm(r.gb, 0, grad, unit)
    grad = norm_back(grad, unit, r.sc0[...], r.gains[0:1, :])
    r.bg[...] = grad.astype(BF)
    r.dh[...] = grad
    moves.start(r.dh, r.ds_out)
    moves.start(r.bg, r.bg_out)
    r.gm[0:GR, :] = dot_t(r.bg[...], r.wout[...]).astype(BF)
    moves.wait(got[-1])
    attend_backward(
        lambda p: r.lengths[first + p],
        r.qkv, 0, r.qkv, 512, r.qkv, 1024, r.gm, r.dqkv, 0, r.dqkv, 512, r.dqkv, 1024,
    )
    moves.start(r.dqkv, r.dqkv_out)


def self_back_loads(r, moves, group):
    return [
        moves.start(getattr(r, f"unit0_{group}"), r.unit0),
        moves.start(getattr(r, f"sc0_{group}"), r.sc0),
        moves.start(r.w_out, r.wout),
        moves.start(getattr(r, f"qkv_{group}"), r.qkv.at[0:GR, :]),
    ]


def feed_back_loads(r, moves, group):
    return [
        moves.start(getattr(r, f"{name}_{group}"), getattr(r, name))
        for name in ("gmem", "unit2", "sc2", "unit1", "sc1")
    ] + [
        moves.start(r.w_down, r.wdown),
        moves.start(getattr(r, f"hid_{group}"), r.hid),
        moves.start(r.w_up, r.wup),
    ]


def feed_back_part(r, moves, got, bg, dhid):
    moves.wait(*got[:5])
    grad = r.gmem[...].astype(F32)
    unit = r.unit2[...].astype(F32)
    count_norm(r.gb, 2, grad, unit)
    grad = norm_back(grad, unit, r.sc2[...], r.gains[2:3, :])
    unit = r.unit1[...].astype(F32)
    count_norm(r.gb, 1, grad, unit)
    grad = norm_back(grad, unit, r.sc1[...], r.gains[1:2, :])
    bg[...] = grad.astype(BF)
    r.dh[...] = grad
    moves.wait(*got[5:])
    r.dh[...] = feed_back(r.wup, r.wdown, r.dh, bg, r.hid, dhid)


def stacked_loads(r, moves, name, held):
    zero_rows(held, 2 * GR)
    return [
        moves.start(getattr(r, f"{name}_{g}"), held.at[g * GR : (g + 1) * GR, :]) for g in range(2)
    ]


def cross_body(r):
    @pl.when(r.role[0] == 0)
    def _():
        moves = Moves(r.sems)
        got = feed_back_loads(r, moves, 0)
        got_self = self_back_loads(r, moves, 0)
        r.gb[...] = jnp.zeros_like(r.gb)
        feed_back_part(r, moves, got, r.fbg, r.dhid)
        moves.start(r.dhid, r.dhid_out)
        moves.start(r.fbg, r.fbg_out)
        self_back_part(r, moves, got_self, 0)
        moves.start(r.gb, r.gb_out)
        moves.finish()

    @pl.when(r.role[0] == 1)
    def _():
        moves = Moves(r.sems)
        names = ("mem", "dk", "dv", "fb", "dq", "mixc", "bg1", "hb2", "dhid2", "act2", "bg2")
        got = {name: stacked_loads(r, moves, name, getattr(r, "all_" + name)) for name in names}
        moves.wait(*got["mem"], *got["dk"], *got["dv"])
        r.gx[0:D, :] = dot_l(r.all_mem[...], r.all_dk[...]).astype(BF)
        r.gx[D : 2 * D, :] = dot_l(r.all_mem[...], r.all_dv[...]).astype(BF)
        start_halves(moves, r.role[1], r.gx, r.gx_out)
        moves.wait(*got["fb"], *got["dq"], *got["mixc"], *got["bg1"])
        r.gc[0:D, :] = dot_l(r.all_fb[...], r.all_dq[...]).astype(BF)
        r.gc[D : 2 * D, :] = dot_l(r.all_mixc[...], r.all_bg1[...]).astype(BF)
        start_halves(moves, r.role[1], r.gc, r.gc_out)
        moves.wait(*got["hb2"], *got["dhid2"], *got["act2"], *got["bg2"])
        feed_weight_grads(r.all_hb2, r.all_dhid2, r.all_act2, r.all_bg2, r.gf)
        start_halves(moves, r.role[1], r.gf, r.gf_out)
        moves.finish()


def feed_body(r):
    @pl.when(r.role[0] == 0)
    def _():
        moves = Moves(r.sems)
        got = feed_back_loads(r, moves, 1)
        got_hb = stacked_loads(r, moves, "hb", r.all_hb)
        got_act = stacked_loads(r, moves, "act", r.all_act)
        zero_rows(r.all_dhid, 2 * GR)
        zero_rows(r.all_bg, 2 * GR)
        got_first = [
            moves.start(r.dhid_0, r.all_dhid.at[0:GR, :]), moves.start(r.fbg_0, r.all_bg.at[0:GR, :]),
        ]
        r.gb[...] = jnp.zeros_like(r.gb)
        feed_back_part(
            r, moves, got, r.all_bg.at[GR : 2 * GR, :], r.all_dhid.at[GR : 2 * GR, :]
        )
        moves.start(r.dh, r.dh_out)
        moves.start(r.gb, r.gb_out)
        moves.wait(*got_hb, *got_act, *got_first)
        feed_weight_grads(r.all_hb, r.all_dhid, r.all_act, r.all_bg, r.gf)
        start_halves(moves, r.role[1], r.gf, r.gf_out)
        moves.finish()

    @pl.when(r.role[0] == 1)
    def _():
        moves = Moves(r.sems)
        got_dh = moves.start(r.dh_0, r.dh)
        got = self_back_loads(r, moves, 0)
        r.gb[...] = jnp.zeros_like(r.gb)
        moves.wait(got_dh)
        self_back_part(r, moves, got, 0)
        moves.start(r.gb, r.gb_out)
        moves.finish()


def self_body(r):
    moves = Moves(r.sems)
    got_dh = moves.start(r.dh_1, r.dh)
    got = self_back_loads(r, moves, 1)
    r.gb[...] = jnp.zeros_like(r.gb)
    moves.wait(got_dh)
    self_back_part(r, moves, got, GP)
    moves.start(r.gb, r.gb_out)
    moves.finish()


EXTRA = 64


def self_weights_body(r):
    moves = Moves(r.sems)
    got_x = stacked_loads(r, moves, "xp", r.xp)
    got_qkv = stacked_loads(r, moves, "dqkv", r.dqkv)
    got_mix = stacked_loads(r, moves, "mix", r.mix)
    got_bg = stacked_loads(r, moves, "bg", r.bg)
    got_in = moves.start(r.w_in, r.win)
    got_ds = stacked_loads(r, moves, "ds", r.ds)
    part = 2 * D + EXTRA
    enc = r.gb_cross[...]
    dec = r.gb_dec0[...] + r.gb_dec1[...]
    picked = jnp.where(r.role[0] == 0, enc, dec) + r.gb_feed[...] + r.gb_self[...]
    small = jnp.concatenate(
        [jnp.sum(picked[8 * i : 8 * i + 8, :], axis=0, keepdims=True) for i in range(6)]
        + [jnp.zeros((EXTRA - 6, D), F32)],
        axis=0,
    ).astype(BF)
    r.ga[2 * D : part, :] = small
    r.ga[part + 2 * D : 2 * part, :] = small
    moves.wait(*got_x, *got_qkv)
    r.ga[0:D, :] = dot_l(r.xp[...], r.dqkv[:, 0:D]).astype(BF)
    r.ga[D : 2 * D, :] = dot_l(r.xp[...], r.dqkv[:, D : 2 * D]).astype(BF)
    r.ga[part : part + D, :] = dot_l(r.xp[...], r.dqkv[:, 2 * D : 3 * D]).astype(BF)
    moves.wait(*got_mix, *got_bg)
    r.ga[part + D : part + 2 * D, :] = dot_l(r.mix[...], r.bg[...]).astype(BF)
    start_halves(moves, r.role[1], r.ga, r.ga_out)
    moves.wait(got_in, *got_ds)

    def leave(p):
        at = rows_at(p * PR, PR)
        to = rows_at(p * SLOT, PR)
        r.dx[to, :] = r.ds[at, :] + dot_t(r.dqkv[at, :], r.win[...])
        r.dx[rows_at(p * SLOT + PR, SLOT - PR), :] = jnp.zeros((SLOT - PR, D), F32)

    loop(2 * GP, leave)
    moves.start(r.dx, r.grads_out)
    moves.finish()


def start_halves(moves, core, held, out):
    half = held.shape[0] // 2
    for i in range(2):
        place = pl.multiple_of(((core + i) & 1) * half, half)
        moves.start(held.at[i * half : (i + 1) * half, :], out.at[pl.ds(place, half), :])


def place_blocks(core, moves, own, other, held, firsts):
    got = []
    for group, shift in ((own, 0), (other, 1)):
        start = 0
        for ref in group:
            size = ref.shape[0]
            place = pl.multiple_of(((core + shift) & 1) * firsts + start, 16)
            got.append(moves.start(ref, held.at[pl.ds(place, size), :]))
            start += size
    return got


def place_early_body(r):
    moves = Moves(r.sems)
    core = r.role[1]
    got_c = place_blocks(core, moves, [r.c], [r.c_other], r.held_c, D)
    got = place_blocks(core, moves, [r.fa, r.fb], [r.fa_other, r.fb_other], r.held, FF)
    moves.wait(*got_c)
    r.ca[...] = r.held_c[0:D, :].astype(F32)
    r.cb[...] = r.held_c[D : 2 * D, :].astype(F32)
    moves.start(r.ca, r.ca_out)
    moves.start(r.cb, r.cb_out)
    moves.wait(*got)
    for n in range(4):
        r.up[:, n * D : (n + 1) * D] = r.held[n * D : (n + 1) * D, :].astype(F32)
    moves.start(r.up, r.up_out)
    r.down[...] = r.held[FF : 2 * FF, :].astype(F32)
    moves.start(r.down, r.down_out)
    moves.finish()


def place_late_body(r):
    moves = Moves(r.sems)
    part = 2 * D + EXTRA
    moves.wait(
        *place_blocks(r.role[1], moves, [r.da, r.db], [r.da_other, r.db_other], r.held, part)
    )
    r.wout[...] = r.held[part + D : part + 2 * D, :].astype(F32)
    moves.start(r.wout, r.out_out)
    for n, start in enumerate((0, D, part)):
        r.win[:, n * D : (n + 1) * D] = r.held[start : start + D, :].astype(F32)
    moves.start(r.win, r.in_out)
    small = r.held[2 * D : 2 * D + 16, :].astype(F32)
    r.gains[...] = small[0:3, :]
    r.biases[...] = small[3:6, :]
    moves.start(r.gains, r.gains_out)
    moves.start(r.biases, r.biases_out)
    moves.finish()


ANY = pl.BlockSpec(memory_space=pl.ANY)
WHOLE = pl.BlockSpec(memory_space=pltpu.VMEM)
SCALARS = pl.BlockSpec(memory_space=pltpu.SMEM)


class Refs:
    def __init__(self, names, refs):
        for name, ref in zip(names, refs):
            setattr(self, name, ref)


def call(body, name, flops, ins, outs, scratch, copies, aliases=None, whole=()):
    scalars = ("role", "lengths")
    specs = [SCALARS if n in scalars else WHOLE if n in whole else ANY for n in ins]
    names = [*ins, *outs, *scratch, "sems"]
    position = list(ins).index
    results = list(outs).index

    def kernel(*refs):
        body(Refs(names, refs))

    found = pl.pallas_call(
        kernel,
        out_shape=[jax.ShapeDtypeStruct(s, t) for s, t in outs.values()],
        in_specs=specs,
        out_specs=[ANY] * len(outs),
        scratch_shapes=[pltpu.VMEM(s, t) for s, t in scratch.values()]
        + [pltpu.SemaphoreType.DMA((copies,))],
        input_output_aliases={position(i): results(o) for i, o in (aliases or {}).items()},
        compiler_params=pltpu.CompilerParams(vmem_limit_bytes=60 * 1024 * 1024),
        cost_estimate=pl.CostEstimate(flops=flops, bytes_accessed=1 << 23, transcendentals=0),
        name=name,
    )(*ins.values())
    return dict(zip(outs, found))


def swapped(x, mask):
    size = lax.axis_size("dp")
    return lax.ppermute(x, "dp", [(i, i ^ mask) for i in range(size)])


def added(keep, recv):
    return (keep.astype(F32) + recv.astype(F32)).astype(BF)


def lowered(cur, mask, bit):
    half = cur.shape[0] // 2
    recv = swapped(lax.dynamic_slice_in_dim(cur, (1 - bit) * half, half, 0), mask)
    return added(lax.dynamic_slice_in_dim(cur, bit * half, half, 0), recv)


def raised(cur, mask, bit):
    other = swapped(cur, mask)
    return jnp.where(
        bit == 0, jnp.concatenate([cur, other], 0), jnp.concatenate([other, cur], 0)
    )


class Sums:
    def __init__(self):
        size = lax.axis_size("dp")
        place = lax.axis_index("dp")
        self.masks = [1 << i for i in range(1, size.bit_length() - 1)]
        self.bits = {mask: (place >> (mask.bit_length() - 1)) & 1 for mask in self.masks}

    def order(self, turn):
        masks = self.masks
        return masks if turn == 0 else masks[1:] + masks[:1]

    def down(self, parts, turns, first, last):
        for step in range(first, last):
            parts = [
                lowered(p, self.order(t)[step], self.bits[self.order(t)[step]])
                for p, t in zip(parts, turns)
            ]
        return parts

    def up(self, parts, turns):
        for step in reversed(range(len(self.masks))):
            parts = [
                raised(p, self.order(t)[step], self.bits[self.order(t)[step]])
                for p, t in zip(parts, turns)
            ]
        return parts


def on_device(
    embeds, lengths, attn_in, attn_out, cross_a, cross_b, ffn_up, ffn_down,
    norm_gains, norm_biases, cotangent,
):
    x, own = embeds[0], lengths[0]
    win, wout, wa, wb, wup, wdown = (
        attn_in[0], attn_out[0], cross_a[0], cross_b[0], ffn_up[0], ffn_down[0],
    )
    gains, biases = norm_gains[0], norm_biases[0]
    slots = 2 * GP * SLOT
    pipe = lax.axis_index("pipe")
    is_encoder = pipe == 0
    odd = lax.axis_index("dp") & 1
    role = jnp.stack([pipe, odd]).astype(jnp.int32)
    onward, back = [(0, 1)], [(1, 0)]

    def bf(*shape):
        return (shape, BF)

    def f32(*shape):
        return (shape, F32)

    flat, flat_f, wide, one, triple = bf(GR, D), f32(GR, D), bf(GR, FF), f32(GR, 1), bf(GR, 3 * D)
    full, slot, slot_f = f32(slots, D), bf(GP * SLOT, D), f32(GP * SLOT, D)
    square, up_w, down_w, in_w = bf(D, D), bf(D, FF), bf(FF, D), bf(D, 3 * D)
    tall, counts = bf(TALL, D), f32(48, D)
    base = dict(role=role, lengths=own, gains=gains, biases=biases)
    whole = ("gains", "biases")

    mine = lax.ppermute(jnp.where(odd == 0, wa, wb), "pipe", onward)
    other = swapped(mine, 1)

    fwd, mem_in, states = [], [], None
    for g in range(2):
        ins = dict(base, x_in=x, w_in=win, w_out=wout, w_up=wup, w_down=wdown)
        if g:
            ins["states_in"] = states
        fwd.append(
            call(
                functools.partial(forward_body, g), f"forward_{g}", 4_000_000_000, ins,
                dict(
                    h_out=flat_f, xp_out=flat, qkv_out=triple, mix_out=flat, unit0_out=flat, sc0_out=one,
                    mem_out=flat, hb_out=flat, hid_out=wide, act_out=wide, unit1_out=flat, sc1_out=one,
                    unit2_out=flat, sc2_out=one, states_out=full,
                ),
                dict(
                    x=slot, win=in_w, wout=square, wup=up_w, wdown=down_w, h=flat_f, xp=flat,
                    qkv=bf(TALL, 3 * D), mix=flat, unit0=flat, sc0=one, mem=flat, hb=flat, hid=wide,
                    act=wide, unit1=flat, sc1=one, unit2=flat, sc2=one, state=flat_f, states=slot_f,
                ),
                24, aliases={"states_in": "states_out"} if g else None, whole=whole,
            )
        )
        states = fwd[g]["states_out"]
        mem_in.append(lax.ppermute(fwd[g]["mem_out"], "pipe", onward))

    dec, gmem_in = [], []
    for g in range(2):
        dec.append(
            call(
                functools.partial(decode_body, g), f"decode_{g}", 8_000_000_000,
                dict(
                    base, h_in=fwd[g]["h_out"], mem_in=mem_in[g], cot_in=cotangent, wq_in=wa, wo_in=wb,
                    mine_in=mine, other_in=other, w_up=wup, w_down=wdown, states_in=states,
                ),
                dict(
                    states_out=full, gmem_out=flat, dh_out=flat_f, fb_out=flat, dq_out=flat, mix_out=flat,
                    bg1_out=flat, dk_out=flat, dv_out=flat, hb_out=flat, dhid_out=wide, act_out=wide,
                    bg2_out=flat, gb_out=counts,
                ),
                dict(
                    h=flat_f, mem=flat, cot=slot, wq=square, wo=square, wkv=bf(2 * D, D), wup=up_w,
                    wdown=down_w, states=slot_f, gmem=flat, fb=flat, q=tall, k=flat, v=flat, mix=flat,
                    dq=flat, dk=flat, dv=flat, bg1=flat, hb=flat, hid=wide, dhid=wide, act=wide, bg2=flat,
                    unit1=flat, sc1=one, valid=one, ds=flat_f, gm=tall, gb=counts,
                ),
                24, aliases={"states_in": "states_out"}, whole=whole,
            )
        )
        states = dec[g]["states_out"]
        gmem_in.append(lax.ppermute(dec[g]["gmem_out"], "pipe", back))

    def of(group, results, **names):
        return {f"{k}_{group}": results[v] for k, v in names.items()}

    enc_names = dict(
        unit2="unit2_out", sc2="sc2_out", unit1="unit1_out", sc1="sc1_out", hid="hid_out",
    )
    self_names = dict(unit0="unit0_out", sc0="sc0_out", qkv="qkv_out")
    back_scratch = dict(
        gmem=flat, unit2=flat, sc2=one, unit1=flat, sc1=one, wdown=down_w, hid=wide, wup=up_w, dh=flat_f,
    )
    self_scratch = dict(
        unit0=flat, sc0=one, wout=square, qkv=bf(TALL, 3 * D), bg=flat, gm=tall, dqkv=triple, gb=counts,
    )
    dec_names = dict(
        dk="dk_out", dv="dv_out", fb="fb_out", dq="dq_out", mixc="mix_out", bg1="bg1_out", hb2="hb_out",
        dhid2="dhid_out", act2="act_out", bg2="bg2_out",
    )
    ins = dict(base, w_up=wup, w_down=wdown, w_out=wout, gmem_0=gmem_in[0])
    ins.update(of(0, fwd[0], **enc_names, **self_names))
    for g in range(2):
        ins.update(of(g, dec[g], **dec_names))
        ins[f"mem_{g}"] = mem_in[g]
    all_flat, all_wide = bf(ALL, D), bf(ALL, FF)
    grads = dict(gf=bf(2 * FF, D))
    cross = call(
        cross_body, "cross_back", 9_000_000_000, ins,
        dict(
            dhid_out=wide, fbg_out=flat, ds_out=flat_f, bg_out=flat, dqkv_out=triple, gb_out=counts,
            gx_out=bf(2 * D, D), gc_out=bf(2 * D, D), gf_out=bf(2 * FF, D),
        ),
        dict(
            **back_scratch, **self_scratch, fbg=flat, dhid=wide,
            **{
                "all_" + n: all_wide if n in ("dhid2", "act2") else all_flat
                for n in ("mem", *dec_names)
            },
            gx=bf(2 * D, D), gc=bf(2 * D, D), **grads,
        ),
        40, whole=whole,
    )
    gx_in = lax.ppermute(cross["gx_out"], "pipe", back)

    ins = dict(
        base, w_up=wup, w_down=wdown, w_out=wout, gmem_1=gmem_in[1], dhid_0=cross["dhid_out"],
        fbg_0=cross["fbg_out"], hb_0=fwd[0]["hb_out"], hb_1=fwd[1]["hb_out"], act_0=fwd[0]["act_out"],
        act_1=fwd[1]["act_out"], dh_0=dec[0]["dh_out"], dh_in=dec[1]["dh_out"], gf_in=cross["gf_out"],
        ds_in=cross["ds_out"], bg_in=cross["bg_out"], dqkv_in=cross["dqkv_out"],
    )
    ins.update(of(1, fwd[1], **enc_names))
    ins.update(of(0, fwd[0], **self_names))
    feed = call(
        feed_body, "feed_back", 9_000_000_000, ins,
        dict(
            dh_out=flat_f, gf_out=bf(2 * FF, D), ds_out=flat_f, bg_out=flat, dqkv_out=triple, gb_out=counts,
        ),
        dict(
            **back_scratch, **self_scratch, all_hb=all_flat, all_act=all_wide, all_dhid=all_wide,
            all_bg=all_flat, **grads,
        ),
        32,
        aliases=dict(
            dh_in="dh_out", gf_in="gf_out", ds_in="ds_out", bg_in="bg_out", dqkv_in="dqkv_out"
        ),
        whole=whole,
    )
    gf = feed["gf_out"]
    gc = jnp.where(is_encoder, gx_in, cross["gc_out"])
    sums = Sums()
    depth = len(sums.masks)
    f_keep = added(gf[:FF], swapped(gf[FF:], 1))
    c_keep = added(gc[:D], swapped(gc[D:], 1))

    last = call(
        self_body, "self_back", 3_000_000_000,
        dict(base, dh_1=feed["dh_out"], w_out=wout, **of(1, fwd[1], **self_names)),
        dict(ds_out=flat_f, bg_out=flat, dqkv_out=triple, gb_out=counts),
        dict(**self_scratch, dh=flat_f),
        16, whole=whole,
    )
    f_keep, c_keep, ds = lax.optimization_barrier((f_keep, c_keep, last["ds_out"]))
    early = sums.down([f_keep[: 2 * D], f_keep[2 * D :], c_keep], (0, 1, 0), 0, 1)
    part = 2 * D + EXTRA
    ins = dict(
        role=role, gb_cross=cross["gb_out"], gb_dec0=dec[0]["gb_out"], gb_dec1=dec[1]["gb_out"],
        gb_feed=feed["gb_out"], gb_self=last["gb_out"], w_in=win, ds_0=feed["ds_out"], ds_1=ds,
        bg_0=feed["bg_out"], bg_1=last["bg_out"], dqkv_0=feed["dqkv_out"], dqkv_1=last["dqkv_out"],
    )
    for g in range(2):
        ins.update(of(g, fwd[g], xp="xp_out", mix="mix_out"))
    late = call(
        self_weights_body, "self_weights", 8_000_000_000, ins,
        dict(grads_out=full, ga_out=bf(2 * part, D)),
        dict(
            ds=f32(ALL, D), bg=all_flat, dqkv=bf(ALL, 3 * D), xp=all_flat, mix=all_flat, win=in_w, dx=full,
            ga=bf(2 * part, D),
        ),
        20, whole=("gb_cross", "gb_dec0", "gb_dec1", "gb_feed", "gb_self"),
    )
    input_grads, ga = late["grads_out"], late["ga_out"]
    a_keep = added(ga[:part], swapped(ga[part:], 1))
    early = sums.down(early, (0, 1, 0), 1, depth)
    late = sums.down([a_keep[:D], a_keep[D:]], (0, 1), 0, depth)
    early = sums.up(early, (0, 1, 0))
    late = sums.up(late, (0, 1))
    early_other = [swapped(p, 1) for p in early]
    late_other = [swapped(p, 1) for p in late]
    placed = call(
        place_early_body, "place_early", 1_000_000_000,
        dict(
            role=role, fa=early[0], fb=early[1], fa_other=early_other[0], fb_other=early_other[1],
            c=early[2], c_other=early_other[2],
        ),
        dict(up_out=f32(D, FF), down_out=f32(FF, D), ca_out=f32(D, D), cb_out=f32(D, D)),
        dict(
            held=bf(2 * FF, D), held_c=bf(2 * D, D), up=f32(D, FF), down=f32(FF, D), ca=f32(D, D),
            cb=f32(D, D),
        ),
        16,
    )
    placed |= call(
        place_late_body, "place_late", 1_000_000_000,
        dict(role=role, da=late[0], db=late[1], da_other=late_other[0], db_other=late_other[1]),
        dict(in_out=f32(D, 3 * D), out_out=f32(D, D), gains_out=f32(3, D), biases_out=f32(3, D)),
        dict(held=bf(2 * part, D), win=f32(D, 3 * D), wout=f32(D, D), gains=f32(3, D), biases=f32(3, D)),
        16,
    )
    outs = (
        states, input_grads, placed["in_out"], placed["out_out"], placed["ca_out"], placed["cb_out"],
        placed["up_out"], placed["down_out"], placed["gains_out"], placed["biases_out"],
    )
    return tuple(out[None] for out in outs)


def solution(mesh):
    cut = P("pipe", "dp", None)
    held = P("pipe", None, None)
    return jax.shard_map(
        on_device,
        mesh=mesh,
        in_specs=(cut, P("pipe", "dp")) + (held,) * 8 + (P("dp", None),),
        out_specs=(cut, cut) + (held,) * 8,
        check_vma=False,
    )
```

```python
import functools

import jax
import jax.numpy as jnp
from jax import lax
from jax.experimental import pallas as pl
from jax.experimental.pallas import tpu as pltpu
from jax.sharding import PartitionSpec as P

HEADS = 8
D = 512
FF = 2048
SLOT = 256
PR = 208
GP = 2
GR = GP * PR
TALL = 512
ALL = 896
NORM_EPSILON = 1e-05
BF = jnp.bfloat16
F32 = jnp.float32
CORE_C = 0.7978845608028654
CUBE_C = 0.044715


def dot(a, b):
    return lax.dot_general(a, b, (((1,), (0,)), ((), ())), preferred_element_type=F32)


def dot_t(a, b):
    return lax.dot_general(a, b, (((1,), (1,)), ((), ())), preferred_element_type=F32)


def dot_l(a, b):
    return lax.dot_general(a, b, (((0,), (0,)), ((), ())), preferred_element_type=F32)


def rows_at(start, size, step=16):
    return pl.ds(pl.multiple_of(start, step), size)


def loop(n, body):
    def run(i, carry):
        body(i)
        return carry

    lax.fori_loop(0, n, run, 0)


def gelu(u):
    return 0.5 * u * (1.0 + jnp.tanh(CORE_C * (u + CUBE_C * u * u * u)))


def gelu_slope(u):
    square = u * u
    bent = jnp.tanh(CORE_C * u * (1.0 + CUBE_C * square))
    return 0.5 * (1.0 + bent) + 0.5 * u * (1.0 - bent * bent) * (
        CORE_C * (1.0 + 3.0 * CUBE_C * square)
    )


def norm_of(summed):
    center = summed - jnp.mean(summed, axis=-1, keepdims=True)
    spread = jnp.mean(center * center, axis=-1, keepdims=True)
    scale = lax.rsqrt(spread + NORM_EPSILON)
    return center * scale, scale


def norm_back(grad, unit, scale, gain):
    lifted = grad * gain
    first = jnp.mean(lifted, axis=-1, keepdims=True)
    second = jnp.mean(lifted * unit, axis=-1, keepdims=True)
    return scale * (lifted - first - unit * second)


def fold8(values):
    return jnp.sum(values.reshape(-1, 8, values.shape[-1]), axis=0)


class Moves:
    def __init__(self, sems):
        self.sems = sems
        self.used = 0
        self.open = []

    def start(self, source, target):
        copy = pltpu.make_async_copy(source, target, self.sems.at[self.used])
        self.used += 1
        copy.start()
        self.open.append(copy)
        return copy

    def wait(self, *copies):
        for copy in copies:
            copy.wait()
            self.open = [c for c in self.open if c is not copy]

    def finish(self):
        for copy in self.open:
            copy.wait()
        self.open = []


def lane_masks():
    lane = lax.broadcasted_iota(jnp.int32, (1, 128), 1)
    low = jnp.where(lane < 64, 1.0, 0.0).astype(BF)
    high = jnp.where(lane < 64, 0.0, 1.0).astype(BF)
    return low, high


def both_heads(rows, low, high):
    return jnp.concatenate([rows * low, rows * high], axis=0)


def merged_heads(stacked):
    lane = lax.broadcasted_iota(jnp.int32, (PR, 128), 1)
    return jnp.where(lane < 64, stacked[:PR], stacked[SLOT : SLOT + PR])


def probs_of(keys, queries, length):
    raw = dot_t(keys, queries)
    place = lax.broadcasted_iota(jnp.int32, raw.shape, 0)
    raw = jnp.where(place < length, raw, -1e30)
    top = jnp.max(raw, axis=0, keepdims=True)
    terms = jnp.exp(raw - top)
    total = jnp.sum(terms, axis=0, keepdims=True)
    return terms * (1.0 / total)


def attend_forward(length_of, q_ref, q_off, k_ref, k_off, v_ref, v_off, out_ref):
    low, high = lane_masks()
    low_q, high_q = low * 0.125, high * 0.125

    def pair(p):
        length = length_of(p)
        base = rows_at(p * PR, PR)
        wide = rows_at(p * PR, SLOT)
        for hp in range(4):
            at = hp * 128
            queries = both_heads(q_ref[wide, q_off + at : q_off + at + 128], low_q, high_q)
            keys = k_ref[base, k_off + at : k_off + at + 128]
            values = v_ref[base, v_off + at : v_off + at + 128]
            probs = probs_of(keys, queries, length).astype(BF)
            out_ref[base, at : at + 128] = merged_heads(dot_l(probs, values)).astype(BF)

    loop(GP, pair)


def attend_backward(
    length_of, q_ref, q_off, k_ref, k_off, v_ref, v_off, g_ref,
    dq_ref, dq_off, dk_ref, dk_off, dv_ref, dv_off,
):
    low, high = lane_masks()
    low_q, high_q = low * 0.125, high * 0.125

    def pair(p):
        length = length_of(p)
        base = rows_at(p * PR, PR)
        wide = rows_at(p * PR, SLOT)
        row = lax.broadcasted_iota(jnp.int32, (SLOT, 128), 0)
        for hp in range(4):
            at = hp * 128
            queries = both_heads(q_ref[wide, q_off + at : q_off + at + 128], low_q, high_q)
            keys = k_ref[base, k_off + at : k_off + at + 128]
            values = v_ref[base, v_off + at : v_off + at + 128]
            grads = jnp.where(row < PR, g_ref[wide, at : at + 128].astype(F32), 0.0).astype(BF)
            grads = both_heads(grads, low, high)
            probs = probs_of(keys, queries, length)
            grad_probs = dot_t(values, grads)
            mean = jnp.sum(probs * grad_probs, axis=0, keepdims=True)
            grad_raw = (probs * (grad_probs - mean)).astype(BF)
            dv_ref[base, dv_off + at : dv_off + at + 128] = dot(probs.astype(BF), grads).astype(BF)
            dk_ref[base, dk_off + at : dk_off + at + 128] = dot(grad_raw, queries).astype(BF)
            dq = merged_heads(dot_l(grad_raw, keys)) * 0.125
            dq_ref[base, dq_off + at : dq_off + at + 128] = dq.astype(BF)

    loop(GP, pair)


def zero_rows(ref, start):
    ref[start:, :] = jnp.zeros((ref.shape[0] - start, ref.shape[1]), ref.dtype)


def feed_forward(w_up, w_down, h_ref, hb_ref, hid_ref, act_ref):
    hb_ref[...] = h_ref[...].astype(BF)

    def column(n):
        cols = rows_at(n * 512, 512, 512)
        hidden = dot(hb_ref[...], w_up[:, cols])
        hid_ref[:, cols] = hidden.astype(BF)
        act_ref[:, cols] = gelu(hidden).astype(BF)

    loop(FF // 512, column)
    return h_ref[...] + dot(act_ref[...], w_down[...])


def feed_back(w_up, w_down, ds_ref, bg_ref, hid_ref, dhid_ref):
    def column(n):
        cols = rows_at(n * 512, 512, 512)
        grad_act = dot_t(bg_ref[...], w_down[cols, :])
        dhid_ref[:, cols] = (grad_act * gelu_slope(hid_ref[:, cols].astype(F32))).astype(BF)

    loop(FF // 512, column)
    return ds_ref[...] + dot_t(dhid_ref[...], w_up[...])


def feed_weight_grads(hb_ref, dhid_ref, act_ref, bg_ref, out_ref):
    def column(n):
        cols = rows_at(n * 512, 512, 512)
        out_ref[rows_at(n * 512, 512, 512), :] = dot_l(hb_ref[...], dhid_ref[:, cols]).astype(BF)
        out_ref[rows_at(FF + n * 512, 512, 512), :] = dot_l(act_ref[:, cols], bg_ref[...]).astype(BF)

    loop(FF // 512, column)


def count_norm(gb, index, grad, unit):
    gb[8 * index : 8 * index + 8, :] += fold8(grad * unit)
    gb[24 + 8 * index : 32 + 8 * index, :] += fold8(grad)


def forward_body(group, r):
    moves = Moves(r.sems)
    is_encoder = r.role[0] == 0
    first = group * GP
    got_x = moves.start(r.x_in.at[first * SLOT : (first + GP) * SLOT, :], r.x)
    got_in = moves.start(r.w_in, r.win)
    got_out = moves.start(r.w_out, r.wout)
    got_up = moves.start(r.w_up, r.wup)
    got_down = moves.start(r.w_down, r.wdown)
    zero_rows(r.qkv, GR)
    moves.wait(got_x)
    for p in range(GP):
        r.xp[p * PR : (p + 1) * PR, :] = r.x[p * SLOT : p * SLOT + PR, :]
    moves.wait(got_in)

    def column(n):
        cols = rows_at(n * 512, 512, 512)
        r.qkv[0:GR, cols] = dot(r.xp[...], r.win[:, cols]).astype(BF)

    loop(3, column)
    moves.start(r.xp, r.xp_out)
    moves.start(r.qkv.at[0:GR, :], r.qkv_out)
    attend_forward(lambda p: r.lengths[first + p], r.qkv, 0, r.qkv, 512, r.qkv, 1024, r.mix)
    moves.start(r.mix, r.mix_out)
    moves.wait(got_out)
    unit, scale = norm_of(r.xp[...].astype(F32) + dot(r.mix[...], r.wout[...]))
    r.unit0[...] = unit.astype(BF)
    r.sc0[...] = scale
    r.h[...] = unit * r.gains[0:1, :] + r.biases[0:1, :]
    moves.start(r.unit0, r.unit0_out)
    moves.start(r.sc0, r.sc0_out)
    moves.start(r.h, r.h_out)
    moves.wait(got_up, got_down)
    first_used = moves.used

    @pl.when(is_encoder)
    def _():
        own = Moves(r.sems)
        own.used = first_used
        summed = feed_forward(r.wup, r.wdown, r.h, r.hb, r.hid, r.act)
        unit, scale = norm_of(summed)
        r.unit1[...] = unit.astype(BF)
        r.sc1[...] = scale
        unit, scale = norm_of(unit * r.gains[1:2, :] + r.biases[1:2, :])
        r.unit2[...] = unit.astype(BF)
        r.sc2[...] = scale
        memory = unit * r.gains[2:3, :] + r.biases[2:3, :]
        r.mem[...] = memory.astype(BF)
        r.state[...] = memory
        row = lax.broadcasted_iota(jnp.int32, (16, D), 0)
        place = lax.broadcasted_iota(jnp.int32, (PR, D), 0)
        for p in range(GP):
            length = r.lengths[first + p]
            last = r.mem[(p + 1) * PR - 16 : (p + 1) * PR, :].astype(F32)
            r.mem[(p + 1) * PR - 16 : (p + 1) * PR, :] = jnp.where(
                row < 8, last, length.astype(F32)
            ).astype(BF)
            r.states[p * SLOT : p * SLOT + PR, :] = jnp.where(
                place < length, r.state[p * PR : (p + 1) * PR, :], 0.0
            )
            r.states[p * SLOT + PR : (p + 1) * SLOT, :] = jnp.zeros((SLOT - PR, D), F32)
        own.start(r.mem, r.mem_out)
        for name in ("hb", "hid", "act", "unit1", "sc1", "unit2", "sc2"):
            own.start(getattr(r, name), getattr(r, name + "_out"))
        own.start(r.states, r.states_out.at[first * SLOT : (first + GP) * SLOT, :])
        own.finish()

    moves.finish()


def decode_body(group, r):
    first = group * GP

    @pl.when(r.role[0] == 1)
    def _():
        moves = Moves(r.sems)
        core = r.role[1]
        got_h = moves.start(r.h_in, r.h)
        got_q = moves.start(r.wq_in, r.wq)
        got_mem = moves.start(r.mem_in, r.mem)
        got_mine = moves.start(r.mine_in, r.wkv.at[pl.ds(pl.multiple_of(core * D, D), D), :])
        got_other = moves.start(r.other_in, r.wkv.at[pl.ds(pl.multiple_of((1 - core) * D, D), D), :])
        got_o = moves.start(r.wo_in, r.wo)
        got_up = moves.start(r.w_up, r.wup)
        got_down = moves.start(r.w_down, r.wdown)
        got_cot = moves.start(r.cot_in.at[first * SLOT : (first + GP) * SLOT, :], r.cot)
        zero_rows(r.q, GR)
        zero_rows(r.gm, GR)
        r.gb[...] = jnp.zeros_like(r.gb)
        moves.wait(got_h, got_q)
        r.fb[...] = r.h[...].astype(BF)
        r.q[0:GR, :] = dot(r.fb[...], r.wq[...]).astype(BF)
        moves.start(r.fb, r.fb_out)
        moves.wait(got_mem, got_mine, got_other)
        r.k[...] = dot(r.mem[...], r.wkv[0:D, :]).astype(BF)
        r.v[...] = dot(r.mem[...], r.wkv[D : 2 * D, :]).astype(BF)

        def length_of(p):
            last = r.mem[rows_at(p * PR + PR - 16, 16), :].astype(F32)
            return last[15:16, :].astype(jnp.int32)

        attend_forward(length_of, r.q, 0, r.k, 0, r.v, 0, r.mix)
        moves.start(r.mix, r.mix_out)
        moves.wait(got_o)
        unit, scale = norm_of(r.h[...] + dot(r.mix[...], r.wo[...]))
        r.unit1[...] = unit.astype(BF)
        r.sc1[...] = scale
        r.h[...] = unit * r.gains[1:2, :] + r.biases[1:2, :]
        moves.wait(got_up, got_down, got_cot)
        for p in range(GP):
            place = lax.broadcasted_iota(jnp.int32, (PR, 1), 0)
            valid = jnp.where(place < r.lengths[first + p], 1.0, 0.0)
            r.valid[p * PR : (p + 1) * PR, :] = valid
            r.ds[p * PR : (p + 1) * PR, :] = r.cot[p * SLOT : p * SLOT + PR, :].astype(F32) * valid
        summed = feed_forward(r.wup, r.wdown, r.h, r.hb, r.hid, r.act)
        moves.start(r.hb, r.hb_out)
        moves.start(r.act, r.act_out)
        unit, scale = norm_of(summed)
        grad = r.ds[...]
        r.h[...] = (unit * r.gains[2:3, :] + r.biases[2:3, :]) * r.valid[...]
        count_norm(r.gb, 2, grad, unit)
        grad_sum = norm_back(grad, unit, scale, r.gains[2:3, :])
        r.bg2[...] = grad_sum.astype(BF)
        r.ds[...] = grad_sum
        moves.start(r.bg2, r.bg2_out)
        for p in range(GP):
            r.states[p * SLOT : p * SLOT + PR, :] = r.h[p * PR : (p + 1) * PR, :]
            r.states[p * SLOT + PR : (p + 1) * SLOT, :] = jnp.zeros((SLOT - PR, D), F32)
        moves.start(r.states, r.states_out.at[first * SLOT : (first + GP) * SLOT, :])
        grad = feed_back(r.wup, r.wdown, r.ds, r.bg2, r.hid, r.dhid)
        moves.start(r.dhid, r.dhid_out)
        unit = r.unit1[...].astype(F32)
        count_norm(r.gb, 1, grad, unit)
        grad_sum = norm_back(grad, unit, r.sc1[...], r.gains[1:2, :])
        r.bg1[...] = grad_sum.astype(BF)
        r.h[...] = grad_sum
        moves.start(r.bg1, r.bg1_out)
        moves.start(r.gb, r.gb_out)
        r.gm[0:GR, :] = dot_t(r.bg1[...], r.wo[...]).astype(BF)
        attend_backward(length_of, r.q, 0, r.k, 0, r.v, 0, r.gm, r.dq, 0, r.dk, 0, r.dv, 0)
        moves.start(r.dq, r.dq_out)
        moves.start(r.dk, r.dk_out)
        moves.start(r.dv, r.dv_out)
        r.gmem[...] = (
            dot_t(r.dk[...], r.wkv[0:D, :]) + dot_t(r.dv[...], r.wkv[D : 2 * D, :])
        ).astype(BF)
        moves.start(r.gmem, r.gmem_out)
        r.ds[...] = r.h[...] + dot_t(r.dq[...], r.wq[...])
        moves.start(r.ds, r.dh_out)
        moves.finish()


def self_back_part(r, moves, got, first):
    zero_rows(r.gm, GR)
    zero_rows(r.qkv, GR)
    moves.wait(*got[:-1])
    grad = r.dh[...]
    unit = r.unit0[...].astype(F32)
    count_norm(r.gb, 0, grad, unit)
    grad = norm_back(grad, unit, r.sc0[...], r.gains[0:1, :])
    r.bg[...] = grad.astype(BF)
    r.dh[...] = grad
    moves.start(r.dh, r.ds_out)
    moves.start(r.bg, r.bg_out)
    r.gm[0:GR, :] = dot_t(r.bg[...], r.wout[...]).astype(BF)
    moves.wait(got[-1])
    attend_backward(
        lambda p: r.lengths[first + p],
        r.qkv, 0, r.qkv, 512, r.qkv, 1024, r.gm, r.dqkv, 0, r.dqkv, 512, r.dqkv, 1024,
    )
    moves.start(r.dqkv, r.dqkv_out)


def self_back_loads(r, moves, group):
    return [
        moves.start(getattr(r, f"unit0_{group}"), r.unit0),
        moves.start(getattr(r, f"sc0_{group}"), r.sc0),
        moves.start(r.w_out, r.wout),
        moves.start(getattr(r, f"qkv_{group}"), r.qkv.at[0:GR, :]),
    ]


def feed_back_loads(r, moves, group):
    return [
        moves.start(getattr(r, f"{name}_{group}"), getattr(r, name))
        for name in ("gmem", "unit2", "sc2", "unit1", "sc1")
    ] + [
        moves.start(r.w_down, r.wdown),
        moves.start(getattr(r, f"hid_{group}"), r.hid),
        moves.start(r.w_up, r.wup),
    ]


def feed_back_part(r, moves, got, bg, dhid):
    moves.wait(*got[:5])
    grad = r.gmem[...].astype(F32)
    unit = r.unit2[...].astype(F32)
    count_norm(r.gb, 2, grad, unit)
    grad = norm_back(grad, unit, r.sc2[...], r.gains[2:3, :])
    unit = r.unit1[...].astype(F32)
    count_norm(r.gb, 1, grad, unit)
    grad = norm_back(grad, unit, r.sc1[...], r.gains[1:2, :])
    bg[...] = grad.astype(BF)
    r.dh[...] = grad
    moves.wait(*got[5:])
    r.dh[...] = feed_back(r.wup, r.wdown, r.dh, bg, r.hid, dhid)


def stacked_loads(r, moves, name, held):
    zero_rows(held, 2 * GR)
    return [
        moves.start(getattr(r, f"{name}_{g}"), held.at[g * GR : (g + 1) * GR, :]) for g in range(2)
    ]


def cross_body(r):
    @pl.when(r.role[0] == 0)
    def _():
        moves = Moves(r.sems)
        got = feed_back_loads(r, moves, 0)
        got_self = self_back_loads(r, moves, 0)
        r.gb[...] = jnp.zeros_like(r.gb)
        feed_back_part(r, moves, got, r.fbg, r.dhid)
        moves.start(r.dhid, r.dhid_out)
        moves.start(r.fbg, r.fbg_out)
        self_back_part(r, moves, got_self, 0)
        moves.start(r.gb, r.gb_out)
        moves.finish()

    @pl.when(r.role[0] == 1)
    def _():
        moves = Moves(r.sems)
        names = ("hb2", "dhid2", "act2", "bg2")
        got = [c for name in names for c in stacked_loads(r, moves, name, getattr(r, "all_" + name))]
        moves.wait(*got)
        feed_weight_grads(r.all_hb2, r.all_dhid2, r.all_act2, r.all_bg2, r.gf)
        send_feed_grads(r, moves)
        moves.finish()


def send_feed_grads(r, moves):
    moves.start(r.gf, r.gf_out)


def cross_grads_body(r):
    @pl.when(r.role[0] == 1)
    def _():
        moves = Moves(r.sems)
        names = ("mem", "dk", "dv", "fb", "dq", "mixc", "bg1")
        got = {name: stacked_loads(r, moves, name, getattr(r, "all_" + name)) for name in names}
        moves.wait(*got["mem"], *got["dk"], *got["dv"])
        r.gx[0:D, :] = dot_l(r.all_mem[...], r.all_dk[...]).astype(BF)
        r.gx[D : 2 * D, :] = dot_l(r.all_mem[...], r.all_dv[...]).astype(BF)
        start_halves(moves, r.role[1], r.gx, r.keep_out.at[0:D, :], r.send_out.at[0:D, :])
        moves.wait(*got["fb"], *got["dq"], *got["mixc"], *got["bg1"])
        r.gc[0:D, :] = dot_l(r.all_fb[...], r.all_dq[...]).astype(BF)
        r.gc[D : 2 * D, :] = dot_l(r.all_mixc[...], r.all_bg1[...]).astype(BF)
        start_halves(
            moves, r.role[1], r.gc, r.keep_out.at[D : 2 * D, :], r.send_out.at[D : 2 * D, :]
        )
        moves.finish()


def feed_body(r):
    @pl.when(r.role[0] == 0)
    def _():
        moves = Moves(r.sems)
        got = feed_back_loads(r, moves, 1)
        got_hb = stacked_loads(r, moves, "hb", r.all_hb)
        got_act = stacked_loads(r, moves, "act", r.all_act)
        zero_rows(r.all_dhid, 2 * GR)
        zero_rows(r.all_bg, 2 * GR)
        got_first = [
            moves.start(r.dhid_0, r.all_dhid.at[0:GR, :]), moves.start(r.fbg_0, r.all_bg.at[0:GR, :]),
        ]
        r.gb[...] = jnp.zeros_like(r.gb)
        feed_back_part(
            r, moves, got, r.all_bg.at[GR : 2 * GR, :], r.all_dhid.at[GR : 2 * GR, :]
        )
        moves.start(r.dh, r.dh_out)
        moves.start(r.gb, r.gb_out)
        moves.wait(*got_hb, *got_act, *got_first)
        feed_weight_grads(r.all_hb, r.all_dhid, r.all_act, r.all_bg, r.gf)
        send_feed_grads(r, moves)
        moves.finish()

    @pl.when(r.role[0] == 1)
    def _():
        moves = Moves(r.sems)
        got_dh = moves.start(r.dh_0, r.dh)
        got = self_back_loads(r, moves, 0)
        r.gb[...] = jnp.zeros_like(r.gb)
        moves.wait(got_dh)
        self_back_part(r, moves, got, 0)
        moves.start(r.gb, r.gb_out)
        moves.finish()


def self_body(r):
    moves = Moves(r.sems)
    got_dh = moves.start(r.dh_1, r.dh)
    got = self_back_loads(r, moves, 1)
    r.gb[...] = jnp.zeros_like(r.gb)
    moves.wait(got_dh)
    self_back_part(r, moves, got, GP)
    moves.start(r.gb, r.gb_out)
    moves.finish()


EXTRA = 64


def self_weights_body(r):
    moves = Moves(r.sems)
    got_x = stacked_loads(r, moves, "xp", r.xp)
    got_qkv = stacked_loads(r, moves, "dqkv", r.dqkv)
    got_mix = stacked_loads(r, moves, "mix", r.mix)
    got_bg = stacked_loads(r, moves, "bg", r.bg)
    got_in = moves.start(r.w_in, r.win)
    got_ds = stacked_loads(r, moves, "ds", r.ds)
    part = 2 * D + EXTRA
    enc = r.gb_cross[...]
    dec = r.gb_dec0[...] + r.gb_dec1[...]
    picked = jnp.where(r.role[0] == 0, enc, dec) + r.gb_feed[...] + r.gb_self[...]
    small = jnp.concatenate(
        [jnp.sum(picked[8 * i : 8 * i + 8, :], axis=0, keepdims=True) for i in range(6)]
        + [jnp.zeros((EXTRA - 6, D), F32)],
        axis=0,
    ).astype(BF)
    r.ga[2 * D : part, :] = small
    r.ga[part + 2 * D : 2 * part, :] = small
    moves.wait(*got_x, *got_qkv)
    r.ga[0:D, :] = dot_l(r.xp[...], r.dqkv[:, 0:D]).astype(BF)
    r.ga[D : 2 * D, :] = dot_l(r.xp[...], r.dqkv[:, D : 2 * D]).astype(BF)
    r.ga[part : part + D, :] = dot_l(r.xp[...], r.dqkv[:, 2 * D : 3 * D]).astype(BF)
    moves.wait(*got_mix, *got_bg)
    r.ga[part + D : part + 2 * D, :] = dot_l(r.mix[...], r.bg[...]).astype(BF)
    start_halves(moves, r.role[1], r.ga, r.keep_out, r.send_out)
    moves.wait(got_in, *got_ds)

    def leave(p):
        at = rows_at(p * PR, PR)
        to = rows_at(p * SLOT, PR)
        r.dx[to, :] = r.ds[at, :] + dot_t(r.dqkv[at, :], r.win[...])
        r.dx[rows_at(p * SLOT + PR, SLOT - PR), :] = jnp.zeros((SLOT - PR, D), F32)

    loop(2 * GP, leave)
    moves.start(r.dx, r.grads_out)
    moves.finish()


def start_halves(moves, core, held, keep, send):
    half = held.shape[0] // 2
    for target, shift in ((keep, 0), (send, 1)):
        start = pl.multiple_of(((core + shift) & 1) * half, 16)
        moves.start(held.at[pl.ds(start, half), :], target)


def place_blocks(core, moves, own, other, held, firsts):
    got = []
    for group, shift in ((own, 0), (other, 1)):
        start = 0
        for ref in group:
            size = ref.shape[0]
            place = pl.multiple_of(((core + shift) & 1) * firsts + start, 16)
            got.append(moves.start(ref, held.at[pl.ds(place, size), :]))
            start += size
    return got


def place_feed_body(r):
    moves = Moves(r.sems)
    got = [
        moves.start(r.gf.at[i * D : (i + 1) * D, :], r.held.at[i * D : (i + 1) * D, :])
        for i in range(8)
    ]
    for i in range(4):
        moves.wait(got[4 + i])
        at = slice(i * D, (i + 1) * D)
        r.down[at, :] = r.held[FF + i * D : FF + (i + 1) * D, :].astype(F32)
        moves.start(r.down.at[at, :], r.down_out.at[at, :])
    moves.wait(*got[:4])
    for i in range(4):
        at = slice(i * 128, (i + 1) * 128)
        for n in range(4):
            r.up[at, n * D : (n + 1) * D] = r.held[
                n * D + i * 128 : n * D + (i + 1) * 128, :
            ].astype(F32)
        moves.start(r.up.at[at, :], r.up_out.at[at, :])
    moves.finish()


def place_rest_body(r):
    moves = Moves(r.sems)
    part = 2 * D + EXTRA
    core = r.role[1]
    got_c = place_blocks(core, moves, [r.c], [r.c_other], r.held_c, D)
    got = place_blocks(core, moves, [r.da, r.db], [r.da_other, r.db_other], r.held, part)
    moves.wait(*got_c)
    r.ca[...] = r.held_c[0:D, :].astype(F32)
    r.cb[...] = r.held_c[D : 2 * D, :].astype(F32)
    moves.start(r.ca, r.ca_out)
    moves.start(r.cb, r.cb_out)
    moves.wait(*got)
    r.wout[...] = r.held[part + D : part + 2 * D, :].astype(F32)
    moves.start(r.wout, r.out_out)
    for n, start in enumerate((0, D, part)):
        r.win[:, n * D : (n + 1) * D] = r.held[start : start + D, :].astype(F32)
    moves.start(r.win, r.in_out)
    small = r.held[2 * D : 2 * D + 16, :].astype(F32)
    r.gains[...] = small[0:3, :]
    r.biases[...] = small[3:6, :]
    moves.start(r.gains, r.gains_out)
    moves.start(r.biases, r.biases_out)
    moves.finish()


ANY = pl.BlockSpec(memory_space=pl.ANY)
WHOLE = pl.BlockSpec(memory_space=pltpu.VMEM)
SCALARS = pl.BlockSpec(memory_space=pltpu.SMEM)


class Refs:
    def __init__(self, names, refs):
        for name, ref in zip(names, refs):
            setattr(self, name, ref)


def call(body, name, flops, ins, outs, scratch, copies, aliases=None, whole=()):
    scalars = ("role", "lengths")
    specs = [SCALARS if n in scalars else WHOLE if n in whole else ANY for n in ins]
    names = [*ins, *outs, *scratch, "sems"]
    position = list(ins).index
    results = list(outs).index

    def kernel(*refs):
        body(Refs(names, refs))

    found = pl.pallas_call(
        kernel,
        out_shape=[jax.ShapeDtypeStruct(s, t) for s, t in outs.values()],
        in_specs=specs,
        out_specs=[ANY] * len(outs),
        scratch_shapes=[pltpu.VMEM(s, t) for s, t in scratch.values()]
        + [pltpu.SemaphoreType.DMA((copies,))],
        input_output_aliases={position(i): results(o) for i, o in (aliases or {}).items()},
        compiler_params=pltpu.CompilerParams(vmem_limit_bytes=60 * 1024 * 1024),
        cost_estimate=pl.CostEstimate(
            flops=flops, bytes_accessed=flops // 1000, transcendentals=0
        ),
        name=name,
    )(*ins.values())
    return dict(zip(outs, found))


def swapped(x, mask):
    size = lax.axis_size("dp")
    return lax.ppermute(x, "dp", [(i, i ^ mask) for i in range(size)])


def added(keep, recv):
    return (keep.astype(F32) + recv.astype(F32)).astype(BF)


def lowered(cur, mask, bit):
    half = cur.shape[0] // 2
    recv = swapped(lax.dynamic_slice_in_dim(cur, (1 - bit) * half, half, 0), mask)
    return added(lax.dynamic_slice_in_dim(cur, bit * half, half, 0), recv)


def raised(cur, mask, bit):
    other = swapped(cur, mask)
    return jnp.where(
        bit == 0, jnp.concatenate([cur, other], 0), jnp.concatenate([other, cur], 0)
    )


class Sums:
    def __init__(self):
        size = lax.axis_size("dp")
        place = lax.axis_index("dp")
        self.masks = [1 << i for i in range(1, size.bit_length() - 1)]
        self.bits = {mask: (place >> (mask.bit_length() - 1)) & 1 for mask in self.masks}

    def order(self, turn):
        masks = self.masks
        return masks if turn == 0 else masks[1:] + masks[:1]

    def down(self, parts, turns, first, last):
        for step in range(first, last):
            parts = [
                lowered(p, self.order(t)[step], self.bits[self.order(t)[step]])
                for p, t in zip(parts, turns)
            ]
        return parts

    def up(self, parts, turns):
        for step in reversed(range(len(self.masks))):
            parts = [
                raised(p, self.order(t)[step], self.bits[self.order(t)[step]])
                for p, t in zip(parts, turns)
            ]
        return parts


def on_device(
    embeds, lengths, attn_in, attn_out, cross_a, cross_b, ffn_up, ffn_down,
    norm_gains, norm_biases, cotangent,
):
    x, own = embeds[0], lengths[0]
    win, wout, wa, wb, wup, wdown = (
        attn_in[0], attn_out[0], cross_a[0], cross_b[0], ffn_up[0], ffn_down[0],
    )
    gains, biases = norm_gains[0], norm_biases[0]
    slots = 2 * GP * SLOT
    pipe = lax.axis_index("pipe")
    is_encoder = pipe == 0
    odd = lax.axis_index("dp") & 1
    role = jnp.stack([pipe, odd]).astype(jnp.int32)
    onward, back = [(0, 1)], [(1, 0)]

    def bf(*shape):
        return (shape, BF)

    def f32(*shape):
        return (shape, F32)

    flat, flat_f, wide, one, triple = bf(GR, D), f32(GR, D), bf(GR, FF), f32(GR, 1), bf(GR, 3 * D)
    full, slot, slot_f = f32(slots, D), bf(GP * SLOT, D), f32(GP * SLOT, D)
    square, up_w, down_w, in_w = bf(D, D), bf(D, FF), bf(FF, D), bf(D, 3 * D)
    tall, counts = bf(TALL, D), f32(48, D)
    base = dict(role=role, lengths=own, gains=gains, biases=biases)
    whole = ("gains", "biases")

    mine = lax.ppermute(jnp.where(odd == 0, wa, wb), "pipe", onward)

    fwd, mem_in, states = [], [], None
    for g in range(2):
        ins = dict(base, x_in=x, w_in=win, w_out=wout, w_up=wup, w_down=wdown)
        if g:
            ins["states_in"] = states
        fwd.append(
            call(
                functools.partial(forward_body, g), f"forward_{g}", 4_000_000_000, ins,
                dict(
                    h_out=flat_f, xp_out=flat, qkv_out=triple, mix_out=flat, unit0_out=flat, sc0_out=one,
                    mem_out=flat, hb_out=flat, hid_out=wide, act_out=wide, unit1_out=flat, sc1_out=one,
                    unit2_out=flat, sc2_out=one, states_out=full,
                ),
                dict(
                    x=slot, win=in_w, wout=square, wup=up_w, wdown=down_w, h=flat_f, xp=flat,
                    qkv=bf(TALL, 3 * D), mix=flat, unit0=flat, sc0=one, mem=flat, hb=flat, hid=wide,
                    act=wide, unit1=flat, sc1=one, unit2=flat, sc2=one, state=flat_f, states=slot_f,
                ),
                24, aliases={"states_in": "states_out"} if g else None, whole=whole,
            )
        )
        states = fwd[g]["states_out"]
        memory = fwd[g]["mem_out"]
        if g == 0:
            mine, memory = lax.optimization_barrier((mine, memory))
            other = swapped(mine, 1)
        mem_in.append(lax.ppermute(memory, "pipe", onward))

    dec, gmem_in = [], []
    for g in range(2):
        dec.append(
            call(
                functools.partial(decode_body, g), f"decode_{g}", 8_000_000_000,
                dict(
                    base, h_in=fwd[g]["h_out"], mem_in=mem_in[g], cot_in=cotangent, wq_in=wa, wo_in=wb,
                    mine_in=mine, other_in=other, w_up=wup, w_down=wdown, states_in=states,
                ),
                dict(
                    states_out=full, gmem_out=flat, dh_out=flat_f, fb_out=flat, dq_out=flat, mix_out=flat,
                    bg1_out=flat, dk_out=flat, dv_out=flat, hb_out=flat, dhid_out=wide, act_out=wide,
                    bg2_out=flat, gb_out=counts,
                ),
                dict(
                    h=flat_f, mem=flat, cot=slot, wq=square, wo=square, wkv=bf(2 * D, D), wup=up_w,
                    wdown=down_w, states=slot_f, gmem=flat, fb=flat, q=tall, k=flat, v=flat, mix=flat,
                    dq=flat, dk=flat, dv=flat, bg1=flat, hb=flat, hid=wide, dhid=wide, act=wide, bg2=flat,
                    unit1=flat, sc1=one, valid=one, ds=flat_f, gm=tall, gb=counts,
                ),
                24, aliases={"states_in": "states_out"}, whole=whole,
            )
        )
        states = dec[g]["states_out"]
        gmem_in.append(lax.ppermute(dec[g]["gmem_out"], "pipe", back))

    def of(group, results, **names):
        return {f"{k}_{group}": results[v] for k, v in names.items()}

    enc_names = dict(
        unit2="unit2_out", sc2="sc2_out", unit1="unit1_out", sc1="sc1_out", hid="hid_out",
    )
    self_names = dict(unit0="unit0_out", sc0="sc0_out", qkv="qkv_out")
    back_scratch = dict(
        gmem=flat, unit2=flat, sc2=one, unit1=flat, sc1=one, wdown=down_w, hid=wide, wup=up_w, dh=flat_f,
    )
    self_scratch = dict(
        unit0=flat, sc0=one, wout=square, qkv=bf(TALL, 3 * D), bg=flat, gm=tall, dqkv=triple, gb=counts,
    )
    dec_names = dict(
        dk="dk_out", dv="dv_out", fb="fb_out", dq="dq_out", mixc="mix_out", bg1="bg1_out", hb2="hb_out",
        dhid2="dhid_out", act2="act_out", bg2="bg2_out",
    )
    all_flat, all_wide = bf(ALL, D), bf(ALL, FF)
    cross_names = {k: v for k, v in dec_names.items() if k in ("dk", "dv", "fb", "dq", "mixc", "bg1")}
    feed_names = {k: v for k, v in dec_names.items() if k not in cross_names}
    ins = dict(base, w_up=wup, w_down=wdown, w_out=wout, gmem_0=gmem_in[0])
    ins.update(of(0, fwd[0], **enc_names, **self_names))
    for g in range(2):
        ins.update(of(g, dec[g], **feed_names))
    grads = dict(gf=bf(2 * FF, D))
    feed_outs = dict(gf_out=bf(2 * FF, D))
    cross = call(
        cross_body, "cross_back", 1_000, ins,
        dict(
            dhid_out=wide, fbg_out=flat, ds_out=flat_f, bg_out=flat, dqkv_out=triple, gb_out=counts,
            **feed_outs,
        ),
        dict(
            **back_scratch, **self_scratch, fbg=flat, dhid=wide,
            all_hb2=all_flat, all_dhid2=all_wide, all_act2=all_wide, all_bg2=all_flat, **grads,
        ),
        40, whole=whole,
    )
    ins = dict(role=role)
    for g in range(2):
        ins.update(of(g, dec[g], **cross_names))
        ins[f"mem_{g}"] = mem_in[g]
    ins["dk_1"], fbg = lax.optimization_barrier((ins["dk_1"], cross["fbg_out"]))
    crossed = call(
        cross_grads_body, "cross_grads", 1_000, ins,
        dict(keep_out=bf(2 * D, D), send_out=bf(2 * D, D)),
        dict(
            **{"all_" + n: all_flat for n in ("mem", *cross_names)}, gx=bf(2 * D, D), gc=bf(2 * D, D),
        ),
        32,
    )
    crossed_keep, crossed_send, fbg = lax.optimization_barrier(
        (crossed["keep_out"], crossed["send_out"], fbg)
    )
    crossed_sent = swapped(crossed_send, 1)

    ins = dict(
        base, w_up=wup, w_down=wdown, w_out=wout, gmem_1=gmem_in[1], dhid_0=cross["dhid_out"],
        fbg_0=fbg, hb_0=fwd[0]["hb_out"], hb_1=fwd[1]["hb_out"], act_0=fwd[0]["act_out"],
        act_1=fwd[1]["act_out"], dh_0=dec[0]["dh_out"], dh_in=dec[1]["dh_out"],
        ds_in=cross["ds_out"], bg_in=cross["bg_out"], dqkv_in=cross["dqkv_out"],
        gf_in=cross["gf_out"],
    )
    ins.update(of(1, fwd[1], **enc_names))
    ins.update(of(0, fwd[0], **self_names))
    feed = call(
        feed_body, "feed_back", 9_000_000_000, ins,
        dict(
            dh_out=flat_f, ds_out=flat_f, bg_out=flat, dqkv_out=triple, gb_out=counts, **feed_outs,
        ),
        dict(
            **back_scratch, **self_scratch, all_hb=all_flat, all_act=all_wide, all_dhid=all_wide,
            all_bg=all_flat, **grads,
        ),
        32,
        aliases={
            name + "_in": name + "_out"
            for name in ("dh", "ds", "bg", "dqkv", "gf")
        },
        whole=whole,
    )
    gf = lax.psum(feed["gf_out"], "dp")
    crossed_x = added(crossed_keep[:D], crossed_sent[:D])
    crossed_c = added(crossed_keep[D:], crossed_sent[D:])
    sums = Sums()
    depth = len(sums.masks)
    part = 2 * D + EXTRA

    def tail():
        last = call(
            self_body, "self_back", 3_000_000_000,
            dict(base, dh_1=feed["dh_out"], w_out=wout, **of(1, fwd[1], **self_names)),
            dict(ds_out=flat_f, bg_out=flat, dqkv_out=triple, gb_out=counts),
            dict(**self_scratch, dh=flat_f),
            16, whole=whole,
        )
        gx_in = lax.ppermute(crossed_x, "pipe", back)
        gx_in, ds = lax.optimization_barrier((gx_in, last["ds_out"]))
        c_keep = jnp.where(is_encoder, gx_in, crossed_c)
        early = sums.down([c_keep], (0,), 0, 1)
        ins = dict(
            role=role, gb_cross=cross["gb_out"], gb_dec0=dec[0]["gb_out"], gb_dec1=dec[1]["gb_out"],
            gb_feed=feed["gb_out"], gb_self=last["gb_out"], w_in=win, ds_0=feed["ds_out"], ds_1=ds,
            bg_0=feed["bg_out"], bg_1=last["bg_out"], dqkv_0=feed["dqkv_out"], dqkv_1=last["dqkv_out"],
        )
        for g in range(2):
            ins.update(of(g, fwd[g], xp="xp_out", mix="mix_out"))
        found = call(
            self_weights_body, "self_weights", 8_000_000_000, ins,
            dict(grads_out=full, keep_out=bf(part, D), send_out=bf(part, D)),
            dict(
                ds=f32(ALL, D), bg=all_flat, dqkv=bf(ALL, 3 * D), xp=all_flat, mix=all_flat, win=in_w,
                dx=full, ga=bf(2 * part, D),
            ),
            20, whole=("gb_cross", "gb_dec0", "gb_dec1", "gb_feed", "gb_self"),
        )
        a_keep = added(found["keep_out"], swapped(found["send_out"], 1))
        early = sums.down(early, (0,), 1, depth)
        late = sums.down([a_keep[:D], a_keep[D:]], (0, 1), 0, depth)
        parts = sums.up(early + late, (0, 0, 1))
        return found["grads_out"], parts, [swapped(p, 1) for p in parts]

    shapes = jax.eval_shape(tail)
    input_grads, parts, others = lax.cond(
        own[0] >= 0,
        tail,
        lambda: jax.tree.map(lambda leaf: jnp.zeros(leaf.shape, leaf.dtype), shapes),
    )
    placed = call(
        place_rest_body, "place_rest", 1_000_000_000,
        dict(
            role=role, c=parts[0], da=parts[1], db=parts[2],
            c_other=others[0], da_other=others[1], db_other=others[2],
        ),
        dict(
            in_out=f32(D, 3 * D), out_out=f32(D, D), gains_out=f32(3, D), biases_out=f32(3, D),
            ca_out=f32(D, D), cb_out=f32(D, D),
        ),
        dict(
            held=bf(2 * part, D), win=f32(D, 3 * D), wout=f32(D, D), gains=f32(3, D), biases=f32(3, D),
            held_c=bf(2 * D, D), ca=f32(D, D), cb=f32(D, D),
        ),
        16,
    )
    placed |= call(
        place_feed_body, "place_feed", 1_000_000_000,
        dict(gf=gf),
        dict(up_out=f32(D, FF), down_out=f32(FF, D)),
        dict(held=bf(2 * FF, D), up=f32(D, FF), down=f32(FF, D)),
        16,
    )
    outs = (
        states, input_grads, placed["in_out"], placed["out_out"], placed["ca_out"], placed["cb_out"],
        placed["up_out"], placed["down_out"], placed["gains_out"], placed["biases_out"],
    )
    return tuple(out[None] for out in outs)


def solution(mesh):
    cut = P("pipe", "dp", None)
    held = P("pipe", None, None)
    return jax.shard_map(
        on_device,
        mesh=mesh,
        in_specs=(cut, P("pipe", "dp")) + (held,) * 8 + (P("dp", None),),
        out_specs=(cut, cut) + (held,) * 8,
        check_vma=False,
    )
```

```python
import functools

import jax
import jax.numpy as jnp
from jax import lax
from jax.experimental import pallas as pl
from jax.experimental.pallas import tpu as pltpu
from jax.sharding import PartitionSpec as P

HEADS = 8
D = 512
FF = 2048
SLOT = 256
PR = 208
GP = 2
GR = GP * PR
TALL = 512
ALL = 896
NORM_EPSILON = 1e-05
BF = jnp.bfloat16
F32 = jnp.float32
CORE_C = 0.7978845608028654
CUBE_C = 0.044715


def dot(a, b):
    return lax.dot_general(a, b, (((1,), (0,)), ((), ())), preferred_element_type=F32)


def dot_t(a, b):
    return lax.dot_general(a, b, (((1,), (1,)), ((), ())), preferred_element_type=F32)


def dot_l(a, b):
    return lax.dot_general(a, b, (((0,), (0,)), ((), ())), preferred_element_type=F32)


def rows_at(start, size, step=16):
    return pl.ds(pl.multiple_of(start, step), size)


def loop(n, body):
    def run(i, carry):
        body(i)
        return carry

    lax.fori_loop(0, n, run, 0)


def gelu_and_slope(u):
    square = u * u
    bent = jnp.tanh(u * (CORE_C + CORE_C * CUBE_C * square))
    half = 0.5 + 0.5 * bent
    bend = (1.0 - bent) * (CORE_C + 3.0 * CORE_C * CUBE_C * square)
    return u * half, half * (1.0 + u * bend)


def norm_of(summed):
    center = summed - jnp.mean(summed, axis=-1, keepdims=True)
    spread = jnp.mean(center * center, axis=-1, keepdims=True)
    scale = lax.rsqrt(spread + NORM_EPSILON)
    return center * scale, scale


def norm_back(grad, unit, scale, gain):
    lifted = grad * gain
    first = jnp.mean(lifted, axis=-1, keepdims=True)
    second = jnp.mean(lifted * unit, axis=-1, keepdims=True)
    return scale * (lifted - first - unit * second)


def fold8(values):
    return jnp.sum(values.reshape(-1, 8, values.shape[-1]), axis=0)


class Moves:
    def __init__(self, sems):
        self.sems = sems
        self.used = 0
        self.open = []

    def start(self, source, target):
        copy = pltpu.make_async_copy(source, target, self.sems.at[self.used])
        self.used += 1
        copy.start()
        self.open.append(copy)
        return copy

    def wait(self, *copies):
        for copy in copies:
            copy.wait()
            self.open = [c for c in self.open if c is not copy]

    def finish(self):
        for copy in self.open:
            copy.wait()
        self.open = []


def lane_masks():
    lane = lax.broadcasted_iota(jnp.int32, (1, 128), 1)
    low = jnp.where(lane < 64, 1.0, 0.0).astype(BF)
    high = jnp.where(lane < 64, 0.0, 1.0).astype(BF)
    return low, high


def both_heads(rows, low, high):
    return jnp.concatenate([rows * low, rows * high], axis=0)


def merged_heads(stacked):
    lane = lax.broadcasted_iota(jnp.int32, (PR, 128), 1)
    return jnp.where(lane < 64, stacked[:PR], stacked[SLOT : SLOT + PR])


def probs_of(keys, queries, length):
    raw = dot_t(keys, queries)
    place = lax.broadcasted_iota(jnp.int32, raw.shape, 0)
    raw = jnp.where(place < length, raw, -1e30)
    top = jnp.max(raw, axis=0, keepdims=True)
    terms = jnp.exp(raw - top)
    total = jnp.sum(terms, axis=0, keepdims=True)
    return terms * (1.0 / total)


def attend_forward(length_of, q_ref, q_off, k_ref, k_off, v_ref, v_off, out_ref):
    low, high = lane_masks()
    low_q, high_q = low * 0.125, high * 0.125

    def pair(p):
        length = length_of(p)
        base = rows_at(p * PR, PR)
        wide = rows_at(p * PR, SLOT)
        for hp in range(4):
            at = hp * 128
            queries = both_heads(q_ref[wide, q_off + at : q_off + at + 128], low_q, high_q)
            keys = k_ref[base, k_off + at : k_off + at + 128]
            values = v_ref[base, v_off + at : v_off + at + 128]
            probs = probs_of(keys, queries, length).astype(BF)
            out_ref[base, at : at + 128] = merged_heads(dot_l(probs, values)).astype(BF)

    loop(GP, pair)


def attend_backward(
    length_of, q_ref, q_off, k_ref, k_off, v_ref, v_off, g_ref,
    dq_ref, dq_off, dk_ref, dk_off, dv_ref, dv_off,
):
    low, high = lane_masks()
    low_q, high_q = low * 0.125, high * 0.125

    def pair(p):
        length = length_of(p)
        base = rows_at(p * PR, PR)
        wide = rows_at(p * PR, SLOT)
        row = lax.broadcasted_iota(jnp.int32, (SLOT, 128), 0)
        for hp in range(4):
            at = hp * 128
            queries = both_heads(q_ref[wide, q_off + at : q_off + at + 128], low_q, high_q)
            keys = k_ref[base, k_off + at : k_off + at + 128]
            values = v_ref[base, v_off + at : v_off + at + 128]
            grads = jnp.where(row < PR, g_ref[wide, at : at + 128].astype(F32), 0.0).astype(BF)
            grads = both_heads(grads, low, high)
            probs = probs_of(keys, queries, length)
            grad_probs = dot_t(values, grads)
            mean = jnp.sum(probs * grad_probs, axis=0, keepdims=True)
            grad_raw = (probs * (grad_probs - mean)).astype(BF)
            dv_ref[base, dv_off + at : dv_off + at + 128] = dot(probs.astype(BF), grads).astype(BF)
            dk_ref[base, dk_off + at : dk_off + at + 128] = dot(grad_raw, queries).astype(BF)
            dq = merged_heads(dot_l(grad_raw, keys)) * 0.125
            dq_ref[base, dq_off + at : dq_off + at + 128] = dq.astype(BF)

    loop(GP, pair)


def zero_rows(ref, start):
    ref[start:, :] = jnp.zeros((ref.shape[0] - start, ref.shape[1]), ref.dtype)


def feed_forward(w_up, w_down, h_ref, hb_ref, slope_ref, act_ref, got_down):
    hb_ref[...] = h_ref[...].astype(BF)

    def column(n):
        cols = rows_at(n * 512, 512, 512)
        active, slope = gelu_and_slope(dot(hb_ref[...], w_up[:, cols]))
        slope_ref[:, cols] = slope.astype(BF)
        act_ref[:, cols] = active.astype(BF)

    loop(FF // 512, column)
    got_down()
    return h_ref[...] + dot(act_ref[...], w_down[...])


def feed_back(w_up, w_down, ds_ref, bg_ref, slope_ref, dhid_ref):
    def column(n):
        cols = rows_at(n * 512, 512, 512)
        grad_act = dot_t(bg_ref[...], w_down[cols, :])
        dhid_ref[:, cols] = (grad_act * slope_ref[:, cols].astype(F32)).astype(BF)

    loop(FF // 512, column)
    return ds_ref[...] + dot_t(dhid_ref[...], w_up[...])


def feed_weight_grads(hb_ref, dhid_ref, act_ref, bg_ref, out_ref):
    def column(n):
        cols = rows_at(n * 512, 512, 512)
        out_ref[rows_at(n * 512, 512, 512), :] = dot_l(hb_ref[...], dhid_ref[:, cols]).astype(BF)
        out_ref[rows_at(FF + n * 512, 512, 512), :] = dot_l(act_ref[:, cols], bg_ref[...]).astype(BF)

    loop(FF // 512, column)


def count_norm(gb, index, grad, unit):
    gb[8 * index : 8 * index + 8, :] += fold8(grad * unit)
    gb[24 + 8 * index : 32 + 8 * index, :] += fold8(grad)


def forward_body(group, r):
    moves = Moves(r.sems)
    is_encoder = r.role[0] == 0
    first = group * GP
    got_x = moves.start(r.x_in.at[first * SLOT : (first + GP) * SLOT, :], r.x)
    got_in = moves.start(r.w_in, r.win)
    zero_rows(r.qkv, GR)
    moves.wait(got_x)
    for p in range(GP):
        r.xp[p * PR : (p + 1) * PR, :] = r.x[p * SLOT : p * SLOT + PR, :]
    moves.wait(got_in)
    got_out = moves.start(r.w_out, r.wout)
    got_q = moves.start(r.w_q, r.wq)
    got_up = moves.start(r.w_up, r.wup)
    got_down = moves.start(r.w_down, r.wdown)

    def column(n):
        cols = rows_at(n * 512, 512, 512)
        r.qkv[0:GR, cols] = dot(r.xp[...], r.win[:, cols]).astype(BF)

    loop(3, column)
    moves.start(r.xp, r.xp_out)
    moves.start(r.qkv.at[0:GR, :], r.qkv_out)
    attend_forward(lambda p: r.lengths[first + p], r.qkv, 0, r.qkv, 512, r.qkv, 1024, r.mix)
    moves.start(r.mix, r.mix_out)
    moves.wait(got_out)
    unit, scale = norm_of(r.xp[...].astype(F32) + dot(r.mix[...], r.wout[...]))
    r.unit0[...] = unit.astype(BF)
    r.sc0[...] = scale
    r.h[...] = unit * r.gains[0:1, :] + r.biases[0:1, :]
    moves.start(r.unit0, r.unit0_out)
    moves.start(r.sc0, r.sc0_out)
    moves.start(r.h, r.h_out)
    moves.wait(got_up, got_down, got_q)
    first_used = moves.used

    @pl.when(jnp.logical_not(is_encoder))
    def _():
        own = Moves(r.sems)
        own.used = first_used
        r.hb[...] = r.h[...].astype(BF)
        r.q[...] = dot(r.hb[...], r.wq[...]).astype(BF)
        own.start(r.hb, r.hb_out)
        own.start(r.q, r.q_out)
        own.finish()

    @pl.when(is_encoder)
    def _():
        own = Moves(r.sems)
        own.used = first_used
        summed = feed_forward(r.wup, r.wdown, r.h, r.hb, r.hid, r.act, lambda: None)
        unit, scale = norm_of(summed)
        r.unit1[...] = unit.astype(BF)
        r.sc1[...] = scale
        unit, scale = norm_of(unit * r.gains[1:2, :] + r.biases[1:2, :])
        r.unit2[...] = unit.astype(BF)
        r.sc2[...] = scale
        memory = unit * r.gains[2:3, :] + r.biases[2:3, :]
        r.mem[...] = memory.astype(BF)
        r.state[...] = memory
        row = lax.broadcasted_iota(jnp.int32, (16, D), 0)
        place = lax.broadcasted_iota(jnp.int32, (PR, D), 0)
        for p in range(GP):
            length = r.lengths[first + p]
            last = r.mem[(p + 1) * PR - 16 : (p + 1) * PR, :].astype(F32)
            r.mem[(p + 1) * PR - 16 : (p + 1) * PR, :] = jnp.where(
                row < 8, last, length.astype(F32)
            ).astype(BF)
            r.states[p * SLOT : p * SLOT + PR, :] = jnp.where(
                place < length, r.state[p * PR : (p + 1) * PR, :], 0.0
            )
            r.states[p * SLOT + PR : (p + 1) * SLOT, :] = jnp.zeros((SLOT - PR, D), F32)
        own.start(r.mem, r.mem_out)
        for name in ("hb", "hid", "act", "unit1", "sc1", "unit2", "sc2"):
            own.start(getattr(r, name), getattr(r, name + "_out"))
        own.start(r.states, r.states_out.at[first * SLOT : (first + GP) * SLOT, :])
        own.finish()

    moves.finish()


def decode_body(group, r):
    first = group * GP

    @pl.when(r.role[0] == 1)
    def _():
        moves = Moves(r.sems)
        core = r.role[1]
        got_mine = moves.start(r.mine_in, r.wkv.at[pl.ds(pl.multiple_of(core * D, D), D), :])
        got_other = moves.start(r.other_in, r.wkv.at[pl.ds(pl.multiple_of((1 - core) * D, D), D), :])
        got_q = moves.start(r.q_in, r.q.at[0:GR, :])
        zero_rows(r.q, GR)
        zero_rows(r.gm, GR)
        r.gb[...] = jnp.zeros_like(r.gb)
        moves.wait(got_mine, got_other)
        got_h = moves.start(r.h_in, r.h)
        got_o = moves.start(r.wo_in, r.wo)
        got_up = moves.start(r.w_up, r.wup)
        got_down = moves.start(r.w_down, r.wdown)
        got_cot = moves.start(r.cot_in.at[first * SLOT : (first + GP) * SLOT, :], r.cot)
        got_wq = moves.start(r.wq_in, r.wq)
        r.k[...] = dot(r.mem[...], r.wkv[0:D, :]).astype(BF)
        r.v[...] = dot(r.mem[...], r.wkv[D : 2 * D, :]).astype(BF)
        moves.wait(got_q)

        def length_of(p):
            last = r.mem[rows_at(p * PR + PR - 16, 16), :].astype(F32)
            return last[15:16, :].astype(jnp.int32)

        attend_forward(length_of, r.q, 0, r.k, 0, r.v, 0, r.mix)
        moves.start(r.mix, r.mix_out)
        moves.wait(got_h, got_o)
        unit, scale = norm_of(r.h[...] + dot(r.mix[...], r.wo[...]))
        r.unit1[...] = unit.astype(BF)
        r.sc1[...] = scale
        r.h[...] = unit * r.gains[1:2, :] + r.biases[1:2, :]
        moves.wait(got_up, got_cot)
        for p in range(GP):
            place = lax.broadcasted_iota(jnp.int32, (PR, 1), 0)
            valid = jnp.where(place < r.lengths[first + p], 1.0, 0.0)
            r.valid[p * PR : (p + 1) * PR, :] = valid
            r.ds[p * PR : (p + 1) * PR, :] = r.cot[p * SLOT : p * SLOT + PR, :].astype(F32) * valid
        summed = feed_forward(
            r.wup, r.wdown, r.h, r.hb, r.hid, r.act, lambda: moves.wait(got_down)
        )
        moves.start(r.hb, r.hb_out)
        moves.start(r.act, r.act_out)
        unit, scale = norm_of(summed)
        grad = r.ds[...]
        decoded = (unit * r.gains[2:3, :] + r.biases[2:3, :]) * r.valid[...]
        for p in range(GP):
            r.states[p * SLOT : p * SLOT + PR, :] = decoded[p * PR : (p + 1) * PR, :]
            r.states[p * SLOT + PR : (p + 1) * SLOT, :] = jnp.zeros((SLOT - PR, D), F32)
        moves.start(r.states, r.states_out.at[first * SLOT : (first + GP) * SLOT, :])
        count_norm(r.gb, 2, grad, unit)
        grad_sum = norm_back(grad, unit, scale, r.gains[2:3, :])
        r.bg2[...] = grad_sum.astype(BF)
        r.ds[...] = grad_sum
        moves.start(r.bg2, r.bg2_out)
        grad = feed_back(r.wup, r.wdown, r.ds, r.bg2, r.hid, r.dhid)
        moves.start(r.dhid, r.dhid_out)
        unit = r.unit1[...].astype(F32)
        count_norm(r.gb, 1, grad, unit)
        grad_sum = norm_back(grad, unit, r.sc1[...], r.gains[1:2, :])
        r.bg1[...] = grad_sum.astype(BF)
        r.h[...] = grad_sum
        moves.start(r.bg1, r.bg1_out)
        moves.start(r.gb, r.gb_out)
        r.gm[0:GR, :] = dot_t(r.bg1[...], r.wo[...]).astype(BF)
        attend_backward(length_of, r.q, 0, r.k, 0, r.v, 0, r.gm, r.dq, 0, r.dk, 0, r.dv, 0)
        moves.start(r.dq, r.dq_out)
        moves.start(r.dk, r.dk_out)
        moves.start(r.dv, r.dv_out)
        r.gmem[...] = (
            dot_t(r.dk[...], r.wkv[0:D, :]) + dot_t(r.dv[...], r.wkv[D : 2 * D, :])
        ).astype(BF)
        moves.start(r.gmem, r.gmem_out)
        moves.wait(got_wq)
        r.ds[...] = r.h[...] + dot_t(r.dq[...], r.wq[...])
        moves.start(r.ds, r.dh_out)
        moves.finish()


def self_back_part(r, moves, got, first):
    zero_rows(r.gm, GR)
    zero_rows(r.qkv, GR)
    moves.wait(*got[:-1])
    grad = r.dh[...]
    unit = r.unit0[...].astype(F32)
    count_norm(r.gb, 0, grad, unit)
    grad = norm_back(grad, unit, r.sc0[...], r.gains[0:1, :])
    r.bg[...] = grad.astype(BF)
    r.dh[...] = grad
    moves.start(r.dh, r.ds_out)
    moves.start(r.bg, r.bg_out)
    r.gm[0:GR, :] = dot_t(r.bg[...], r.wout[...]).astype(BF)
    moves.wait(got[-1])
    attend_backward(
        lambda p: r.lengths[first + p],
        r.qkv, 0, r.qkv, 512, r.qkv, 1024, r.gm, r.dqkv, 0, r.dqkv, 512, r.dqkv, 1024,
    )
    moves.start(r.dqkv, r.dqkv_out)


def self_back_loads(r, moves, group):
    return [
        moves.start(getattr(r, f"unit0_{group}"), r.unit0),
        moves.start(getattr(r, f"sc0_{group}"), r.sc0),
        moves.start(r.w_out, r.wout),
        moves.start(getattr(r, f"qkv_{group}"), r.qkv.at[0:GR, :]),
    ]


def feed_back_loads(r, moves, group):
    return [
        moves.start(getattr(r, f"{name}_{group}"), getattr(r, name))
        for name in ("unit2", "sc2", "unit1", "sc1")
    ] + [
        moves.start(r.w_down, r.wdown),
        moves.start(getattr(r, f"hid_{group}"), r.hid),
        moves.start(r.w_up, r.wup),
    ]


def feed_back_part(r, moves, got, bg, dhid, then=lambda: None):
    moves.wait(*got[:4])
    then()
    grad = r.gmem[...].astype(F32)
    unit = r.unit2[...].astype(F32)
    count_norm(r.gb, 2, grad, unit)
    grad = norm_back(grad, unit, r.sc2[...], r.gains[2:3, :])
    unit = r.unit1[...].astype(F32)
    count_norm(r.gb, 1, grad, unit)
    grad = norm_back(grad, unit, r.sc1[...], r.gains[1:2, :])
    bg[...] = grad.astype(BF)
    r.dh[...] = grad
    moves.wait(*got[4:])
    r.dh[...] = feed_back(r.wup, r.wdown, r.dh, bg, r.hid, dhid)


def stacked_loads(r, moves, name, held):
    zero_rows(held, 2 * GR)
    return [
        moves.start(getattr(r, f"{name}_{g}"), held.at[g * GR : (g + 1) * GR, :]) for g in range(2)
    ]


def cross_body(r):
    @pl.when(r.role[0] == 0)
    def _():
        moves = Moves(r.sems)
        got = feed_back_loads(r, moves, 0)
        got_self = self_back_loads(r, moves, 0)
        got_grads = [group_loads(r, moves, "hb", 0, r.hb), group_loads(r, moves, "act", 0, r.act)]
        r.gb[...] = jnp.zeros_like(r.gb)
        zero_rows(r.dhid, GR)
        zero_rows(r.fbg, GR)
        feed_back_part(r, moves, got, r.fbg.at[0:GR, :], r.dhid.at[0:GR, :])
        first_feed_grads(r, moves, got_grads)
        self_back_part(r, moves, got_self, 0)
        moves.start(r.gb, r.gb_out)
        moves.finish()

    @pl.when(r.role[0] == 1)
    def _():
        moves = Moves(r.sems)
        names = ("hb2", "dhid2", "act2", "bg2")
        got = [c for name in names for c in stacked_loads(r, moves, name, getattr(r, "all_" + name))]
        moves.wait(*got)
        feed_weight_grads(r.all_hb2, r.all_dhid2, r.all_act2, r.all_bg2, r.gf)
        moves.start(r.gf, r.gf_out)
        moves.finish()


def first_feed_grads(r, moves, got):
    moves.wait(*got)
    feed_weight_grads(r.hb, r.dhid, r.act, r.fbg, r.gf)
    moves.start(r.gf, r.gf_out)


def group_loads(r, moves, name, group, held):
    zero_rows(held, GR)
    return moves.start(getattr(r, f"{name}_{group}"), held.at[0:GR, :])


def cross_grads_body(r):
    @pl.when(r.role[0] == 1)
    def _():
        moves = Moves(r.sems)
        names = ("mem", "dk", "dv", "fb", "dq", "mixc", "bg1")
        got = {name: stacked_loads(r, moves, name, getattr(r, "all_" + name)) for name in names}
        moves.wait(*got["mem"], *got["dk"], *got["dv"])
        r.gx[0:D, :] = dot_l(r.all_mem[...], r.all_dk[...]).astype(BF)
        r.gx[D : 2 * D, :] = dot_l(r.all_mem[...], r.all_dv[...]).astype(BF)
        start_halves(moves, r.role[1], r.gx, r.keep_out.at[0:D, :], r.send_out.at[0:D, :])
        moves.wait(*got["fb"], *got["dq"], *got["mixc"], *got["bg1"])
        r.gc[0:D, :] = dot_l(r.all_fb[...], r.all_dq[...]).astype(BF)
        r.gc[D : 2 * D, :] = dot_l(r.all_mixc[...], r.all_bg1[...]).astype(BF)
        start_halves(
            moves, r.role[1], r.gc, r.keep_out.at[D : 2 * D, :], r.send_out.at[D : 2 * D, :]
        )
        moves.finish()


def feed_body(r):
    @pl.when(r.role[0] == 0)
    def _():
        moves = Moves(r.sems)
        got = feed_back_loads(r, moves, 1)
        r.gb[...] = jnp.zeros_like(r.gb)
        zero_rows(r.dhid, GR)
        zero_rows(r.fbg, GR)
        got_grads = []

        def load():
            got_grads.append(group_loads(r, moves, "hb", 1, r.hb))
            got_grads.append(group_loads(r, moves, "act", 1, r.act))
            got_grads.append(moves.start(r.gf_in, r.gf))

        feed_back_part(r, moves, got, r.fbg.at[0:GR, :], r.dhid.at[0:GR, :], load)
        moves.start(r.dh, r.dh_out)
        moves.start(r.gb, r.gb_out)
        moves.wait(*got_grads)
        for n in range(4):
            cols = slice(n * D, (n + 1) * D)
            rows = slice(FF + n * D, FF + (n + 1) * D)
            grad = r.gf[cols, :].astype(F32) + dot_l(r.hb[...], r.dhid[:, cols])
            r.gf[cols, :] = grad.astype(BF)
            moves.start(r.gf.at[cols, :], r.gf_out.at[cols, :])
            grad = r.gf[rows, :].astype(F32) + dot_l(r.act[:, cols], r.fbg[...])
            r.gf[rows, :] = grad.astype(BF)
            moves.start(r.gf.at[rows, :], r.gf_out.at[rows, :])
        moves.finish()

    @pl.when(r.role[0] == 1)
    def _():
        moves = Moves(r.sems)
        got_dh = moves.start(r.dh_0, r.dh)
        got = self_back_loads(r, moves, 0)
        r.gb[...] = jnp.zeros_like(r.gb)
        moves.wait(got_dh)
        self_back_part(r, moves, got, 0)
        moves.start(r.gb, r.gb_out)
        moves.finish()


def self_body(r):
    moves = Moves(r.sems)
    got_dh = moves.start(r.dh_1, r.dh)
    got = self_back_loads(r, moves, 1)
    r.gb[...] = jnp.zeros_like(r.gb)
    moves.wait(got_dh)
    self_back_part(r, moves, got, GP)
    moves.start(r.gb, r.gb_out)
    moves.finish()


EXTRA = 64


def self_weights_body(r):
    moves = Moves(r.sems)
    got_x = stacked_loads(r, moves, "xp", r.xp)
    got_qkv = stacked_loads(r, moves, "dqkv", r.dqkv)
    got_mix = stacked_loads(r, moves, "mix", r.mix)
    got_bg = stacked_loads(r, moves, "bg", r.bg)
    got_in = moves.start(r.w_in, r.win)
    got_ds = stacked_loads(r, moves, "ds", r.ds)
    part = 2 * D + EXTRA
    enc = r.gb_cross[...]
    dec = r.gb_dec0[...] + r.gb_dec1[...]
    picked = jnp.where(r.role[0] == 0, enc, dec) + r.gb_feed[...] + r.gb_self[...]
    small = jnp.concatenate(
        [jnp.sum(picked[8 * i : 8 * i + 8, :], axis=0, keepdims=True) for i in range(6)]
        + [jnp.zeros((EXTRA - 6, D), F32)],
        axis=0,
    ).astype(BF)
    r.ga[2 * D : part, :] = small
    r.ga[part + 2 * D : 2 * part, :] = small
    moves.wait(*got_x, *got_qkv)
    r.ga[0:D, :] = dot_l(r.xp[...], r.dqkv[:, 0:D]).astype(BF)
    r.ga[D : 2 * D, :] = dot_l(r.xp[...], r.dqkv[:, D : 2 * D]).astype(BF)
    r.ga[part : part + D, :] = dot_l(r.xp[...], r.dqkv[:, 2 * D : 3 * D]).astype(BF)
    moves.wait(*got_mix, *got_bg)
    r.ga[part + D : part + 2 * D, :] = dot_l(r.mix[...], r.bg[...]).astype(BF)
    start_halves(moves, r.role[1], r.ga, r.keep_out, r.send_out)
    moves.wait(got_in, *got_ds)

    def leave(p):
        at = rows_at(p * PR, PR)
        to = rows_at(p * SLOT, PR)
        r.dx[to, :] = r.ds[at, :] + dot_t(r.dqkv[at, :], r.win[...])
        r.dx[rows_at(p * SLOT + PR, SLOT - PR), :] = jnp.zeros((SLOT - PR, D), F32)

    loop(2 * GP, leave)
    moves.start(r.dx, r.grads_out)
    moves.finish()


def start_halves(moves, core, held, keep, send):
    half = held.shape[0] // 2
    for target, shift in ((keep, 0), (send, 1)):
        start = pl.multiple_of(((core + shift) & 1) * half, 16)
        moves.start(held.at[pl.ds(start, half), :], target)


def place_blocks(core, moves, own, other, held, firsts):
    got = []
    for group, shift in ((own, 0), (other, 1)):
        start = 0
        for ref in group:
            size = ref.shape[0]
            place = pl.multiple_of(((core + shift) & 1) * firsts + start, 16)
            got.append(moves.start(ref, held.at[pl.ds(place, size), :]))
            start += size
    return got


def place_feed_body(r):
    moves = Moves(r.sems)
    got = [
        moves.start(r.gf.at[i * D : (i + 1) * D, :], r.held.at[i * D : (i + 1) * D, :])
        for i in range(8)
    ]
    for i in range(4):
        moves.wait(got[4 + i])
        at = slice(i * D, (i + 1) * D)
        r.down[at, :] = r.held[FF + i * D : FF + (i + 1) * D, :].astype(F32)
        moves.start(r.down.at[at, :], r.down_out.at[at, :])
    moves.wait(*got[:4])
    for i in range(4):
        at = slice(i * 128, (i + 1) * 128)
        for n in range(4):
            r.up[at, n * D : (n + 1) * D] = r.held[
                n * D + i * 128 : n * D + (i + 1) * 128, :
            ].astype(F32)
        moves.start(r.up.at[at, :], r.up_out.at[at, :])
    moves.finish()


def place_rest_body(r):
    moves = Moves(r.sems)
    part = 2 * D + EXTRA
    core = r.role[1]
    got_c = place_blocks(core, moves, [r.c], [r.c_other], r.held_c, D)
    got = place_blocks(core, moves, [r.da, r.db], [r.da_other, r.db_other], r.held, part)
    moves.wait(*got_c)
    r.ca[...] = r.held_c[0:D, :].astype(F32)
    r.cb[...] = r.held_c[D : 2 * D, :].astype(F32)
    moves.start(r.ca, r.ca_out)
    moves.start(r.cb, r.cb_out)
    moves.wait(*got)
    r.wout[...] = r.held[part + D : part + 2 * D, :].astype(F32)
    moves.start(r.wout, r.out_out)
    for n, start in enumerate((0, D, part)):
        r.win[:, n * D : (n + 1) * D] = r.held[start : start + D, :].astype(F32)
    moves.start(r.win, r.in_out)
    small = r.held[2 * D : 2 * D + 16, :].astype(F32)
    r.gains[...] = small[0:3, :]
    r.biases[...] = small[3:6, :]
    moves.start(r.gains, r.gains_out)
    moves.start(r.biases, r.biases_out)
    moves.finish()


ANY = pl.BlockSpec(memory_space=pl.ANY)
WHOLE = pl.BlockSpec(memory_space=pltpu.VMEM)
SCALARS = pl.BlockSpec(memory_space=pltpu.SMEM)


def in_vmem(array):
    return pltpu.with_memory_space_constraint(array, pltpu.VMEM)


class Refs:
    def __init__(self, names, refs):
        for name, ref in zip(names, refs):
            setattr(self, name, ref)


def call(body, name, flops, ins, outs, scratch, copies, aliases=None, whole=()):
    scalars = ("role", "lengths")
    specs = [SCALARS if n in scalars else WHOLE if n in whole else ANY for n in ins]
    names = [*ins, *outs, *scratch, "sems"]
    position = list(ins).index
    results = list(outs).index

    def kernel(*refs):
        body(Refs(names, refs))

    found = pl.pallas_call(
        kernel,
        out_shape=[jax.ShapeDtypeStruct(s, t) for s, t in outs.values()],
        in_specs=specs,
        out_specs=[ANY] * len(outs),
        scratch_shapes=[pltpu.VMEM(s, t) for s, t in scratch.values()]
        + [pltpu.SemaphoreType.DMA((copies,))],
        input_output_aliases={position(i): results(o) for i, o in (aliases or {}).items()},
        compiler_params=pltpu.CompilerParams(vmem_limit_bytes=60 * 1024 * 1024),
        cost_estimate=pl.CostEstimate(
            flops=flops, bytes_accessed=flops // 1000, transcendentals=0
        ),
        name=name,
    )(*ins.values())
    return dict(zip(outs, found))


def swapped(x, mask):
    size = lax.axis_size("dp")
    return lax.ppermute(x, "dp", [(i, i ^ mask) for i in range(size)])


def added(keep, recv):
    return (keep.astype(F32) + recv.astype(F32)).astype(BF)


def lowered(cur, mask, bit):
    half = cur.shape[0] // 2
    recv = swapped(lax.dynamic_slice_in_dim(cur, (1 - bit) * half, half, 0), mask)
    return added(lax.dynamic_slice_in_dim(cur, bit * half, half, 0), recv)


def raised(cur, mask, bit):
    other = swapped(cur, mask)
    return jnp.where(
        bit == 0, jnp.concatenate([cur, other], 0), jnp.concatenate([other, cur], 0)
    )


class Sums:
    def __init__(self):
        size = lax.axis_size("dp")
        place = lax.axis_index("dp")
        self.masks = [1 << i for i in range(1, size.bit_length() - 1)]
        self.bits = {mask: (place >> (mask.bit_length() - 1)) & 1 for mask in self.masks}

    def order(self, turn):
        masks = self.masks
        return masks if turn == 0 else masks[1:] + masks[:1]

    def down(self, parts, turns, first, last):
        for step in range(first, last):
            parts = [
                lowered(p, self.order(t)[step], self.bits[self.order(t)[step]])
                for p, t in zip(parts, turns)
            ]
        return parts

    def up(self, parts, turns):
        for step in reversed(range(len(self.masks))):
            parts = [
                raised(p, self.order(t)[step], self.bits[self.order(t)[step]])
                for p, t in zip(parts, turns)
            ]
        return parts


def on_device(
    embeds, lengths, attn_in, attn_out, cross_a, cross_b, ffn_up, ffn_down,
    norm_gains, norm_biases, cotangent,
):
    x, own = embeds[0], lengths[0]
    win, wout, wa, wb, wup, wdown = (
        attn_in[0], attn_out[0], cross_a[0], cross_b[0], ffn_up[0], ffn_down[0],
    )
    gains, biases = norm_gains[0], norm_biases[0]
    slots = 2 * GP * SLOT
    pipe = lax.axis_index("pipe")
    is_encoder = pipe == 0
    odd = lax.axis_index("dp") & 1
    role = jnp.stack([pipe, odd]).astype(jnp.int32)
    onward, back = [(0, 1)], [(1, 0)]

    def bf(*shape):
        return (shape, BF)

    def f32(*shape):
        return (shape, F32)

    flat, flat_f, wide, one, triple = bf(GR, D), f32(GR, D), bf(GR, FF), f32(GR, 1), bf(GR, 3 * D)
    full, slot, slot_f = f32(slots, D), bf(GP * SLOT, D), f32(GP * SLOT, D)
    square, up_w, down_w, in_w = bf(D, D), bf(D, FF), bf(FF, D), bf(D, 3 * D)
    tall, counts = bf(TALL, D), f32(48, D)
    base = dict(role=role, lengths=own, gains=gains, biases=biases)
    whole = ("gains", "biases")

    mine = lax.ppermute(jnp.where(odd == 0, wa, wb), "pipe", onward)

    fwd, mem_in, states = [], [], None
    for g in range(2):
        ins = dict(base, x_in=x, w_in=win, w_out=wout, w_up=wup, w_down=wdown, w_q=wa)
        if g:
            ins["states_in"] = states
        fwd.append(
            call(
                functools.partial(forward_body, g), f"forward_{g}", 4_000_000_000, ins,
                dict(
                    h_out=flat_f, xp_out=flat, qkv_out=triple, mix_out=flat, unit0_out=flat, sc0_out=one,
                    mem_out=flat, hb_out=flat, hid_out=wide, act_out=wide, unit1_out=flat, sc1_out=one,
                    unit2_out=flat, sc2_out=one, q_out=flat, states_out=full,
                ),
                dict(
                    q=flat, wq=square, x=slot, win=in_w, wout=square, wup=up_w, wdown=down_w, h=flat_f, xp=flat,
                    qkv=bf(TALL, 3 * D), mix=flat, unit0=flat, sc0=one, mem=flat, hb=flat, hid=wide,
                    act=wide, unit1=flat, sc1=one, unit2=flat, sc2=one, state=flat_f, states=slot_f,
                ),
                24, aliases={"states_in": "states_out"} if g else None, whole=whole,
            )
        )
        states = fwd[g]["states_out"]
        memory = fwd[g]["mem_out"]
        if g == 0:
            mine, memory = lax.optimization_barrier((mine, memory))
            other = swapped(mine, 1)
        mem_in.append(lax.ppermute(memory, "pipe", onward))

    dec, gmem_in = [], []
    for g in range(2):
        dec.append(
            call(
                functools.partial(decode_body, g), f"decode_{g}", 8_000_000_000,
                dict(
                    base, h_in=fwd[g]["h_out"], q_in=fwd[g]["q_out"], mem=in_vmem(mem_in[g]), cot_in=cotangent, wq_in=wa, wo_in=wb,
                    mine_in=in_vmem(mine), other_in=in_vmem(other), w_up=wup, w_down=wdown, states_in=states,
                ),
                dict(
                    states_out=full, gmem_out=flat, dh_out=flat_f, dq_out=flat, mix_out=flat,
                    bg1_out=flat, dk_out=flat, dv_out=flat, hb_out=flat, dhid_out=wide, act_out=wide,
                    bg2_out=flat, gb_out=counts,
                ),
                dict(
                    h=flat_f, cot=slot, wq=square, wo=square, wkv=bf(2 * D, D), wup=up_w,
                    wdown=down_w, states=slot_f, gmem=flat, q=tall, k=flat, v=flat, mix=flat,
                    dq=flat, dk=flat, dv=flat, bg1=flat, hb=flat, hid=wide, dhid=wide, act=wide, bg2=flat,
                    unit1=flat, sc1=one, valid=one, ds=flat_f, gm=tall, gb=counts,
                ),
                24, aliases={"states_in": "states_out"}, whole=whole + ("mem", "mine_in", "other_in"),
            )
        )
        states = dec[g]["states_out"]
        gmem_in.append(lax.ppermute(dec[g]["gmem_out"], "pipe", back))

    def of(group, results, **names):
        return {f"{k}_{group}": results[v] for k, v in names.items()}

    enc_names = dict(
        unit2="unit2_out", sc2="sc2_out", unit1="unit1_out", sc1="sc1_out", hid="hid_out",
    )
    self_names = dict(unit0="unit0_out", sc0="sc0_out", qkv="qkv_out")
    back_scratch = dict(
        unit2=flat, sc2=one, unit1=flat, sc1=one, wdown=down_w, hid=wide, wup=up_w, dh=flat_f,
    )
    self_scratch = dict(
        unit0=flat, sc0=one, wout=square, qkv=bf(TALL, 3 * D), bg=flat, gm=tall, dqkv=triple, gb=counts,
    )
    dec_names = dict(
        dk="dk_out", dv="dv_out", dq="dq_out", mixc="mix_out", bg1="bg1_out", hb2="hb_out",
        dhid2="dhid_out", act2="act_out", bg2="bg2_out",
    )
    all_flat, all_wide = bf(ALL, D), bf(ALL, FF)
    cross_names = {k: v for k, v in dec_names.items() if k in ("dk", "dv", "dq", "mixc", "bg1")}
    feed_names = {k: v for k, v in dec_names.items() if k not in cross_names}
    ins = dict(
        base, w_up=wup, w_down=wdown, w_out=wout, gmem=in_vmem(gmem_in[0]),
        hb_0=fwd[0]["hb_out"], act_0=fwd[0]["act_out"],
    )
    ins.update(of(0, fwd[0], **enc_names, **self_names))
    for g in range(2):
        ins.update(of(g, dec[g], **feed_names))
    feed_scratch = dict(
        gf=bf(2 * FF, D), hb=tall, act=bf(TALL, FF), fbg=tall, dhid=bf(TALL, FF),
    )
    feed_outs = dict(gf_out=bf(2 * FF, D))
    cross = call(
        cross_body, "cross_back", 1_000, ins,
        dict(
            ds_out=flat_f, bg_out=flat, dqkv_out=triple, gb_out=counts, **feed_outs,
        ),
        dict(
            **back_scratch, **self_scratch, **feed_scratch,
            all_hb2=all_flat, all_dhid2=all_wide, all_act2=all_wide, all_bg2=all_flat,
        ),
        40, whole=whole + ("gmem",),
    )
    ins = dict(role=role)
    for g in range(2):
        ins.update(of(g, dec[g], **cross_names))
        ins[f"fb_{g}"] = fwd[g]["hb_out"]
        ins[f"mem_{g}"] = mem_in[g]
    ins["dk_1"], gf = lax.optimization_barrier((ins["dk_1"], cross["gf_out"]))
    crossed = call(
        cross_grads_body, "cross_grads", 1_000, ins,
        dict(keep_out=bf(2 * D, D), send_out=bf(2 * D, D)),
        dict(
            **{"all_" + n: all_flat for n in ("mem", "fb", *cross_names)}, gx=bf(2 * D, D), gc=bf(2 * D, D),
        ),
        32,
    )
    crossed_keep, crossed_send, gf = lax.optimization_barrier(
        (crossed["keep_out"], crossed["send_out"], gf)
    )
    crossed_sent = swapped(crossed_send, 1)

    ins = dict(
        base, w_up=wup, w_down=wdown, w_out=wout, gmem=in_vmem(gmem_in[1]), hb_1=fwd[1]["hb_out"],
        act_1=fwd[1]["act_out"], dh_0=dec[0]["dh_out"], dh_in=dec[1]["dh_out"],
        ds_in=cross["ds_out"], bg_in=cross["bg_out"], dqkv_in=cross["dqkv_out"], gf_in=gf,
    )
    ins.update(of(1, fwd[1], **enc_names))
    ins.update(of(0, fwd[0], **self_names))
    feed = call(
        feed_body, "feed_back", 1_000, ins,
        dict(
            dh_out=flat_f, ds_out=flat_f, bg_out=flat, dqkv_out=triple, gb_out=counts, **feed_outs,
        ),
        dict(**back_scratch, **self_scratch, **feed_scratch),
        32,
        aliases={
            name + "_in": name + "_out"
            for name in ("dh", "ds", "bg", "dqkv", "gf")
        },
        whole=whole + ("gmem",),
    )
    gf = lax.psum(feed["gf_out"], "dp")
    crossed_x = added(crossed_keep[:D], crossed_sent[:D])
    crossed_c = added(crossed_keep[D:], crossed_sent[D:])
    sums = Sums()
    depth = len(sums.masks)
    part = 2 * D + EXTRA

    def tail():
        last = call(
            self_body, "self_back", 3_000_000_000,
            dict(base, dh_1=feed["dh_out"], w_out=wout, **of(1, fwd[1], **self_names)),
            dict(ds_out=flat_f, bg_out=flat, dqkv_out=triple, gb_out=counts),
            dict(**self_scratch, dh=flat_f),
            16, whole=whole,
        )
        gx_in = lax.ppermute(crossed_x, "pipe", back)
        gx_in, ds = lax.optimization_barrier((gx_in, last["ds_out"]))
        c_keep = jnp.where(is_encoder, gx_in, crossed_c)
        early = sums.down([c_keep], (0,), 0, 1)
        ins = dict(
            role=role, gb_cross=cross["gb_out"], gb_dec0=dec[0]["gb_out"], gb_dec1=dec[1]["gb_out"],
            gb_feed=feed["gb_out"], gb_self=last["gb_out"], w_in=win, ds_0=feed["ds_out"], ds_1=ds,
            bg_0=feed["bg_out"], bg_1=last["bg_out"], dqkv_0=feed["dqkv_out"], dqkv_1=last["dqkv_out"],
        )
        for g in range(2):
            ins.update(of(g, fwd[g], xp="xp_out", mix="mix_out"))
        found = call(
            self_weights_body, "self_weights", 8_000_000_000, ins,
            dict(grads_out=full, keep_out=bf(part, D), send_out=bf(part, D)),
            dict(
                ds=f32(ALL, D), bg=all_flat, dqkv=bf(ALL, 3 * D), xp=all_flat, mix=all_flat, win=in_w,
                dx=full, ga=bf(2 * part, D),
            ),
            20, whole=("gb_cross", "gb_dec0", "gb_dec1", "gb_feed", "gb_self"),
        )
        a_keep = added(found["keep_out"], swapped(found["send_out"], 1))
        early = sums.down(early, (0,), 1, depth)
        late = sums.down([a_keep[:D], a_keep[D:]], (0, 1), 0, depth)
        parts = sums.up(early + late, (0, 0, 1))
        return found["grads_out"], parts, [swapped(p, 1) for p in parts]

    shapes = jax.eval_shape(tail)
    input_grads, parts, others = lax.cond(
        own[0] >= 0,
        tail,
        lambda: jax.tree.map(lambda leaf: jnp.zeros(leaf.shape, leaf.dtype), shapes),
    )
    placed = call(
        place_rest_body, "place_rest", 1_000_000_000,
        dict(
            role=role, c=parts[0], da=parts[1], db=parts[2],
            c_other=others[0], da_other=others[1], db_other=others[2],
        ),
        dict(
            in_out=f32(D, 3 * D), out_out=f32(D, D), gains_out=f32(3, D), biases_out=f32(3, D),
            ca_out=f32(D, D), cb_out=f32(D, D),
        ),
        dict(
            held=bf(2 * part, D), win=f32(D, 3 * D), wout=f32(D, D), gains=f32(3, D), biases=f32(3, D),
            held_c=bf(2 * D, D), ca=f32(D, D), cb=f32(D, D),
        ),
        16,
    )
    placed |= call(
        place_feed_body, "place_feed", 1_000_000_000,
        dict(gf=gf),
        dict(up_out=f32(D, FF), down_out=f32(FF, D)),
        dict(held=bf(2 * FF, D), up=f32(D, FF), down=f32(FF, D)),
        16,
    )
    outs = (
        states, input_grads, placed["in_out"], placed["out_out"], placed["ca_out"], placed["cb_out"],
        placed["up_out"], placed["down_out"], placed["gains_out"], placed["biases_out"],
    )
    return tuple(out[None] for out in outs)


def solution(mesh):
    cut = P("pipe", "dp", None)
    held = P("pipe", None, None)
    return jax.shard_map(
        on_device,
        mesh=mesh,
        in_specs=(cut, P("pipe", "dp")) + (held,) * 8 + (P("dp", None),),
        out_specs=(cut, cut) + (held,) * 8,
        check_vma=False,
    )
```

```python
import functools

import jax
import jax.numpy as jnp
from jax import lax
from jax.experimental import pallas as pl
from jax.experimental.pallas import tpu as pltpu
from jax.sharding import PartitionSpec as P

HEADS = 8
D = 512
FF = 2048
SLOT = 256
PR = 208
GP = 2
GR = GP * PR
TALL = 512
ALL = 896
NORM_EPSILON = 1e-05
BF = jnp.bfloat16
F32 = jnp.float32
CORE_C = 0.7978845608028654
CUBE_C = 0.044715


def dot(a, b):
    return lax.dot_general(a, b, (((1,), (0,)), ((), ())), preferred_element_type=F32)


def dot_t(a, b):
    return lax.dot_general(a, b, (((1,), (1,)), ((), ())), preferred_element_type=F32)


def dot_l(a, b):
    return lax.dot_general(a, b, (((0,), (0,)), ((), ())), preferred_element_type=F32)


def rows_at(start, size, step=16):
    if isinstance(start, int):
        return pl.ds(start, size)
    return pl.ds(pl.multiple_of(start, step), size)


def loop(n, body):
    def run(i, carry):
        body(i)
        return carry

    lax.fori_loop(0, n, run, 0)


def gelu_and_slope(u):
    square = u * u
    bent = jnp.tanh(u * (CORE_C + CORE_C * CUBE_C * square))
    half = 0.5 + 0.5 * bent
    bend = (1.0 - bent) * (CORE_C + 3.0 * CORE_C * CUBE_C * square)
    return u * half, half * (1.0 + u * bend)


def norm_of(summed):
    center = summed - jnp.mean(summed, axis=-1, keepdims=True)
    spread = jnp.mean(center * center, axis=-1, keepdims=True)
    scale = lax.rsqrt(spread + NORM_EPSILON)
    return center * scale, scale


def norm_back(grad, unit, scale, gain):
    lifted = grad * gain
    first = jnp.mean(lifted, axis=-1, keepdims=True)
    second = jnp.mean(lifted * unit, axis=-1, keepdims=True)
    return scale * (lifted - first - unit * second)


def fold8(values):
    return jnp.sum(values.reshape(-1, 8, values.shape[-1]), axis=0)


class Moves:
    def __init__(self, sems):
        self.sems = sems
        self.used = 0
        self.open = []

    def start(self, source, target):
        copy = pltpu.make_async_copy(source, target, self.sems.at[self.used])
        self.used += 1
        copy.start()
        self.open.append(copy)
        return copy

    def wait(self, *copies):
        for copy in copies:
            copy.wait()
            self.open = [c for c in self.open if c is not copy]

    def finish(self):
        for copy in self.open:
            copy.wait()
        self.open = []


def lane_masks():
    lane = lax.broadcasted_iota(jnp.int32, (1, 128), 1)
    low = jnp.where(lane < 64, 1.0, 0.0).astype(BF)
    high = jnp.where(lane < 64, 0.0, 1.0).astype(BF)
    return low, high


def both_heads(rows, low, high):
    return jnp.concatenate([rows * low, rows * high], axis=0)


def merged_heads(stacked):
    lane = lax.broadcasted_iota(jnp.int32, (PR, 128), 1)
    return jnp.where(lane < 64, stacked[:PR], stacked[SLOT : SLOT + PR])


def probs_of(keys, queries, length):
    raw = dot_t(keys, queries)
    place = lax.broadcasted_iota(jnp.int32, raw.shape, 0)
    raw = jnp.where(place < length, raw, -1e30)
    top = jnp.max(raw, axis=0, keepdims=True)
    terms = jnp.exp(raw - top)
    total = jnp.sum(terms, axis=0, keepdims=True)
    return terms * (1.0 / total)


def attend_forward(length_of, q_ref, q_off, k_ref, k_off, v_ref, v_off, out_ref):
    low, high = lane_masks()
    low_q, high_q = low * 0.125, high * 0.125

    def pair(p):
        length = length_of(p)
        base = rows_at(p * PR, PR)
        wide = rows_at(p * PR, SLOT)
        for hp in range(4):
            at = hp * 128
            queries = both_heads(q_ref[wide, q_off + at : q_off + at + 128], low_q, high_q)
            keys = k_ref[base, k_off + at : k_off + at + 128]
            values = v_ref[base, v_off + at : v_off + at + 128]
            probs = probs_of(keys, queries, length).astype(BF)
            out_ref[base, at : at + 128] = merged_heads(dot_l(probs, values)).astype(BF)

    loop(GP, pair)


def attend_backward(
    length_of, q_ref, q_off, k_ref, k_off, v_ref, v_off, g_ref,
    dq_ref, dq_off, dk_ref, dk_off, dv_ref, dv_off,
):
    low, high = lane_masks()
    low_q, high_q = low * 0.125, high * 0.125

    def pair(p):
        length = length_of(p)
        base = rows_at(p * PR, PR)
        wide = rows_at(p * PR, SLOT)
        row = lax.broadcasted_iota(jnp.int32, (SLOT, 128), 0)
        for hp in range(4):
            at = hp * 128
            queries = both_heads(q_ref[wide, q_off + at : q_off + at + 128], low_q, high_q)
            keys = k_ref[base, k_off + at : k_off + at + 128]
            values = v_ref[base, v_off + at : v_off + at + 128]
            grads = jnp.where(row < PR, g_ref[wide, at : at + 128].astype(F32), 0.0).astype(BF)
            grads = both_heads(grads, low, high)
            probs = probs_of(keys, queries, length)
            grad_probs = dot_t(values, grads)
            mean = jnp.sum(probs * grad_probs, axis=0, keepdims=True)
            grad_raw = (probs * (grad_probs - mean)).astype(BF)
            dv_ref[base, dv_off + at : dv_off + at + 128] = dot(probs.astype(BF), grads).astype(BF)
            dk_ref[base, dk_off + at : dk_off + at + 128] = dot(grad_raw, queries).astype(BF)
            dq = merged_heads(dot_l(grad_raw, keys)) * 0.125
            dq_ref[base, dq_off + at : dq_off + at + 128] = dq.astype(BF)

    loop(GP, pair)


def zero_rows(ref, start):
    ref[start:, :] = jnp.zeros((ref.shape[0] - start, ref.shape[1]), ref.dtype)


def feed_forward(w_up, w_down, h_ref, hb_ref, slope_ref, act_ref, got_down, leave):
    hb_ref[...] = h_ref[...].astype(BF)

    for n in range(FF // 512):
        cols = slice(n * 512, (n + 1) * 512)
        active, slope = gelu_and_slope(dot(hb_ref[...], w_up[:, cols]))
        slope_ref[:, cols] = slope.astype(BF)
        act_ref[:, cols] = active.astype(BF)
        leave(cols)

    got_down()
    return h_ref[...] + dot(act_ref[...], w_down[...])


def feed_back(w_up, w_down, ds_ref, bg_ref, slope_ref, dhid_ref):
    for n in range(FF // 512):
        cols = slice(n * 512, (n + 1) * 512)
        grad_act = dot_t(bg_ref[...], w_down[cols, :])
        dhid_ref[:, cols] = (grad_act * slope_ref[:, cols].astype(F32)).astype(BF)

    return ds_ref[...] + dot_t(dhid_ref[...], w_up[...])


def feed_weight_grads(hb_ref, dhid_ref, act_ref, bg_ref, out_ref):
    def column(n):
        cols = rows_at(n * 512, 512, 512)
        out_ref[rows_at(n * 512, 512, 512), :] = dot_l(hb_ref[...], dhid_ref[:, cols]).astype(BF)
        out_ref[rows_at(FF + n * 512, 512, 512), :] = dot_l(act_ref[:, cols], bg_ref[...]).astype(BF)

    loop(FF // 512, column)


def count_norm(gb, index, grad, unit):
    gb[8 * index : 8 * index + 8, :] += fold8(grad * unit)
    gb[24 + 8 * index : 32 + 8 * index, :] += fold8(grad)


def forward_body(group, r):
    moves = Moves(r.sems)
    is_encoder = r.role[0] == 0
    first = group * GP
    got_x = moves.start(r.x_in.at[first * SLOT : (first + GP) * SLOT, :], r.x)
    got_in = moves.start(r.w_in, r.win)
    zero_rows(r.qkv, GR)
    moves.wait(got_x)
    for p in range(GP):
        r.xp[p * PR : (p + 1) * PR, :] = r.x[p * SLOT : p * SLOT + PR, :]
    moves.wait(got_in)
    got_out = moves.start(r.w_out, r.wout)
    got_q = moves.start(r.w_q, r.wq)
    got_up = moves.start(r.w_up, r.wup)
    got_down = moves.start(r.w_down, r.wdown)

    def column(n):
        cols = rows_at(n * 512, 512, 512)
        r.qkv[0:GR, cols] = dot(r.xp[...], r.win[:, cols]).astype(BF)

    loop(3, column)
    moves.start(r.xp, r.xp_out)
    moves.start(r.qkv.at[0:GR, :], r.qkv_out)
    attend_forward(lambda p: r.lengths[first + p], r.qkv, 0, r.qkv, 512, r.qkv, 1024, r.mix)
    moves.start(r.mix, r.mix_out)
    moves.wait(got_out)
    unit, scale = norm_of(r.xp[...].astype(F32) + dot(r.mix[...], r.wout[...]))
    r.unit0[...] = unit.astype(BF)
    r.sc0[...] = scale
    r.h[...] = unit * r.gains[0:1, :] + r.biases[0:1, :]
    moves.start(r.unit0, r.unit0_out)
    moves.start(r.sc0, r.sc0_out)
    moves.start(r.h, r.h_out)
    moves.wait(got_up, got_down, got_q)
    first_used = moves.used

    @pl.when(jnp.logical_not(is_encoder))
    def _():
        own = Moves(r.sems)
        own.used = first_used
        r.hb[...] = r.h[...].astype(BF)
        r.q[...] = dot(r.hb[...], r.wq[...]).astype(BF)
        own.start(r.hb, r.hb_out)
        own.start(r.q, r.q_out)
        own.finish()

    @pl.when(is_encoder)
    def _():
        own = Moves(r.sems)
        own.used = first_used

        def leave(cols):
            own.start(r.hid.at[:, cols], r.hid_out.at[:, cols])
            own.start(r.act.at[:, cols], r.act_out.at[:, cols])

        summed = feed_forward(r.wup, r.wdown, r.h, r.hb, r.hid, r.act, lambda: None, leave)
        own.start(r.hb, r.hb_out)
        unit, scale = norm_of(summed)
        r.unit1[...] = unit.astype(BF)
        r.sc1[...] = scale
        unit, scale = norm_of(unit * r.gains[1:2, :] + r.biases[1:2, :])
        r.unit2[...] = unit.astype(BF)
        r.sc2[...] = scale
        memory = unit * r.gains[2:3, :] + r.biases[2:3, :]
        r.mem[...] = memory.astype(BF)
        r.state[...] = memory
        row = lax.broadcasted_iota(jnp.int32, (16, D), 0)
        place = lax.broadcasted_iota(jnp.int32, (PR, D), 0)
        for p in range(GP):
            length = r.lengths[first + p]
            last = r.mem[(p + 1) * PR - 16 : (p + 1) * PR, :].astype(F32)
            r.mem[(p + 1) * PR - 16 : (p + 1) * PR, :] = jnp.where(
                row < 8, last, length.astype(F32)
            ).astype(BF)
            r.states[p * SLOT : p * SLOT + PR, :] = jnp.where(
                place < length, r.state[p * PR : (p + 1) * PR, :], 0.0
            )
            r.states[p * SLOT + PR : (p + 1) * SLOT, :] = jnp.zeros((SLOT - PR, D), F32)
        own.start(r.mem, r.mem_out)
        for name in ("unit1", "sc1", "unit2", "sc2"):
            own.start(getattr(r, name), getattr(r, name + "_out"))
        own.start(r.states, r.states_out.at[first * SLOT : (first + GP) * SLOT, :])
        own.finish()

    moves.finish()


def decode_body(group, r):
    first = group * GP

    @pl.when(r.role[0] == 1)
    def _():
        moves = Moves(r.sems)
        core = r.role[1]
        got_mine = moves.start(r.mine_in, r.wkv.at[pl.ds(pl.multiple_of(core * D, D), D), :])
        got_other = moves.start(r.other_in, r.wkv.at[pl.ds(pl.multiple_of((1 - core) * D, D), D), :])
        got_q = moves.start(r.q_in, r.q.at[0:GR, :])
        zero_rows(r.q, GR)
        zero_rows(r.gm, GR)
        r.gb[...] = jnp.zeros_like(r.gb)
        moves.wait(got_mine, got_other)
        got_h = moves.start(r.h_in, r.h)
        got_o = moves.start(r.wo_in, r.wo)
        got_up = moves.start(r.w_up, r.wup)
        got_down = moves.start(r.w_down, r.wdown)
        got_cot = moves.start(r.cot_in.at[first * SLOT : (first + GP) * SLOT, :], r.cot)
        r.k[...] = dot(r.mem[...], r.wkv[0:D, :]).astype(BF)
        r.v[...] = dot(r.mem[...], r.wkv[D : 2 * D, :]).astype(BF)
        moves.wait(got_q)

        def length_of(p):
            last = r.mem[rows_at(p * PR + PR - 16, 16), :].astype(F32)
            return last[15:16, :].astype(jnp.int32)

        attend_forward(length_of, r.q, 0, r.k, 0, r.v, 0, r.mix)
        moves.start(r.mix, r.mix_out)
        moves.wait(got_h, got_o)
        unit, scale = norm_of(r.h[...] + dot(r.mix[...], r.wo[...]))
        r.unit1[...] = unit.astype(BF)
        r.sc1[...] = scale
        r.h[...] = unit * r.gains[1:2, :] + r.biases[1:2, :]
        moves.wait(got_up, got_cot)
        for p in range(GP):
            place = lax.broadcasted_iota(jnp.int32, (PR, 1), 0)
            valid = jnp.where(place < r.lengths[first + p], 1.0, 0.0)
            r.valid[p * PR : (p + 1) * PR, :] = valid
            r.ds[p * PR : (p + 1) * PR, :] = r.cot[p * SLOT : p * SLOT + PR, :].astype(F32) * valid
        summed = feed_forward(
            r.wup, r.wdown, r.h, r.hb, r.hid, r.act, lambda: moves.wait(got_down),
            lambda cols: moves.start(r.act.at[:, cols], r.act_out.at[:, cols]),
        )
        moves.start(r.hb, r.hb_out)
        unit, scale = norm_of(summed)
        grad = r.ds[...]
        decoded = (unit * r.gains[2:3, :] + r.biases[2:3, :]) * r.valid[...]
        for p in range(GP):
            r.states[p * SLOT : p * SLOT + PR, :] = decoded[p * PR : (p + 1) * PR, :]
            r.states[p * SLOT + PR : (p + 1) * SLOT, :] = jnp.zeros((SLOT - PR, D), F32)
        moves.start(r.states, r.states_out.at[first * SLOT : (first + GP) * SLOT, :])
        count_norm(r.gb, 2, grad, unit)
        grad_sum = norm_back(grad, unit, scale, r.gains[2:3, :])
        r.bg2[...] = grad_sum.astype(BF)
        r.ds[...] = grad_sum
        moves.start(r.bg2, r.bg2_out)
        grad = feed_back(r.wup, r.wdown, r.ds, r.bg2, r.hid, r.dhid)
        moves.start(r.dhid, r.dhid_out)
        unit = r.unit1[...].astype(F32)
        count_norm(r.gb, 1, grad, unit)
        grad_sum = norm_back(grad, unit, r.sc1[...], r.gains[1:2, :])
        r.bg1[...] = grad_sum.astype(BF)
        r.h[...] = grad_sum
        moves.start(r.h, r.dh_out)
        moves.start(r.bg1, r.bg1_out)
        moves.start(r.gb, r.gb_out)
        r.gm[0:GR, :] = dot_t(r.bg1[...], r.wo[...]).astype(BF)
        attend_backward(length_of, r.q, 0, r.k, 0, r.v, 0, r.gm, r.dq, 0, r.dk, 0, r.dv, 0)
        moves.start(r.dq, r.dq_out)
        moves.start(r.dk, r.dk_out)
        moves.start(r.dv, r.dv_out)
        r.gmem[...] = (
            dot_t(r.dk[...], r.wkv[0:D, :]) + dot_t(r.dv[...], r.wkv[D : 2 * D, :])
        ).astype(BF)
        moves.start(r.gmem, r.gmem_out)
        moves.finish()


def self_back_part(r, moves, got, first, outs):
    zero_rows(r.gm, GR)
    zero_rows(r.qkv, GR)
    moves.wait(*got[:-1])
    grad = r.dh[...]
    unit = r.unit0[...].astype(F32)
    count_norm(r.gb, 0, grad, unit)
    grad = norm_back(grad, unit, r.sc0[...], r.gains[0:1, :])
    r.bg[...] = grad.astype(BF)
    r.dh[...] = grad
    moves.start(r.dh, outs[0])
    moves.start(r.bg, outs[1])
    r.gm[0:GR, :] = dot_t(r.bg[...], r.wout[...]).astype(BF)
    moves.wait(got[-1])
    attend_backward(
        lambda p: r.lengths[first + p],
        r.qkv, 0, r.qkv, 512, r.qkv, 1024, r.gm, r.dqkv, 0, r.dqkv, 512, r.dqkv, 1024,
    )
    moves.start(r.dqkv, outs[2])


def self_back_loads(r, moves, group):
    return [
        moves.start(getattr(r, f"unit0_{group}"), r.unit0),
        moves.start(getattr(r, f"sc0_{group}"), r.sc0),
        moves.start(r.w_out, r.wout),
        moves.start(getattr(r, f"qkv_{group}"), r.qkv.at[0:GR, :]),
    ]


def feed_back_loads(r, moves, group):
    return [
        moves.start(getattr(r, f"{name}_{group}"), getattr(r, name))
        for name in ("unit2", "sc2", "unit1", "sc1")
    ] + [
        moves.start(r.w_down, r.wdown),
        moves.start(getattr(r, f"hid_{group}"), r.hid),
        moves.start(r.w_up, r.wup),
    ]


def feed_back_part(r, moves, got, bg, dhid, then=lambda: None):
    moves.wait(*got[:4])
    then()
    grad = r.gmem[...].astype(F32)
    unit = r.unit2[...].astype(F32)
    count_norm(r.gb, 2, grad, unit)
    grad = norm_back(grad, unit, r.sc2[...], r.gains[2:3, :])
    unit = r.unit1[...].astype(F32)
    count_norm(r.gb, 1, grad, unit)
    grad = norm_back(grad, unit, r.sc1[...], r.gains[1:2, :])
    bg[...] = grad.astype(BF)
    r.dh[...] = grad
    moves.wait(*got[4:])
    r.dh[...] = feed_back(r.wup, r.wdown, r.dh, bg, r.hid, dhid)


def stacked_loads(r, moves, name, held):
    zero_rows(held, 2 * GR)
    return [
        moves.start(getattr(r, f"{name}_{g}"), held.at[g * GR : (g + 1) * GR, :]) for g in range(2)
    ]


def cross_body(r):
    @pl.when(r.role[0] == 0)
    def _():
        moves = Moves(r.sems)
        got = feed_back_loads(r, moves, 0)
        got_self = self_back_loads(r, moves, 0)
        got_grads = [group_loads(r, moves, "hb", 0, r.hb), group_loads(r, moves, "act", 0, r.act)]
        r.gb[...] = jnp.zeros_like(r.gb)
        zero_rows(r.dhid, GR)
        zero_rows(r.fbg, GR)
        feed_back_part(r, moves, got, r.fbg.at[0:GR, :], r.dhid.at[0:GR, :])
        first_feed_grads(r, moves, got_grads)
        self_back_part(r, moves, got_self, 0, (r.ds_out, r.bg_out, r.dqkv_out))
        moves.start(r.gb, r.gb_out)
        moves.finish()

    @pl.when(r.role[0] == 1)
    def _():
        moves = Moves(r.sems)
        names = ("hb2", "dhid2", "act2", "bg2")
        got = [c for name in names for c in stacked_loads(r, moves, name, getattr(r, "all_" + name))]
        moves.wait(*got)
        feed_weight_grads(r.all_hb2, r.all_dhid2, r.all_act2, r.all_bg2, r.gf)
        moves.start(r.gf, r.gf_out)
        moves.finish()


def first_feed_grads(r, moves, got):
    moves.wait(*got)
    feed_weight_grads(r.hb, r.dhid, r.act, r.fbg, r.gf)
    moves.start(r.gf, r.gf_out)


def group_loads(r, moves, name, group, held):
    zero_rows(held, GR)
    return moves.start(getattr(r, f"{name}_{group}"), held.at[0:GR, :])


def cross_grads_body(r):
    @pl.when(r.role[0] == 1)
    def _():
        moves = Moves(r.sems)
        names = ("mem", "dk", "dv", "fb", "dq", "mixc", "bg1")
        got = {name: stacked_loads(r, moves, name, getattr(r, "all_" + name)) for name in names}
        moves.wait(*got["mem"], *got["dk"], *got["dv"])
        r.gx[0:D, :] = dot_l(r.all_mem[...], r.all_dk[...]).astype(BF)
        r.gx[D : 2 * D, :] = dot_l(r.all_mem[...], r.all_dv[...]).astype(BF)
        start_halves(moves, r.role[1], r.gx, r.keep_out.at[0:D, :], r.send_out.at[0:D, :])
        moves.wait(*got["fb"], *got["dq"], *got["mixc"], *got["bg1"])
        r.gc[0:D, :] = dot_l(r.all_fb[...], r.all_dq[...]).astype(BF)
        r.gc[D : 2 * D, :] = dot_l(r.all_mixc[...], r.all_bg1[...]).astype(BF)
        start_halves(
            moves, r.role[1], r.gc, r.keep_out.at[D : 2 * D, :], r.send_out.at[D : 2 * D, :]
        )
        moves.finish()


def feed_body(r):
    @pl.when(r.role[0] == 0)
    def _():
        moves = Moves(r.sems)
        got = feed_back_loads(r, moves, 1)
        r.gb[...] = jnp.zeros_like(r.gb)
        zero_rows(r.dhid, GR)
        zero_rows(r.fbg, GR)
        got_grads = []

        def load():
            got_grads.append(group_loads(r, moves, "hb", 1, r.hb))
            got_grads.append(group_loads(r, moves, "act", 1, r.act))
            got_grads.append(moves.start(r.gf_in, r.gf))

        feed_back_part(r, moves, got, r.fbg.at[0:GR, :], r.dhid.at[0:GR, :], load)
        moves.start(r.dh, r.dh_out)
        moves.start(r.gb, r.gb_out)
        moves.wait(*got_grads)
        for n in range(4):
            cols = slice(n * D, (n + 1) * D)
            rows = slice(FF + n * D, FF + (n + 1) * D)
            grad = r.gf[cols, :].astype(F32) + dot_l(r.hb[...], r.dhid[:, cols])
            r.gf[cols, :] = grad.astype(BF)
            moves.start(r.gf.at[cols, :], r.gf_out.at[cols, :])
            grad = r.gf[rows, :].astype(F32) + dot_l(r.act[:, cols], r.fbg[...])
            r.gf[rows, :] = grad.astype(BF)
            moves.start(r.gf.at[rows, :], r.gf_out.at[rows, :])
        moves.finish()


def with_queries(r, moves, group):
    got = [moves.start(getattr(r, f"dq_{group}"), r.dq), moves.start(r.w_q, r.wq)]
    moves.wait(*got)
    r.dh[...] += dot_t(r.dq[...], r.wq[...])


def self_body(r):
    r.gb[...] = jnp.zeros_like(r.gb)

    @pl.when(r.role[0] == 1)
    def _():
        own = Moves(r.sems)
        own.used = 20
        got_dh = own.start(r.dh_0, r.dh)
        got = self_back_loads(r, own, 0)
        own.wait(got_dh)
        with_queries(r, own, 0)
        self_back_part(r, own, got, 0, (r.ds0_out, r.bg0_out, r.dqkv0_out))
        own.finish()

    moves = Moves(r.sems)
    got_dh = moves.start(r.dh_1, r.dh)
    got = self_back_loads(r, moves, 1)
    moves.wait(got_dh)

    @pl.when(r.role[0] == 1)
    def _():
        own = Moves(r.sems)
        own.used = 40
        with_queries(r, own, 1)

    self_back_part(r, moves, got, GP, (r.ds_out, r.bg_out, r.dqkv_out))
    moves.start(r.gb, r.gb_out)
    moves.finish()


EXTRA = 64


def chosen_loads(r, moves, name, held):
    zero_rows(held, 2 * GR)
    target = held.at[0:GR, :]
    sem = moves.sems.at[moves.used]
    moves.used += 1
    ours, theirs = (
        pltpu.make_async_copy(getattr(r, f"{name}{which}"), target, sem) for which in ("_enc", "_dec")
    )

    @pl.when(r.role[0] == 0)
    def _():
        ours.start()

    @pl.when(r.role[0] == 1)
    def _():
        theirs.start()

    moves.open.append(ours)
    return [ours, moves.start(getattr(r, f"{name}_1"), held.at[GR : 2 * GR, :])]


def self_weights_body(r):
    moves = Moves(r.sems)
    got_x = stacked_loads(r, moves, "xp", r.xp)
    got_qkv = chosen_loads(r, moves, "dqkv", r.dqkv)
    got_mix = stacked_loads(r, moves, "mix", r.mix)
    got_bg = chosen_loads(r, moves, "bg", r.bg)
    got_in = moves.start(r.w_in, r.win)
    got_ds = chosen_loads(r, moves, "ds", r.ds)
    part = 2 * D + EXTRA
    enc = r.gb_cross[...] + r.gb_feed[...]
    dec = r.gb_dec0[...] + r.gb_dec1[...]
    picked = jnp.where(r.role[0] == 0, enc, dec) + r.gb_self[...]
    small = jnp.concatenate(
        [jnp.sum(picked[8 * i : 8 * i + 8, :], axis=0, keepdims=True) for i in range(6)]
        + [jnp.zeros((EXTRA - 6, D), F32)],
        axis=0,
    ).astype(BF)
    r.ga[2 * D : part, :] = small
    r.ga[part + 2 * D : 2 * part, :] = small
    moves.wait(*got_x, *got_qkv)
    r.ga[0:D, :] = dot_l(r.xp[...], r.dqkv[:, 0:D]).astype(BF)
    r.ga[D : 2 * D, :] = dot_l(r.xp[...], r.dqkv[:, D : 2 * D]).astype(BF)
    r.ga[part : part + D, :] = dot_l(r.xp[...], r.dqkv[:, 2 * D : 3 * D]).astype(BF)
    moves.wait(*got_mix, *got_bg)
    r.ga[part + D : part + 2 * D, :] = dot_l(r.mix[...], r.bg[...]).astype(BF)
    start_halves(moves, r.role[1], r.ga, r.keep_out, r.send_out)
    moves.wait(got_in, *got_ds)

    def leave(p):
        at = rows_at(p * PR, PR)
        to = rows_at(p * SLOT, PR)
        r.dx[to, :] = r.ds[at, :] + dot_t(r.dqkv[at, :], r.win[...])
        r.dx[rows_at(p * SLOT + PR, SLOT - PR), :] = jnp.zeros((SLOT - PR, D), F32)

    loop(2 * GP, leave)
    moves.start(r.dx, r.grads_out)
    moves.finish()


def start_halves(moves, core, held, keep, send):
    half = held.shape[0] // 2
    for target, shift in ((keep, 0), (send, 1)):
        start = pl.multiple_of(((core + shift) & 1) * half, 16)
        moves.start(held.at[pl.ds(start, half), :], target)


def place_blocks(core, moves, own, other, held, firsts):
    got = []
    for group, shift in ((own, 0), (other, 1)):
        start = 0
        for ref in group:
            size = ref.shape[0]
            place = pl.multiple_of(((core + shift) & 1) * firsts + start, 16)
            got.append(moves.start(ref, held.at[pl.ds(place, size), :]))
            start += size
    return got


def place_feed_body(r):
    moves = Moves(r.sems)
    got = [
        moves.start(r.gf.at[i * D : (i + 1) * D, :], r.held.at[i * D : (i + 1) * D, :])
        for i in range(8)
    ]
    for i in range(4):
        moves.wait(got[4 + i])
        at = slice(i * D, (i + 1) * D)
        r.down[at, :] = r.held[FF + i * D : FF + (i + 1) * D, :].astype(F32)
        moves.start(r.down.at[at, :], r.down_out.at[at, :])
    moves.wait(*got[:4])
    for i in range(4):
        at = slice(i * 128, (i + 1) * 128)
        for n in range(4):
            r.up[at, n * D : (n + 1) * D] = r.held[
                n * D + i * 128 : n * D + (i + 1) * 128, :
            ].astype(F32)
        moves.start(r.up.at[at, :], r.up_out.at[at, :])
    moves.finish()


def place_rest_body(r):
    moves = Moves(r.sems)
    part = 2 * D + EXTRA
    core = r.role[1]
    got_c = place_blocks(core, moves, [r.c], [r.c_other], r.held_c, D)
    got = place_blocks(core, moves, [r.da, r.db], [r.da_other, r.db_other], r.held, part)
    moves.wait(*got_c)
    r.ca[...] = r.held_c[0:D, :].astype(F32)
    r.cb[...] = r.held_c[D : 2 * D, :].astype(F32)
    moves.start(r.ca, r.ca_out)
    moves.start(r.cb, r.cb_out)
    moves.wait(*got)
    r.wout[...] = r.held[part + D : part + 2 * D, :].astype(F32)
    moves.start(r.wout, r.out_out)
    for n, start in enumerate((0, D, part)):
        r.win[:, n * D : (n + 1) * D] = r.held[start : start + D, :].astype(F32)
    moves.start(r.win, r.in_out)
    small = r.held[2 * D : 2 * D + 16, :].astype(F32)
    r.gains[...] = small[0:3, :]
    r.biases[...] = small[3:6, :]
    moves.start(r.gains, r.gains_out)
    moves.start(r.biases, r.biases_out)
    moves.finish()


ANY = pl.BlockSpec(memory_space=pl.ANY)
WHOLE = pl.BlockSpec(memory_space=pltpu.VMEM)
SCALARS = pl.BlockSpec(memory_space=pltpu.SMEM)


def in_vmem(array):
    return pltpu.with_memory_space_constraint(array, pltpu.VMEM)


class Refs:
    def __init__(self, names, refs):
        for name, ref in zip(names, refs):
            setattr(self, name, ref)


def call(body, name, flops, ins, outs, scratch, copies, aliases=None, whole=()):
    scalars = ("role", "lengths")
    specs = [SCALARS if n in scalars else WHOLE if n in whole else ANY for n in ins]
    names = [*ins, *outs, *scratch, "sems"]
    position = list(ins).index
    results = list(outs).index

    def kernel(*refs):
        body(Refs(names, refs))

    found = pl.pallas_call(
        kernel,
        out_shape=[jax.ShapeDtypeStruct(s, t) for s, t in outs.values()],
        in_specs=specs,
        out_specs=[ANY] * len(outs),
        scratch_shapes=[pltpu.VMEM(s, t) for s, t in scratch.values()]
        + [pltpu.SemaphoreType.DMA((copies,))],
        input_output_aliases={position(i): results(o) for i, o in (aliases or {}).items()},
        compiler_params=pltpu.CompilerParams(vmem_limit_bytes=60 * 1024 * 1024),
        cost_estimate=pl.CostEstimate(
            flops=flops, bytes_accessed=flops // 1000, transcendentals=0
        ),
        name=name,
    )(*ins.values())
    return dict(zip(outs, found))


def swapped(x, mask):
    size = lax.axis_size("dp")
    return lax.ppermute(x, "dp", [(i, i ^ mask) for i in range(size)])


def added(keep, recv):
    return (keep.astype(F32) + recv.astype(F32)).astype(BF)


def lowered(cur, mask, bit):
    half = cur.shape[0] // 2
    recv = swapped(lax.dynamic_slice_in_dim(cur, (1 - bit) * half, half, 0), mask)
    return added(lax.dynamic_slice_in_dim(cur, bit * half, half, 0), recv)


def raised(cur, mask, bit):
    other = swapped(cur, mask)
    return jnp.where(
        bit == 0, jnp.concatenate([cur, other], 0), jnp.concatenate([other, cur], 0)
    )


class Sums:
    def __init__(self):
        size = lax.axis_size("dp")
        place = lax.axis_index("dp")
        self.masks = [1 << i for i in range(1, size.bit_length() - 1)]
        self.bits = {mask: (place >> (mask.bit_length() - 1)) & 1 for mask in self.masks}

    def order(self, turn):
        masks = self.masks
        return masks if turn == 0 else masks[1:] + masks[:1]

    def down(self, parts, turns, first, last):
        for step in range(first, last):
            parts = [
                lowered(p, self.order(t)[step], self.bits[self.order(t)[step]])
                for p, t in zip(parts, turns)
            ]
        return parts

    def up(self, parts, turns):
        for step in reversed(range(len(self.masks))):
            parts = [
                raised(p, self.order(t)[step], self.bits[self.order(t)[step]])
                for p, t in zip(parts, turns)
            ]
        return parts


def on_device(
    embeds, lengths, attn_in, attn_out, cross_a, cross_b, ffn_up, ffn_down,
    norm_gains, norm_biases, cotangent,
):
    x, own = embeds[0], lengths[0]
    win, wout, wa, wb, wup, wdown = (
        attn_in[0], attn_out[0], cross_a[0], cross_b[0], ffn_up[0], ffn_down[0],
    )
    gains, biases = norm_gains[0], norm_biases[0]
    slots = 2 * GP * SLOT
    pipe = lax.axis_index("pipe")
    is_encoder = pipe == 0
    odd = lax.axis_index("dp") & 1
    role = jnp.stack([pipe, odd]).astype(jnp.int32)
    onward, back = [(0, 1)], [(1, 0)]

    def bf(*shape):
        return (shape, BF)

    def f32(*shape):
        return (shape, F32)

    flat, flat_f, wide, one, triple = bf(GR, D), f32(GR, D), bf(GR, FF), f32(GR, 1), bf(GR, 3 * D)
    full, slot, slot_f = f32(slots, D), bf(GP * SLOT, D), f32(GP * SLOT, D)
    square, up_w, down_w, in_w = bf(D, D), bf(D, FF), bf(FF, D), bf(D, 3 * D)
    tall, counts = bf(TALL, D), f32(48, D)
    base = dict(role=role, lengths=own, gains=gains, biases=biases)
    whole = ("gains", "biases")

    mine = lax.ppermute(jnp.where(odd == 0, wa, wb), "pipe", onward)

    fwd, mem_in, states = [], [], None
    for g in range(2):
        ins = dict(base, x_in=x, w_in=win, w_out=wout, w_up=wup, w_down=wdown, w_q=wa)
        if g:
            ins["states_in"] = states
        fwd.append(
            call(
                functools.partial(forward_body, g), f"forward_{g}", 4_000_000_000, ins,
                dict(
                    h_out=flat_f, xp_out=flat, qkv_out=triple, mix_out=flat, unit0_out=flat, sc0_out=one,
                    mem_out=flat, hb_out=flat, hid_out=wide, act_out=wide, unit1_out=flat, sc1_out=one,
                    unit2_out=flat, sc2_out=one, q_out=flat, states_out=full,
                ),
                dict(
                    q=flat, wq=square, x=slot, win=in_w, wout=square, wup=up_w, wdown=down_w, h=flat_f, xp=flat,
                    qkv=bf(TALL, 3 * D), mix=flat, unit0=flat, sc0=one, mem=flat, hb=flat, hid=wide,
                    act=wide, unit1=flat, sc1=one, unit2=flat, sc2=one, state=flat_f, states=slot_f,
                ),
                36, aliases={"states_in": "states_out"} if g else None, whole=whole,
            )
        )
        states = fwd[g]["states_out"]
        memory = fwd[g]["mem_out"]
        if g == 0:
            mine, memory = lax.optimization_barrier((mine, memory))
            other = swapped(mine, 1)
        mem_in.append(lax.ppermute(memory, "pipe", onward))

    dec, gmem_in = [], []
    for g in range(2):
        dec.append(
            call(
                functools.partial(decode_body, g), f"decode_{g}", 8_000_000_000,
                dict(
                    base, h_in=fwd[g]["h_out"], q_in=fwd[g]["q_out"], mem=in_vmem(mem_in[g]), cot_in=cotangent, wo_in=wb,
                    mine_in=in_vmem(mine), other_in=in_vmem(other), w_up=wup, w_down=wdown, states_in=states,
                ),
                dict(
                    states_out=full, gmem_out=flat, dh_out=flat_f, dq_out=flat, mix_out=flat,
                    bg1_out=flat, dk_out=flat, dv_out=flat, hb_out=flat, dhid_out=wide, act_out=wide,
                    bg2_out=flat, gb_out=counts,
                ),
                dict(
                    h=flat_f, cot=slot, wo=square, wkv=bf(2 * D, D), wup=up_w,
                    wdown=down_w, states=slot_f, gmem=flat, q=tall, k=flat, v=flat, mix=flat,
                    dq=flat, dk=flat, dv=flat, bg1=flat, hb=flat, hid=wide, dhid=wide, act=wide, bg2=flat,
                    unit1=flat, sc1=one, valid=one, ds=flat_f, gm=tall, gb=counts,
                ),
                36, aliases={"states_in": "states_out"}, whole=whole + ("mem", "mine_in", "other_in"),
            )
        )
        states = dec[g]["states_out"]
        gmem_in.append(lax.ppermute(dec[g]["gmem_out"], "pipe", back))

    def of(group, results, **names):
        return {f"{k}_{group}": results[v] for k, v in names.items()}

    enc_names = dict(
        unit2="unit2_out", sc2="sc2_out", unit1="unit1_out", sc1="sc1_out", hid="hid_out",
    )
    self_names = dict(unit0="unit0_out", sc0="sc0_out", qkv="qkv_out")
    back_scratch = dict(
        unit2=flat, sc2=one, unit1=flat, sc1=one, wdown=down_w, hid=wide, wup=up_w, dh=flat_f,
    )
    self_scratch = dict(
        unit0=flat, sc0=one, wout=square, qkv=bf(TALL, 3 * D), bg=flat, gm=tall, dqkv=triple, gb=counts,
    )
    dec_names = dict(
        dk="dk_out", dv="dv_out", dq="dq_out", mixc="mix_out", bg1="bg1_out", hb2="hb_out",
        dhid2="dhid_out", act2="act_out", bg2="bg2_out",
    )
    all_flat, all_wide = bf(ALL, D), bf(ALL, FF)
    cross_names = {k: v for k, v in dec_names.items() if k in ("dk", "dv", "dq", "mixc", "bg1")}
    feed_names = {k: v for k, v in dec_names.items() if k not in cross_names}
    ins = dict(
        base, w_up=wup, w_down=wdown, w_out=wout, gmem=in_vmem(gmem_in[0]),
        hb_0=fwd[0]["hb_out"], act_0=fwd[0]["act_out"],
    )
    ins.update(of(0, fwd[0], **enc_names, **self_names))
    for g in range(2):
        ins.update(of(g, dec[g], **feed_names))
    feed_scratch = dict(
        gf=bf(2 * FF, D), hb=tall, act=bf(TALL, FF), fbg=tall, dhid=bf(TALL, FF),
    )
    feed_outs = dict(gf_out=bf(2 * FF, D))
    cross = call(
        cross_body, "cross_back", 1_000, ins,
        dict(
            ds_out=flat_f, bg_out=flat, dqkv_out=triple, gb_out=counts, **feed_outs,
        ),
        dict(
            **back_scratch, **self_scratch, **feed_scratch,
            all_hb2=all_flat, all_dhid2=all_wide, all_act2=all_wide, all_bg2=all_flat,
        ),
        40, whole=whole + ("gmem",),
    )
    ins = dict(role=role)
    for g in range(2):
        ins.update(of(g, dec[g], **cross_names))
        ins[f"fb_{g}"] = fwd[g]["hb_out"]
        ins[f"mem_{g}"] = mem_in[g]
    ins["dk_1"], gf = lax.optimization_barrier((ins["dk_1"], cross["gf_out"]))
    crossed = call(
        cross_grads_body, "cross_grads", 1_000, ins,
        dict(keep_out=bf(2 * D, D), send_out=bf(2 * D, D)),
        dict(
            **{"all_" + n: all_flat for n in ("mem", "fb", *cross_names)}, gx=bf(2 * D, D), gc=bf(2 * D, D),
        ),
        32,
    )
    crossed_keep, crossed_send, gf = lax.optimization_barrier(
        (crossed["keep_out"], crossed["send_out"], gf)
    )
    crossed_sent = swapped(crossed_send, 1)

    ins = dict(
        base, w_up=wup, w_down=wdown, w_out=wout, gmem=in_vmem(gmem_in[1]), hb_1=fwd[1]["hb_out"],
        act_1=fwd[1]["act_out"], dh_in=dec[1]["dh_out"], gf_in=gf,
    )
    ins.update(of(1, fwd[1], **enc_names))
    feed = call(
        feed_body, "feed_back", 1_000, ins,
        dict(dh_out=flat_f, gb_out=counts, **feed_outs),
        dict(**back_scratch, **feed_scratch, gb=counts),
        32, aliases={name + "_in": name + "_out" for name in ("dh", "gf")}, whole=whole + ("gmem",),
    )
    gf = lax.psum(feed["gf_out"], "dp")
    crossed_x = added(crossed_keep[:D], crossed_sent[:D])
    crossed_c = added(crossed_keep[D:], crossed_sent[D:])
    sums = Sums()
    depth = len(sums.masks)
    part = 2 * D + EXTRA

    def tail():
        last = call(
            self_body, "self_back", 3_000_000_000,
            dict(
                base, dh_0=dec[0]["dh_out"], dh_1=feed["dh_out"], w_out=wout, w_q=wa,
                **of(0, dec[0], dq="dq_out"), **of(1, dec[1], dq="dq_out"),
                **of(0, fwd[0], **self_names), **of(1, fwd[1], **self_names),
            ),
            dict(
                ds_out=flat_f, bg_out=flat, dqkv_out=triple, gb_out=counts,
                ds0_out=flat_f, bg0_out=flat, dqkv0_out=triple,
            ),
            dict(**self_scratch, dh=flat_f, dq=flat, wq=square),
            48, whole=whole,
        )
        gx_in = lax.ppermute(crossed_x, "pipe", back)
        gx_in, ds = lax.optimization_barrier((gx_in, last["ds_out"]))
        c_keep = jnp.where(is_encoder, gx_in, crossed_c)
        early = sums.down([c_keep], (0,), 0, 1)
        ins = dict(
            role=role, gb_cross=cross["gb_out"], gb_dec0=dec[0]["gb_out"], gb_dec1=dec[1]["gb_out"],
            gb_feed=feed["gb_out"], gb_self=last["gb_out"], w_in=win, ds_enc=cross["ds_out"], ds_dec=last["ds0_out"], ds_1=ds,
            bg_enc=cross["bg_out"], bg_dec=last["bg0_out"], bg_1=last["bg_out"], dqkv_enc=cross["dqkv_out"], dqkv_dec=last["dqkv0_out"], dqkv_1=last["dqkv_out"],
        )
        for g in range(2):
            ins.update(of(g, fwd[g], xp="xp_out", mix="mix_out"))
        found = call(
            self_weights_body, "self_weights", 8_000_000_000, ins,
            dict(grads_out=full, keep_out=bf(part, D), send_out=bf(part, D)),
            dict(
                ds=f32(ALL, D), bg=all_flat, dqkv=bf(ALL, 3 * D), xp=all_flat, mix=all_flat, win=in_w,
                dx=full, ga=bf(2 * part, D),
            ),
            20, whole=("gb_cross", "gb_dec0", "gb_dec1", "gb_feed", "gb_self"),
        )
        a_keep = added(found["keep_out"], swapped(found["send_out"], 1))
        early = sums.down(early, (0,), 1, depth)
        late = sums.down([a_keep[:D], a_keep[D:]], (0, 1), 0, depth)
        parts = sums.up(early + late, (0, 0, 1))
        return found["grads_out"], parts, [swapped(p, 1) for p in parts]

    shapes = jax.eval_shape(tail)
    input_grads, parts, others = lax.cond(
        own[0] >= 0,
        tail,
        lambda: jax.tree.map(lambda leaf: jnp.zeros(leaf.shape, leaf.dtype), shapes),
    )
    placed = call(
        place_rest_body, "place_rest", 1_000_000_000,
        dict(
            role=role, c=parts[0], da=parts[1], db=parts[2],
            c_other=others[0], da_other=others[1], db_other=others[2],
        ),
        dict(
            in_out=f32(D, 3 * D), out_out=f32(D, D), gains_out=f32(3, D), biases_out=f32(3, D),
            ca_out=f32(D, D), cb_out=f32(D, D),
        ),
        dict(
            held=bf(2 * part, D), win=f32(D, 3 * D), wout=f32(D, D), gains=f32(3, D), biases=f32(3, D),
            held_c=bf(2 * D, D), ca=f32(D, D), cb=f32(D, D),
        ),
        16,
    )
    placed |= call(
        place_feed_body, "place_feed", 1_000_000_000,
        dict(gf=gf),
        dict(up_out=f32(D, FF), down_out=f32(FF, D)),
        dict(held=bf(2 * FF, D), up=f32(D, FF), down=f32(FF, D)),
        16,
    )
    outs = (
        states, input_grads, placed["in_out"], placed["out_out"], placed["ca_out"], placed["cb_out"],
        placed["up_out"], placed["down_out"], placed["gains_out"], placed["biases_out"],
    )
    return tuple(out[None] for out in outs)


def solution(mesh):
    cut = P("pipe", "dp", None)
    held = P("pipe", None, None)
    return jax.shard_map(
        on_device,
        mesh=mesh,
        in_specs=(cut, P("pipe", "dp")) + (held,) * 8 + (P("dp", None),),
        out_specs=(cut, cut) + (held,) * 8,
        check_vma=False,
    )
```

```python
import functools

import jax
import jax.numpy as jnp
from jax import lax
from jax.experimental import pallas as pl
from jax.experimental.pallas import tpu as pltpu
from jax.sharding import PartitionSpec as P

HEADS = 8
D = 512
FF = 2048
SLOT = 256
PR = 208
GP = 2
GR = GP * PR
TALL = 512
ALL = 896
NORM_EPSILON = 1e-05
BF = jnp.bfloat16
F32 = jnp.float32
CORE_C = 0.7978845608028654
CUBE_C = 0.044715


def dot(a, b):
    return lax.dot_general(a, b, (((1,), (0,)), ((), ())), preferred_element_type=F32)


def dot_t(a, b):
    return lax.dot_general(a, b, (((1,), (1,)), ((), ())), preferred_element_type=F32)


def dot_l(a, b):
    return lax.dot_general(a, b, (((0,), (0,)), ((), ())), preferred_element_type=F32)


def rows_at(start, size, step=16):
    if isinstance(start, int):
        return pl.ds(start, size)
    return pl.ds(pl.multiple_of(start, step), size)


def loop(n, body):
    def run(i, carry):
        body(i)
        return carry

    lax.fori_loop(0, n, run, 0)


def gelu_and_slope(u):
    square = u * u
    bent = jnp.tanh(u * (CORE_C + CORE_C * CUBE_C * square))
    half = 0.5 + 0.5 * bent
    bend = (1.0 - bent) * (CORE_C + 3.0 * CORE_C * CUBE_C * square)
    return u * half, half * (1.0 + u * bend)


def norm_of(summed):
    center = summed - jnp.mean(summed, axis=-1, keepdims=True)
    spread = jnp.mean(center * center, axis=-1, keepdims=True)
    scale = lax.rsqrt(spread + NORM_EPSILON)
    return center * scale, scale


def norm_back(grad, unit, scale, gain):
    lifted = grad * gain
    first = jnp.mean(lifted, axis=-1, keepdims=True)
    second = jnp.mean(lifted * unit, axis=-1, keepdims=True)
    return scale * (lifted - first - unit * second)


def fold8(values):
    return jnp.sum(values.reshape(-1, 8, values.shape[-1]), axis=0)


class Moves:
    def __init__(self, sems):
        self.sems = sems
        self.used = 0
        self.open = []

    def start(self, source, target):
        copy = pltpu.make_async_copy(source, target, self.sems.at[self.used])
        self.used += 1
        copy.start()
        self.open.append(copy)
        return copy

    def wait(self, *copies):
        for copy in copies:
            copy.wait()
            self.open = [c for c in self.open if c is not copy]

    def finish(self):
        for copy in self.open:
            copy.wait()
        self.open = []


def lane_masks():
    lane = lax.broadcasted_iota(jnp.int32, (1, 128), 1)
    low = jnp.where(lane < 64, 1.0, 0.0).astype(BF)
    high = jnp.where(lane < 64, 0.0, 1.0).astype(BF)
    return low, high


def both_heads(rows, low, high):
    return jnp.concatenate([rows * low, rows * high], axis=0)


def merged_heads(stacked):
    lane = lax.broadcasted_iota(jnp.int32, (PR, 128), 1)
    return jnp.where(lane < 64, stacked[:PR], stacked[SLOT : SLOT + PR])


def probs_of(keys, queries, length):
    raw = dot_t(keys, queries)
    place = lax.broadcasted_iota(jnp.int32, raw.shape, 0)
    raw = jnp.where(place < length, raw, -1e30)
    top = jnp.max(raw, axis=0, keepdims=True)
    terms = jnp.exp(raw - top)
    total = jnp.sum(terms, axis=0, keepdims=True)
    return terms * (1.0 / total)


def attend_forward(length_of, q_ref, q_off, k_ref, k_off, v_ref, v_off, out_ref, kept=None):
    low, high = lane_masks()
    low_q, high_q = low * 0.125, high * 0.125

    def pair(p):
        length = length_of(p)
        base = rows_at(p * PR, PR)
        wide = rows_at(p * PR, SLOT)
        for hp in range(4):
            at = hp * 128
            queries = both_heads(q_ref[wide, q_off + at : q_off + at + 128], low_q, high_q)
            keys = k_ref[base, k_off + at : k_off + at + 128]
            values = v_ref[base, v_off + at : v_off + at + 128]
            probs = probs_of(keys, queries, length).astype(BF)
            if kept is not None:
                kept[rows_at((p * 4 + hp) * PR, PR), :] = probs
            out_ref[base, at : at + 128] = merged_heads(dot_l(probs, values)).astype(BF)

    loop(GP, pair)


def attend_backward(
    length_of, q_ref, q_off, k_ref, k_off, v_ref, v_off, g_ref,
    dq_ref, dq_off, dk_ref, dk_off, dv_ref, dv_off, kept=None,
):
    low, high = lane_masks()
    low_q, high_q = low * 0.125, high * 0.125

    def pair(p):
        length = length_of(p)
        base = rows_at(p * PR, PR)
        wide = rows_at(p * PR, SLOT)
        row = lax.broadcasted_iota(jnp.int32, (SLOT, 128), 0)
        for hp in range(4):
            at = hp * 128
            queries = both_heads(q_ref[wide, q_off + at : q_off + at + 128], low_q, high_q)
            keys = k_ref[base, k_off + at : k_off + at + 128]
            values = v_ref[base, v_off + at : v_off + at + 128]
            grads = jnp.where(row < PR, g_ref[wide, at : at + 128].astype(F32), 0.0).astype(BF)
            grads = both_heads(grads, low, high)
            if kept is None:
                probs = probs_of(keys, queries, length)
                probs_low = probs.astype(BF)
            else:
                probs_low = kept[rows_at((p * 4 + hp) * PR, PR), :]
                probs = probs_low.astype(F32)
            grad_probs = dot_t(values, grads)
            mean = jnp.sum(probs * grad_probs, axis=0, keepdims=True)
            grad_raw = (probs * (grad_probs - mean)).astype(BF)
            dv_ref[base, dv_off + at : dv_off + at + 128] = dot(probs_low, grads).astype(BF)
            dk_ref[base, dk_off + at : dk_off + at + 128] = dot(grad_raw, queries).astype(BF)
            dq = merged_heads(dot_l(grad_raw, keys)) * 0.125
            dq_ref[base, dq_off + at : dq_off + at + 128] = dq.astype(BF)

    loop(GP, pair)


def zero_rows(ref, start):
    ref[start:, :] = jnp.zeros((ref.shape[0] - start, ref.shape[1]), ref.dtype)


def feed_forward(w_up, w_down, h_ref, hb_ref, slope_ref, act_ref, got_down, leave):
    hb_ref[...] = h_ref[...].astype(BF)

    for n in range(FF // 512):
        cols = slice(n * 512, (n + 1) * 512)
        active, slope = gelu_and_slope(dot(hb_ref[...], w_up[:, cols]))
        slope_ref[:, cols] = slope.astype(BF)
        act_ref[:, cols] = active.astype(BF)
        leave(cols)

    got_down()
    return h_ref[...] + dot(act_ref[...], w_down[...])


def feed_back(w_up, w_down, ds_ref, bg_ref, slope_ref, dhid_ref):
    for n in range(FF // 512):
        cols = slice(n * 512, (n + 1) * 512)
        grad_act = dot_t(bg_ref[...], w_down[cols, :])
        dhid_ref[:, cols] = (grad_act * slope_ref[:, cols].astype(F32)).astype(BF)

    return ds_ref[...] + dot_t(dhid_ref[...], w_up[...])


def feed_weight_grads(hb_ref, dhid_ref, act_ref, bg_ref, out_ref):
    def column(n):
        cols = rows_at(n * 512, 512, 512)
        out_ref[rows_at(n * 512, 512, 512), :] = dot_l(hb_ref[...], dhid_ref[:, cols]).astype(BF)
        out_ref[rows_at(FF + n * 512, 512, 512), :] = dot_l(act_ref[:, cols], bg_ref[...]).astype(BF)

    loop(FF // 512, column)


def count_norm(gb, index, grad, unit):
    gb[8 * index : 8 * index + 8, :] += fold8(grad * unit)
    gb[24 + 8 * index : 32 + 8 * index, :] += fold8(grad)


def forward_body(group, r):
    moves = Moves(r.sems)
    is_encoder = r.role[0] == 0
    first = group * GP
    got_x = moves.start(r.x_in.at[first * SLOT : (first + GP) * SLOT, :], r.x)
    got_in = moves.start(r.w_in, r.win)
    zero_rows(r.qkv, GR)
    moves.wait(got_x)
    for p in range(GP):
        r.xp[p * PR : (p + 1) * PR, :] = r.x[p * SLOT : p * SLOT + PR, :]
    moves.wait(got_in)
    got_out = moves.start(r.w_out, r.wout)
    got_q = moves.start(r.w_q, r.wq)
    got_up = moves.start(r.w_up, r.wup)
    got_down = moves.start(r.w_down, r.wdown)

    def column(n):
        cols = rows_at(n * 512, 512, 512)
        r.qkv[0:GR, cols] = dot(r.xp[...], r.win[:, cols]).astype(BF)

    loop(3, column)
    moves.start(r.xp, r.xp_out)
    moves.start(r.qkv.at[0:GR, :], r.qkv_out)
    attend_forward(lambda p: r.lengths[first + p], r.qkv, 0, r.qkv, 512, r.qkv, 1024, r.mix)
    moves.start(r.mix, r.mix_out)
    moves.wait(got_out)
    unit, scale = norm_of(r.xp[...].astype(F32) + dot(r.mix[...], r.wout[...]))
    r.unit0[...] = unit.astype(BF)
    r.sc0[...] = scale
    r.h[...] = unit * r.gains[0:1, :] + r.biases[0:1, :]
    moves.start(r.unit0, r.unit0_out)
    moves.start(r.sc0, r.sc0_out)
    moves.start(r.h, r.h_out)
    moves.wait(got_up, got_down, got_q)
    first_used = moves.used

    @pl.when(jnp.logical_not(is_encoder))
    def _():
        own = Moves(r.sems)
        own.used = first_used
        r.hb[...] = r.h[...].astype(BF)
        r.q[...] = dot(r.hb[...], r.wq[...]).astype(BF)
        own.start(r.hb, r.hb_out)
        own.start(r.q, r.q_out)
        own.finish()

    @pl.when(is_encoder)
    def _():
        own = Moves(r.sems)
        own.used = first_used

        def leave(cols):
            own.start(r.hid.at[:, cols], r.hid_out.at[:, cols])
            own.start(r.act.at[:, cols], r.act_out.at[:, cols])

        summed = feed_forward(r.wup, r.wdown, r.h, r.hb, r.hid, r.act, lambda: None, leave)
        own.start(r.hb, r.hb_out)
        unit, scale = norm_of(summed)
        r.unit1[...] = unit.astype(BF)
        r.sc1[...] = scale
        unit, scale = norm_of(unit * r.gains[1:2, :] + r.biases[1:2, :])
        r.unit2[...] = unit.astype(BF)
        r.sc2[...] = scale
        memory = unit * r.gains[2:3, :] + r.biases[2:3, :]
        r.mem[...] = memory.astype(BF)
        r.state[...] = memory
        row = lax.broadcasted_iota(jnp.int32, (16, D), 0)
        place = lax.broadcasted_iota(jnp.int32, (PR, D), 0)
        for p in range(GP):
            length = r.lengths[first + p]
            last = r.mem[(p + 1) * PR - 16 : (p + 1) * PR, :].astype(F32)
            r.mem[(p + 1) * PR - 16 : (p + 1) * PR, :] = jnp.where(
                row < 8, last, length.astype(F32)
            ).astype(BF)
            r.states[p * SLOT : p * SLOT + PR, :] = jnp.where(
                place < length, r.state[p * PR : (p + 1) * PR, :], 0.0
            )
            r.states[p * SLOT + PR : (p + 1) * SLOT, :] = jnp.zeros((SLOT - PR, D), F32)
        own.start(r.mem, r.mem_out)
        for name in ("unit1", "sc1", "unit2", "sc2"):
            own.start(getattr(r, name), getattr(r, name + "_out"))
        own.start(r.states, r.states_out.at[first * SLOT : (first + GP) * SLOT, :])
        own.finish()

    moves.finish()


def decode_body(group, r):
    first = group * GP

    @pl.when(r.role[0] == 1)
    def _():
        moves = Moves(r.sems)
        core = r.role[1]
        got_mine = moves.start(r.mine_in, r.wkv.at[pl.ds(pl.multiple_of(core * D, D), D), :])
        got_other = moves.start(r.other_in, r.wkv.at[pl.ds(pl.multiple_of((1 - core) * D, D), D), :])
        got_q = moves.start(r.q_in, r.q.at[0:GR, :])
        zero_rows(r.q, GR)
        zero_rows(r.gm, GR)
        r.gb[...] = jnp.zeros_like(r.gb)
        moves.wait(got_mine, got_other)
        got_h = moves.start(r.h_in, r.h)
        got_o = moves.start(r.wo_in, r.wo)
        got_up = moves.start(r.w_up, r.wup)
        got_down = moves.start(r.w_down, r.wdown)
        got_cot = moves.start(r.cot_in.at[first * SLOT : (first + GP) * SLOT, :], r.cot)
        r.k[...] = dot(r.mem[...], r.wkv[0:D, :]).astype(BF)
        r.v[...] = dot(r.mem[...], r.wkv[D : 2 * D, :]).astype(BF)
        moves.wait(got_q)

        def length_of(p):
            last = r.mem[rows_at(p * PR + PR - 16, 16), :].astype(F32)
            return last[15:16, :].astype(jnp.int32)

        attend_forward(length_of, r.q, 0, r.k, 0, r.v, 0, r.mix, r.kept)
        moves.start(r.mix, r.mix_out)
        moves.wait(got_h, got_o)
        unit, scale = norm_of(r.h[...] + dot(r.mix[...], r.wo[...]))
        r.unit1[...] = unit.astype(BF)
        r.sc1[...] = scale
        r.h[...] = unit * r.gains[1:2, :] + r.biases[1:2, :]
        moves.wait(got_up, got_cot)
        for p in range(GP):
            place = lax.broadcasted_iota(jnp.int32, (PR, 1), 0)
            valid = jnp.where(place < r.lengths[first + p], 1.0, 0.0)
            r.valid[p * PR : (p + 1) * PR, :] = valid
            r.ds[p * PR : (p + 1) * PR, :] = r.cot[p * SLOT : p * SLOT + PR, :].astype(F32) * valid
        summed = feed_forward(
            r.wup, r.wdown, r.h, r.hb, r.hid, r.act, lambda: moves.wait(got_down),
            lambda cols: moves.start(r.act.at[:, cols], r.act_out.at[:, cols]),
        )
        moves.start(r.hb, r.hb_out)
        unit, scale = norm_of(summed)
        grad = r.ds[...]
        decoded = (unit * r.gains[2:3, :] + r.biases[2:3, :]) * r.valid[...]
        for p in range(GP):
            r.states[p * SLOT : p * SLOT + PR, :] = decoded[p * PR : (p + 1) * PR, :]
            r.states[p * SLOT + PR : (p + 1) * SLOT, :] = jnp.zeros((SLOT - PR, D), F32)
        moves.start(r.states, r.states_out.at[first * SLOT : (first + GP) * SLOT, :])
        count_norm(r.gb, 2, grad, unit)
        grad_sum = norm_back(grad, unit, scale, r.gains[2:3, :])
        r.bg2[...] = grad_sum.astype(BF)
        r.ds[...] = grad_sum
        moves.start(r.bg2, r.bg2_out)
        grad = feed_back(r.wup, r.wdown, r.ds, r.bg2, r.hid, r.dhid)
        moves.start(r.dhid, r.dhid_out)
        unit = r.unit1[...].astype(F32)
        count_norm(r.gb, 1, grad, unit)
        grad_sum = norm_back(grad, unit, r.sc1[...], r.gains[1:2, :])
        r.bg1[...] = grad_sum.astype(BF)
        r.h[...] = grad_sum
        moves.start(r.h, r.dh_out)
        moves.start(r.bg1, r.bg1_out)
        moves.start(r.gb, r.gb_out)
        r.gm[0:GR, :] = dot_t(r.bg1[...], r.wo[...]).astype(BF)
        attend_backward(
            length_of, r.q, 0, r.k, 0, r.v, 0, r.gm, r.dq, 0, r.dk, 0, r.dv, 0, r.kept
        )
        moves.start(r.dq, r.dq_out)
        moves.start(r.dk, r.dk_out)
        moves.start(r.dv, r.dv_out)
        r.gmem[...] = (
            dot_t(r.dk[...], r.wkv[0:D, :]) + dot_t(r.dv[...], r.wkv[D : 2 * D, :])
        ).astype(BF)
        moves.start(r.gmem, r.gmem_out)
        moves.finish()


def self_back_part(r, moves, got, first, outs):
    zero_rows(r.gm, GR)
    zero_rows(r.qkv, GR)
    moves.wait(*got[:-1])
    grad = r.dh[...]
    unit = r.unit0[...].astype(F32)
    count_norm(r.gb, 0, grad, unit)
    grad = norm_back(grad, unit, r.sc0[...], r.gains[0:1, :])
    r.bg[...] = grad.astype(BF)
    r.dh[...] = grad
    moves.start(r.dh, outs[0])
    moves.start(r.bg, outs[1])
    r.gm[0:GR, :] = dot_t(r.bg[...], r.wout[...]).astype(BF)
    moves.wait(got[-1])
    attend_backward(
        lambda p: r.lengths[first + p],
        r.qkv, 0, r.qkv, 512, r.qkv, 1024, r.gm, r.dqkv, 0, r.dqkv, 512, r.dqkv, 1024,
    )
    moves.start(r.dqkv, outs[2])


def self_back_loads(r, moves, group):
    return [
        moves.start(getattr(r, f"unit0_{group}"), r.unit0),
        moves.start(getattr(r, f"sc0_{group}"), r.sc0),
        moves.start(r.w_out, r.wout),
        moves.start(getattr(r, f"qkv_{group}"), r.qkv.at[0:GR, :]),
    ]


def feed_back_loads(r, moves, group):
    return [
        moves.start(getattr(r, f"{name}_{group}"), getattr(r, name))
        for name in ("unit2", "sc2", "unit1", "sc1")
    ] + [
        moves.start(r.w_down, r.wdown),
        moves.start(getattr(r, f"hid_{group}"), r.hid),
        moves.start(r.w_up, r.wup),
    ]


def feed_back_part(r, moves, got, bg, dhid, then=lambda: None):
    moves.wait(*got[:4])
    then()
    grad = r.gmem[...].astype(F32)
    unit = r.unit2[...].astype(F32)
    count_norm(r.gb, 2, grad, unit)
    grad = norm_back(grad, unit, r.sc2[...], r.gains[2:3, :])
    unit = r.unit1[...].astype(F32)
    count_norm(r.gb, 1, grad, unit)
    grad = norm_back(grad, unit, r.sc1[...], r.gains[1:2, :])
    bg[...] = grad.astype(BF)
    r.dh[...] = grad
    moves.wait(*got[4:])
    r.dh[...] = feed_back(r.wup, r.wdown, r.dh, bg, r.hid, dhid)


def stacked_loads(r, moves, name, held):
    zero_rows(held, 2 * GR)
    return [
        moves.start(getattr(r, f"{name}_{g}"), held.at[g * GR : (g + 1) * GR, :]) for g in range(2)
    ]


def cross_body(r):
    @pl.when(r.role[0] == 0)
    def _():
        moves = Moves(r.sems)
        got = feed_back_loads(r, moves, 0)
        got_self = self_back_loads(r, moves, 0)
        got_grads = [group_loads(r, moves, "hb", 0, r.hb), group_loads(r, moves, "act", 0, r.act)]
        r.gb[...] = jnp.zeros_like(r.gb)
        zero_rows(r.dhid, GR)
        zero_rows(r.fbg, GR)
        feed_back_part(r, moves, got, r.fbg.at[0:GR, :], r.dhid.at[0:GR, :])
        first_feed_grads(r, moves, got_grads)
        self_back_part(r, moves, got_self, 0, (r.ds_out, r.bg_out, r.dqkv_out))
        moves.start(r.gb, r.gb_out)
        moves.finish()

    @pl.when(r.role[0] == 1)
    def _():
        moves = Moves(r.sems)
        names = ("hb2", "dhid2", "act2", "bg2")
        got = [c for name in names for c in stacked_loads(r, moves, name, getattr(r, "all_" + name))]
        moves.wait(*got)
        feed_weight_grads(r.all_hb2, r.all_dhid2, r.all_act2, r.all_bg2, r.gf)
        moves.start(r.gf, r.gf_out)
        moves.finish()


def first_feed_grads(r, moves, got):
    moves.wait(*got)
    feed_weight_grads(r.hb, r.dhid, r.act, r.fbg, r.gf)
    moves.start(r.gf, r.gf_out)


def group_loads(r, moves, name, group, held):
    zero_rows(held, GR)
    return moves.start(getattr(r, f"{name}_{group}"), held.at[0:GR, :])


def cross_grads_body(r):
    @pl.when(r.role[0] == 1)
    def _():
        moves = Moves(r.sems)
        names = ("mem", "dk", "dv", "fb", "dq", "mixc", "bg1")
        got = {name: stacked_loads(r, moves, name, getattr(r, "all_" + name)) for name in names}
        moves.wait(*got["mem"], *got["dk"], *got["dv"])
        r.gx[0:D, :] = dot_l(r.all_mem[...], r.all_dk[...]).astype(BF)
        r.gx[D : 2 * D, :] = dot_l(r.all_mem[...], r.all_dv[...]).astype(BF)
        start_halves(moves, r.role[1], r.gx, r.keep_out.at[0:D, :], r.send_out.at[0:D, :])
        moves.wait(*got["fb"], *got["dq"], *got["mixc"], *got["bg1"])
        r.gc[0:D, :] = dot_l(r.all_fb[...], r.all_dq[...]).astype(BF)
        r.gc[D : 2 * D, :] = dot_l(r.all_mixc[...], r.all_bg1[...]).astype(BF)
        start_halves(
            moves, r.role[1], r.gc, r.keep_out.at[D : 2 * D, :], r.send_out.at[D : 2 * D, :]
        )
        moves.finish()


def feed_body(r):
    @pl.when(r.role[0] == 0)
    def _():
        moves = Moves(r.sems)
        got = feed_back_loads(r, moves, 1)
        r.gb[...] = jnp.zeros_like(r.gb)
        zero_rows(r.dhid, GR)
        zero_rows(r.fbg, GR)
        got_grads = []

        def load():
            got_grads.append(group_loads(r, moves, "hb", 1, r.hb))
            got_grads.append(group_loads(r, moves, "act", 1, r.act))
            got_grads.append(moves.start(r.gf_in, r.gf))

        feed_back_part(r, moves, got, r.fbg.at[0:GR, :], r.dhid.at[0:GR, :], load)
        moves.start(r.dh, r.dh_out)
        moves.start(r.gb, r.gb_out)
        moves.wait(*got_grads)
        for n in range(4):
            cols = slice(n * D, (n + 1) * D)
            rows = slice(FF + n * D, FF + (n + 1) * D)
            grad = r.gf[cols, :].astype(F32) + dot_l(r.hb[...], r.dhid[:, cols])
            r.gf[cols, :] = grad.astype(BF)
            moves.start(r.gf.at[cols, :], r.gf_out.at[cols, :])
            grad = r.gf[rows, :].astype(F32) + dot_l(r.act[:, cols], r.fbg[...])
            r.gf[rows, :] = grad.astype(BF)
            moves.start(r.gf.at[rows, :], r.gf_out.at[rows, :])
        moves.finish()


def self_body(r):
    r.gb[...] = jnp.zeros_like(r.gb)
    moves = Moves(r.sems)
    got_dh = moves.start(r.dh_1, r.dh)
    got = self_back_loads(r, moves, 1)

    @pl.when(r.role[0] == 1)
    def _():
        own = Moves(r.sems)
        own.used = 20
        held = ("dh", "unit0", "sc0", "wout", "qkv", "bg", "gm", "dqkv")
        names = (*held, "gains", "lengths", "gb", "unit0_0", "sc0_0", "qkv_0", "w_out")
        first = Refs(names, [getattr(r, n + "_first" if n in held else n) for n in names])
        got_first = own.start(r.dh_0, first.dh)
        got_loads = self_back_loads(first, own, 0)
        got_dq = own.start(r.dq_0, r.dq_first)
        got_dq1 = own.start(r.dq_1, r.dq)
        got_wq = own.start(r.w_q, r.wq)
        own.wait(got_first, got_dq, got_wq)
        first.dh[...] += dot_t(r.dq_first[...], r.wq[...])
        self_back_part(first, own, got_loads, 0, (r.ds0_out, r.bg0_out, r.dqkv0_out))
        own.wait(got_dq1)
        got_dh.wait()
        r.dh[...] += dot_t(r.dq[...], r.wq[...])
        own.finish()

    @pl.when(r.role[0] == 0)
    def _():
        got_dh.wait()

    moves.open = [c for c in moves.open if c is not got_dh]
    self_back_part(r, moves, got, GP, (r.ds_out, r.bg_out, r.dqkv_out))
    moves.start(r.gb, r.gb_out)
    moves.finish()


EXTRA = 64


def chosen_loads(r, moves, name, held):
    zero_rows(held, 2 * GR)
    target = held.at[0:GR, :]
    sem = moves.sems.at[moves.used]
    moves.used += 1
    ours, theirs = (
        pltpu.make_async_copy(getattr(r, f"{name}{which}"), target, sem) for which in ("_enc", "_dec")
    )

    @pl.when(r.role[0] == 0)
    def _():
        ours.start()

    @pl.when(r.role[0] == 1)
    def _():
        theirs.start()

    moves.open.append(ours)
    return [ours, moves.start(getattr(r, f"{name}_1"), held.at[GR : 2 * GR, :])]


def self_weights_body(r):
    moves = Moves(r.sems)
    got_x = stacked_loads(r, moves, "xp", r.xp)
    got_qkv = chosen_loads(r, moves, "dqkv", r.dqkv)
    got_mix = stacked_loads(r, moves, "mix", r.mix)
    got_bg = chosen_loads(r, moves, "bg", r.bg)
    part = 2 * D + EXTRA
    enc = r.gb_cross[...] + r.gb_feed[...]
    dec = r.gb_dec0[...] + r.gb_dec1[...]
    picked = jnp.where(r.role[0] == 0, enc, dec) + r.gb_self[...]
    small = jnp.concatenate(
        [jnp.sum(picked[8 * i : 8 * i + 8, :], axis=0, keepdims=True) for i in range(6)]
        + [jnp.zeros((EXTRA - 6, D), F32)],
        axis=0,
    ).astype(BF)
    r.ga[2 * D : part, :] = small
    r.ga[part + 2 * D : 2 * part, :] = small
    moves.wait(*got_x, *got_qkv)
    r.ga[0:D, :] = dot_l(r.xp[...], r.dqkv[:, 0:D]).astype(BF)
    r.ga[D : 2 * D, :] = dot_l(r.xp[...], r.dqkv[:, D : 2 * D]).astype(BF)
    r.ga[part : part + D, :] = dot_l(r.xp[...], r.dqkv[:, 2 * D : 3 * D]).astype(BF)
    moves.wait(*got_mix, *got_bg)
    r.ga[part + D : part + 2 * D, :] = dot_l(r.mix[...], r.bg[...]).astype(BF)
    start_halves(moves, r.role[1], r.ga, r.keep_out, r.send_out)
    moves.finish()


def self_inputs_body(r):
    moves = Moves(r.sems)
    got = chosen_loads(r, moves, "dqkv", r.dqkv)
    got.append(moves.start(r.w_in, r.win))
    got += chosen_loads(r, moves, "ds", r.ds)
    moves.wait(*got)

    def leave(p):
        at = rows_at(p * PR, PR)
        to = rows_at(p * SLOT, PR)
        r.dx[to, :] = r.ds[at, :] + dot_t(r.dqkv[at, :], r.win[...])
        r.dx[rows_at(p * SLOT + PR, SLOT - PR), :] = jnp.zeros((SLOT - PR, D), F32)

    loop(2 * GP, leave)
    moves.start(r.dx, r.grads_out)
    moves.finish()


def start_halves(moves, core, held, keep, send):
    half = held.shape[0] // 2
    for target, shift in ((keep, 0), (send, 1)):
        start = pl.multiple_of(((core + shift) & 1) * half, 16)
        moves.start(held.at[pl.ds(start, half), :], target)


def place_blocks(core, moves, own, other, held, firsts):
    got = []
    for group, shift in ((own, 0), (other, 1)):
        start = 0
        for ref in group:
            size = ref.shape[0]
            place = pl.multiple_of(((core + shift) & 1) * firsts + start, 16)
            got.append(moves.start(ref, held.at[pl.ds(place, size), :]))
            start += size
    return got


def place_feed_body(r):
    moves = Moves(r.sems)
    got = [
        moves.start(r.gf.at[i * D : (i + 1) * D, :], r.held.at[i * D : (i + 1) * D, :])
        for i in range(8)
    ]
    for i in range(4):
        moves.wait(got[4 + i])
        at = slice(i * D, (i + 1) * D)
        r.down[at, :] = r.held[FF + i * D : FF + (i + 1) * D, :].astype(F32)
        moves.start(r.down.at[at, :], r.down_out.at[at, :])
    moves.wait(*got[:4])
    for i in range(4):
        at = slice(i * 128, (i + 1) * 128)
        for n in range(4):
            r.up[at, n * D : (n + 1) * D] = r.held[
                n * D + i * 128 : n * D + (i + 1) * 128, :
            ].astype(F32)
        moves.start(r.up.at[at, :], r.up_out.at[at, :])
    moves.finish()


def place_rest_body(r):
    moves = Moves(r.sems)
    part = 2 * D + EXTRA
    core = r.role[1]
    got_c = place_blocks(core, moves, [r.c], [r.c_other], r.held_c, D)
    got = place_blocks(core, moves, [r.da, r.db], [r.da_other, r.db_other], r.held, part)
    moves.wait(*got_c)
    r.ca[...] = r.held_c[0:D, :].astype(F32)
    r.cb[...] = r.held_c[D : 2 * D, :].astype(F32)
    moves.start(r.ca, r.ca_out)
    moves.start(r.cb, r.cb_out)
    moves.wait(*got)
    r.wout[...] = r.held[part + D : part + 2 * D, :].astype(F32)
    moves.start(r.wout, r.out_out)
    for n, start in enumerate((0, D, part)):
        r.win[:, n * D : (n + 1) * D] = r.held[start : start + D, :].astype(F32)
    moves.start(r.win, r.in_out)
    small = r.held[2 * D : 2 * D + 16, :].astype(F32)
    for i in range(3):
        r.gains[i] = small[i : i + 1, :]
        r.biases[i] = small[3 + i : 4 + i, :]
    moves.start(r.gains, r.gains_out)
    moves.start(r.biases, r.biases_out)
    moves.finish()


ANY = pl.BlockSpec(memory_space=pl.ANY)
WHOLE = pl.BlockSpec(memory_space=pltpu.VMEM)
SCALARS = pl.BlockSpec(memory_space=pltpu.SMEM)


def in_vmem(array):
    return pltpu.with_memory_space_constraint(array, pltpu.VMEM)


class Refs:
    def __init__(self, names, refs):
        for name, ref in zip(names, refs):
            setattr(self, name, ref)


def call(body, name, flops, ins, outs, scratch, copies, aliases=None, whole=()):
    scalars = ("role", "lengths")
    specs = [SCALARS if n in scalars else WHOLE if n in whole else ANY for n in ins]
    names = [*ins, *outs, *scratch, "sems"]
    position = list(ins).index
    results = list(outs).index

    def kernel(*refs):
        body(Refs(names, refs))

    found = pl.pallas_call(
        kernel,
        out_shape=[jax.ShapeDtypeStruct(s, t) for s, t in outs.values()],
        in_specs=specs,
        out_specs=[ANY] * len(outs),
        scratch_shapes=[pltpu.VMEM(s, t) for s, t in scratch.values()]
        + [pltpu.SemaphoreType.DMA((copies,))],
        input_output_aliases={position(i): results(o) for i, o in (aliases or {}).items()},
        compiler_params=pltpu.CompilerParams(vmem_limit_bytes=60 * 1024 * 1024),
        cost_estimate=pl.CostEstimate(
            flops=flops, bytes_accessed=flops // 1000, transcendentals=0
        ),
        name=name,
    )(*ins.values())
    return dict(zip(outs, found))


def swapped(x, mask, decoders=False):
    size = lax.axis_size("dp")
    if decoders:
        pairs = [(size + i, size + (i ^ mask)) for i in range(size)]
        return lax.ppermute(x, ("pipe", "dp"), pairs)
    return lax.ppermute(x, "dp", [(i, i ^ mask) for i in range(size)])


def added(keep, recv):
    return (keep.astype(F32) + recv.astype(F32)).astype(BF)


def lowered(cur, mask, bit):
    half = cur.shape[0] // 2
    recv = swapped(lax.dynamic_slice_in_dim(cur, (1 - bit) * half, half, 0), mask)
    return added(lax.dynamic_slice_in_dim(cur, bit * half, half, 0), recv)


def raised(cur, mask, bit):
    other = swapped(cur, mask)
    return jnp.where(
        bit == 0, jnp.concatenate([cur, other], 0), jnp.concatenate([other, cur], 0)
    )


class Sums:
    def __init__(self):
        size = lax.axis_size("dp")
        place = lax.axis_index("dp")
        self.masks = [1 << i for i in range(1, size.bit_length() - 1)]
        self.bits = {mask: (place >> (mask.bit_length() - 1)) & 1 for mask in self.masks}

    def order(self, turn):
        masks = self.masks
        return masks if turn == 0 else masks[1:] + masks[:1]

    def down(self, parts, turns, first, last):
        for step in range(first, last):
            parts = [
                lowered(p, self.order(t)[step], self.bits[self.order(t)[step]])
                for p, t in zip(parts, turns)
            ]
        return parts

    def up(self, parts, turns):
        for step in reversed(range(len(self.masks))):
            parts = [
                raised(p, self.order(t)[step], self.bits[self.order(t)[step]])
                for p, t in zip(parts, turns)
            ]
        return parts


def on_device(
    embeds, lengths, attn_in, attn_out, cross_a, cross_b, ffn_up, ffn_down,
    norm_gains, norm_biases, cotangent,
):
    x, own = embeds[0], lengths[0]
    win, wout, wa, wb, wup, wdown = (
        attn_in[0], attn_out[0], cross_a[0], cross_b[0], ffn_up[0], ffn_down[0],
    )
    gains, biases = norm_gains[0], norm_biases[0]
    slots = 2 * GP * SLOT
    pipe = lax.axis_index("pipe")
    is_encoder = pipe == 0
    odd = lax.axis_index("dp") & 1
    role = jnp.stack([pipe, odd]).astype(jnp.int32)
    onward, back = [(0, 1)], [(1, 0)]

    def bf(*shape):
        return (shape, BF)

    def f32(*shape):
        return (shape, F32)

    flat, flat_f, wide, one, triple = bf(GR, D), f32(GR, D), bf(GR, FF), f32(GR, 1), bf(GR, 3 * D)
    full, slot, slot_f = f32(slots, D), bf(GP * SLOT, D), f32(GP * SLOT, D)
    square, up_w, down_w, in_w = bf(D, D), bf(D, FF), bf(FF, D), bf(D, 3 * D)
    tall, counts = bf(TALL, D), f32(48, D)
    base = dict(role=role, lengths=own, gains=gains, biases=biases)
    whole = ("gains", "biases")

    mine = lax.ppermute(jnp.where(odd == 0, wa, wb), "pipe", onward)

    fwd, mem_in, states = [], [], None
    for g in range(2):
        ins = dict(base, x_in=x, w_in=win, w_out=wout, w_up=wup, w_down=wdown, w_q=wa)
        if g:
            ins["states_in"] = states
        fwd.append(
            call(
                functools.partial(forward_body, g), f"forward_{g}", 4_000_000_000, ins,
                dict(
                    h_out=flat_f, xp_out=flat, qkv_out=triple, mix_out=flat, unit0_out=flat, sc0_out=one,
                    mem_out=flat, hb_out=flat, hid_out=wide, act_out=wide, unit1_out=flat, sc1_out=one,
                    unit2_out=flat, sc2_out=one, q_out=flat, states_out=full,
                ),
                dict(
                    q=flat, wq=square, x=slot, win=in_w, wout=square, wup=up_w, wdown=down_w, h=flat_f, xp=flat,
                    qkv=bf(TALL, 3 * D), mix=flat, unit0=flat, sc0=one, mem=flat, hb=flat, hid=wide,
                    act=wide, unit1=flat, sc1=one, unit2=flat, sc2=one, state=flat_f, states=slot_f,
                ),
                36, aliases={"states_in": "states_out"} if g else None, whole=whole,
            )
        )
        states = fwd[g]["states_out"]
        memory = fwd[g]["mem_out"]
        if g == 0:
            mine, memory = lax.optimization_barrier((mine, memory))
            other = swapped(mine, 1)
        mem_in.append(lax.ppermute(memory, "pipe", onward))

    dec, gmem_in = [], []
    for g in range(2):
        dec.append(
            call(
                functools.partial(decode_body, g), f"decode_{g}", 8_000_000_000,
                dict(
                    base, h_in=fwd[g]["h_out"], q_in=fwd[g]["q_out"], mem=in_vmem(mem_in[g]), cot_in=cotangent, wo_in=wb,
                    mine_in=in_vmem(mine), other_in=in_vmem(other), w_up=wup, w_down=wdown, states_in=states,
                ),
                dict(
                    states_out=full, gmem_out=flat, dh_out=flat_f, dq_out=flat, mix_out=flat,
                    bg1_out=flat, dk_out=flat, dv_out=flat, hb_out=flat, dhid_out=wide, act_out=wide,
                    bg2_out=flat, gb_out=counts,
                ),
                dict(
                    kept=bf(GP * 4 * PR, 2 * SLOT), h=flat_f, cot=slot, wo=square, wkv=bf(2 * D, D), wup=up_w,
                    wdown=down_w, states=slot_f, gmem=flat, q=tall, k=flat, v=flat, mix=flat,
                    dq=flat, dk=flat, dv=flat, bg1=flat, hb=flat, hid=wide, dhid=wide, act=wide, bg2=flat,
                    unit1=flat, sc1=one, valid=one, ds=flat_f, gm=tall, gb=counts,
                ),
                36, aliases={"states_in": "states_out"}, whole=whole + ("mem", "mine_in", "other_in"),
            )
        )
        states = dec[g]["states_out"]
        gmem_in.append(lax.ppermute(dec[g]["gmem_out"], "pipe", back))

    def of(group, results, **names):
        return {f"{k}_{group}": results[v] for k, v in names.items()}

    enc_names = dict(
        unit2="unit2_out", sc2="sc2_out", unit1="unit1_out", sc1="sc1_out", hid="hid_out",
    )
    self_names = dict(unit0="unit0_out", sc0="sc0_out", qkv="qkv_out")
    back_scratch = dict(
        unit2=flat, sc2=one, unit1=flat, sc1=one, wdown=down_w, hid=wide, wup=up_w, dh=flat_f,
    )
    self_scratch = dict(
        unit0=flat, sc0=one, wout=square, qkv=bf(TALL, 3 * D), bg=flat, gm=tall, dqkv=triple, gb=counts,
    )
    dec_names = dict(
        dk="dk_out", dv="dv_out", dq="dq_out", mixc="mix_out", bg1="bg1_out", hb2="hb_out",
        dhid2="dhid_out", act2="act_out", bg2="bg2_out",
    )
    all_flat, all_wide = bf(ALL, D), bf(ALL, FF)
    cross_names = {k: v for k, v in dec_names.items() if k in ("dk", "dv", "dq", "mixc", "bg1")}
    feed_names = {k: v for k, v in dec_names.items() if k not in cross_names}
    ins = dict(
        base, w_up=wup, w_down=wdown, w_out=wout, gmem=in_vmem(gmem_in[0]),
        hb_0=fwd[0]["hb_out"], act_0=fwd[0]["act_out"],
    )
    ins.update(of(0, fwd[0], **enc_names, **self_names))
    for g in range(2):
        ins.update(of(g, dec[g], **feed_names))
    feed_scratch = dict(
        gf=bf(2 * FF, D), hb=tall, act=bf(TALL, FF), fbg=tall, dhid=bf(TALL, FF),
    )
    feed_outs = dict(gf_out=bf(2 * FF, D))
    cross = call(
        cross_body, "cross_back", 1_000, ins,
        dict(
            ds_out=flat_f, bg_out=flat, dqkv_out=triple, gb_out=counts, **feed_outs,
        ),
        dict(
            **back_scratch, **self_scratch, **feed_scratch,
            all_hb2=all_flat, all_dhid2=all_wide, all_act2=all_wide, all_bg2=all_flat,
        ),
        40, whole=whole + ("gmem",),
    )
    ins = dict(role=role)
    for g in range(2):
        ins.update(of(g, dec[g], **cross_names))
        ins[f"fb_{g}"] = fwd[g]["hb_out"]
        ins[f"mem_{g}"] = mem_in[g]
    ins["dk_1"], gf = lax.optimization_barrier((ins["dk_1"], cross["gf_out"]))
    crossed = call(
        cross_grads_body, "cross_grads", 1_000, ins,
        dict(keep_out=bf(2 * D, D), send_out=bf(2 * D, D)),
        dict(
            **{"all_" + n: all_flat for n in ("mem", "fb", *cross_names)}, gx=bf(2 * D, D), gc=bf(2 * D, D),
        ),
        32,
    )
    crossed_keep, crossed_send, gf = lax.optimization_barrier(
        (crossed["keep_out"], crossed["send_out"], gf)
    )
    crossed_sent = swapped(crossed_send, 1, True)

    ins = dict(
        base, w_up=wup, w_down=wdown, w_out=wout, gmem=in_vmem(gmem_in[1]), hb_1=fwd[1]["hb_out"],
        act_1=fwd[1]["act_out"], dh_in=dec[1]["dh_out"], gf_in=gf,
    )
    ins.update(of(1, fwd[1], **enc_names))
    feed = call(
        feed_body, "feed_back", 1_000, ins,
        dict(dh_out=flat_f, gb_out=counts, **feed_outs),
        dict(**back_scratch, **feed_scratch, gb=counts),
        32, aliases={name + "_in": name + "_out" for name in ("dh", "gf")}, whole=whole + ("gmem",),
    )
    gf = lax.psum(feed["gf_out"], "dp")
    crossed_x = added(crossed_keep[:D], crossed_sent[:D])
    crossed_c = added(crossed_keep[D:], crossed_sent[D:])
    sums = Sums()
    depth = len(sums.masks)
    part = 2 * D + EXTRA

    def tail():
        last = call(
            self_body, "self_back", 3_000_000_000,
            dict(
                base, dh_0=dec[0]["dh_out"], dh_1=feed["dh_out"], w_out=wout, w_q=wa,
                **of(0, dec[0], dq="dq_out"), **of(1, dec[1], dq="dq_out"),
                **of(0, fwd[0], **self_names), **of(1, fwd[1], **self_names),
            ),
            dict(
                ds_out=flat_f, bg_out=flat, dqkv_out=triple, gb_out=counts,
                ds0_out=flat_f, bg0_out=flat, dqkv0_out=triple,
            ),
            dict(
                **self_scratch, dh=flat_f, dq=flat, wq=square, dh_first=flat_f, dq_first=flat,
                **{n + "_first": self_scratch[n] for n in self_scratch if n != "gb"},
            ),
            48, whole=whole,
        )
        gx_in = lax.ppermute(crossed_x, "pipe", back)
        gx_in, last["bg_out"] = lax.optimization_barrier((gx_in, last["bg_out"]))
        ds = last["ds_out"]
        c_keep = jnp.where(is_encoder, gx_in, crossed_c)
        early = sums.down([c_keep], (0,), 0, 1)
        dqkv = dict(dqkv_enc=cross["dqkv_out"], dqkv_dec=last["dqkv0_out"], dqkv_1=last["dqkv_out"])
        ins = dict(
            role=role, gb_cross=cross["gb_out"], gb_dec0=dec[0]["gb_out"], gb_dec1=dec[1]["gb_out"],
            gb_feed=feed["gb_out"], gb_self=last["gb_out"], bg_enc=cross["bg_out"],
            bg_dec=last["bg0_out"], bg_1=last["bg_out"], **dqkv,
        )
        for g in range(2):
            ins.update(of(g, fwd[g], xp="xp_out", mix="mix_out"))
        found = call(
            self_weights_body, "self_weights", 4_000_000_000, ins,
            dict(keep_out=bf(part, D), send_out=bf(part, D)),
            dict(bg=all_flat, dqkv=bf(ALL, 3 * D), xp=all_flat, mix=all_flat, ga=bf(2 * part, D)),
            20, whole=("gb_cross", "gb_dec0", "gb_dec1", "gb_feed", "gb_self"),
        )
        found |= call(
            self_inputs_body, "self_inputs", 6_000_000_000,
            dict(
                role=role, w_in=win, ds_enc=cross["ds_out"], ds_dec=last["ds0_out"], ds_1=ds, **dqkv,
            ),
            dict(grads_out=full),
            dict(ds=f32(ALL, D), dqkv=bf(ALL, 3 * D), win=in_w, dx=full),
            12,
        )
        a_keep = added(found["keep_out"], swapped(found["send_out"], 1))
        early = sums.down(early, (0,), 1, depth)
        late = sums.down([a_keep[:D], a_keep[D:]], (0, 1), 0, 1)
        late, grads = lax.optimization_barrier((late, found["grads_out"]))
        late = sums.down(late, (0, 1), 1, depth)
        parts = sums.up(early + late, (0, 0, 1))
        return grads, parts, [swapped(p, 1) for p in parts]

    shapes = jax.eval_shape(tail)
    input_grads, parts, others = lax.cond(
        own[0] >= 0,
        tail,
        lambda: jax.tree.map(lambda leaf: jnp.zeros(leaf.shape, leaf.dtype), shapes),
    )
    placed = call(
        place_rest_body, "place_rest", 1_000_000_000,
        dict(
            role=role, c=parts[0], da=parts[1], db=parts[2],
            c_other=others[0], da_other=others[1], db_other=others[2],
        ),
        dict(
            in_out=f32(D, 3 * D), out_out=f32(D, D), gains_out=f32(3, 1, D), biases_out=f32(3, 1, D),
            ca_out=f32(D, D), cb_out=f32(D, D),
        ),
        dict(
            held=bf(2 * part, D), win=f32(D, 3 * D), wout=f32(D, D), gains=f32(3, 1, D), biases=f32(3, 1, D),
            held_c=bf(2 * D, D), ca=f32(D, D), cb=f32(D, D),
        ),
        16,
    )
    placed |= call(
        place_feed_body, "place_feed", 1_000_000_000,
        dict(gf=gf),
        dict(up_out=f32(D, FF), down_out=f32(FF, D)),
        dict(held=bf(2 * FF, D), up=f32(D, FF), down=f32(FF, D)),
        16,
    )
    outs = (
        states, input_grads, placed["in_out"], placed["out_out"], placed["ca_out"], placed["cb_out"],
        placed["up_out"], placed["down_out"],
    )
    small = (placed["gains_out"], placed["biases_out"])
    return tuple(out[None] for out in outs) + tuple(out.transpose(1, 0, 2) for out in small)


def solution(mesh):
    cut = P("pipe", "dp", None)
    held = P("pipe", None, None)
    return jax.shard_map(
        on_device,
        mesh=mesh,
        in_specs=(cut, P("pipe", "dp")) + (held,) * 8 + (P("dp", None),),
        out_specs=(cut, cut) + (held,) * 8,
        check_vma=False,
    )
```

```python
import functools

import jax
import jax.numpy as jnp
from jax import lax
from jax.experimental import pallas as pl
from jax.experimental.pallas import tpu as pltpu
from jax.sharding import PartitionSpec as P

HEADS = 8
D = 512
FF = 2048
SLOT = 256
PR = 208
GP = 2
GR = GP * PR
TALL = 512
ALL = 896
NORM_EPSILON = 1e-05
BF = jnp.bfloat16
F32 = jnp.float32
CORE_C = 0.7978845608028654
CUBE_C = 0.044715


def dot(a, b):
    return lax.dot_general(a, b, (((1,), (0,)), ((), ())), preferred_element_type=F32)


def dot_t(a, b):
    return lax.dot_general(a, b, (((1,), (1,)), ((), ())), preferred_element_type=F32)


def dot_l(a, b):
    return lax.dot_general(a, b, (((0,), (0,)), ((), ())), preferred_element_type=F32)


def rows_at(start, size, step=16):
    if isinstance(start, int):
        return pl.ds(start, size)
    return pl.ds(pl.multiple_of(start, step), size)


def loop(n, body):
    def run(i, carry):
        body(i)
        return carry

    lax.fori_loop(0, n, run, 0)


def gelu_and_slope(u):
    square = u * u
    bent = jnp.tanh(u * (CORE_C + CORE_C * CUBE_C * square))
    half = 0.5 + 0.5 * bent
    bend = (1.0 - bent) * (CORE_C + 3.0 * CORE_C * CUBE_C * square)
    return u * half, half * (1.0 + u * bend)


def norm_of(summed):
    center = summed - jnp.mean(summed, axis=-1, keepdims=True)
    spread = jnp.mean(center * center, axis=-1, keepdims=True)
    scale = lax.rsqrt(spread + NORM_EPSILON)
    return center * scale, scale


def norm_back(grad, unit, scale, gain):
    lifted = grad * gain
    first = jnp.mean(lifted, axis=-1, keepdims=True)
    second = jnp.mean(lifted * unit, axis=-1, keepdims=True)
    return scale * (lifted - first - unit * second)


def fold8(values):
    return jnp.sum(values.reshape(-1, 8, values.shape[-1]), axis=0)


class Moves:
    def __init__(self, sems):
        self.sems = sems
        self.used = 0
        self.open = []

    def start(self, source, target):
        copy = pltpu.make_async_copy(source, target, self.sems.at[self.used])
        self.used += 1
        copy.start()
        self.open.append(copy)
        return copy

    def wait(self, *copies):
        for copy in copies:
            copy.wait()
            self.open = [c for c in self.open if c is not copy]

    def finish(self):
        for copy in self.open:
            copy.wait()
        self.open = []


def lane_masks():
    lane = lax.broadcasted_iota(jnp.int32, (1, 128), 1)
    low = jnp.where(lane < 64, 1.0, 0.0).astype(BF)
    high = jnp.where(lane < 64, 0.0, 1.0).astype(BF)
    return low, high


def both_heads(rows, low, high):
    return jnp.concatenate([rows * low, rows * high], axis=0)


def merged_heads(stacked):
    lane = lax.broadcasted_iota(jnp.int32, (PR, 128), 1)
    return jnp.where(lane < 64, stacked[:PR], stacked[SLOT : SLOT + PR])


def probs_of(keys, queries, length):
    raw = dot_t(keys, queries)
    place = lax.broadcasted_iota(jnp.int32, raw.shape, 0)
    raw = jnp.where(place < length, raw, -1e30)
    top = jnp.max(raw, axis=0, keepdims=True)
    terms = jnp.exp(raw - top)
    total = jnp.sum(terms, axis=0, keepdims=True)
    return terms * (1.0 / total)


def attend_forward(length_of, q_ref, q_off, k_ref, k_off, v_ref, v_off, out_ref, kept=None):
    low, high = lane_masks()
    low_q, high_q = low * 0.125, high * 0.125

    def pair(p):
        length = length_of(p)
        base = rows_at(p * PR, PR)
        wide = rows_at(p * PR, SLOT)
        for hp in range(4):
            at = hp * 128
            queries = both_heads(q_ref[wide, q_off + at : q_off + at + 128], low_q, high_q)
            keys = k_ref[base, k_off + at : k_off + at + 128]
            values = v_ref[base, v_off + at : v_off + at + 128]
            probs = probs_of(keys, queries, length).astype(BF)
            if kept is not None:
                kept[rows_at((p * 4 + hp) * PR, PR), :] = probs
            out_ref[base, at : at + 128] = merged_heads(dot_l(probs, values)).astype(BF)

    loop(GP, pair)


def attend_backward(
    length_of, q_ref, q_off, k_ref, k_off, v_ref, v_off, g_ref,
    dq_ref, dq_off, dk_ref, dk_off, dv_ref, dv_off, kept=None,
):
    low, high = lane_masks()
    low_q, high_q = low * 0.125, high * 0.125

    def pair(p):
        length = length_of(p)
        base = rows_at(p * PR, PR)
        wide = rows_at(p * PR, SLOT)
        row = lax.broadcasted_iota(jnp.int32, (SLOT, 128), 0)
        for hp in range(4):
            at = hp * 128
            queries = both_heads(q_ref[wide, q_off + at : q_off + at + 128], low_q, high_q)
            keys = k_ref[base, k_off + at : k_off + at + 128]
            values = v_ref[base, v_off + at : v_off + at + 128]
            grads = jnp.where(row < PR, g_ref[wide, at : at + 128].astype(F32), 0.0).astype(BF)
            grads = both_heads(grads, low, high)
            if kept is None:
                probs = probs_of(keys, queries, length)
                probs_low = probs.astype(BF)
            else:
                probs_low = kept[rows_at((p * 4 + hp) * PR, PR), :]
                probs = probs_low.astype(F32)
            grad_probs = dot_t(values, grads)
            mean = jnp.sum(probs * grad_probs, axis=0, keepdims=True)
            grad_raw = (probs * (grad_probs - mean)).astype(BF)
            dv_ref[base, dv_off + at : dv_off + at + 128] = dot(probs_low, grads).astype(BF)
            dk_ref[base, dk_off + at : dk_off + at + 128] = dot(grad_raw, queries).astype(BF)
            dq = merged_heads(dot_l(grad_raw, keys)) * 0.125
            dq_ref[base, dq_off + at : dq_off + at + 128] = dq.astype(BF)

    loop(GP, pair)


def zero_rows(ref, start):
    ref[start:, :] = jnp.zeros((ref.shape[0] - start, ref.shape[1]), ref.dtype)


def feed_forward(w_up, w_down, h_ref, hb_ref, slope_ref, act_ref, got_down, leave):
    hb_ref[...] = h_ref[...].astype(BF)

    for n in range(FF // 512):
        cols = slice(n * 512, (n + 1) * 512)
        active, slope = gelu_and_slope(dot(hb_ref[...], w_up[:, cols]))
        slope_ref[:, cols] = slope.astype(BF)
        act_ref[:, cols] = active.astype(BF)
        leave(cols)

    got_down()
    return h_ref[...] + dot(act_ref[...], w_down[...])


def feed_back(w_up, w_down, ds_ref, bg_ref, slope_ref, dhid_ref):
    for n in range(FF // 512):
        cols = slice(n * 512, (n + 1) * 512)
        grad_act = dot_t(bg_ref[...], w_down[cols, :])
        dhid_ref[:, cols] = (grad_act * slope_ref[:, cols].astype(F32)).astype(BF)

    return ds_ref[...] + dot_t(dhid_ref[...], w_up[...])


def feed_weight_grads(hb_ref, dhid_ref, act_ref, bg_ref, out_ref):
    def column(n):
        cols = rows_at(n * 512, 512, 512)
        out_ref[rows_at(n * 512, 512, 512), :] = dot_l(hb_ref[...], dhid_ref[:, cols]).astype(BF)
        out_ref[rows_at(FF + n * 512, 512, 512), :] = dot_l(act_ref[:, cols], bg_ref[...]).astype(BF)

    loop(FF // 512, column)


def count_norm(gb, index, grad, unit):
    gb[8 * index : 8 * index + 8, :] += fold8(grad * unit)
    gb[24 + 8 * index : 32 + 8 * index, :] += fold8(grad)


def forward_body(group, r):
    moves = Moves(r.sems)
    is_encoder = r.role[0] == 0
    first = group * GP
    got_x = moves.start(r.x_in.at[first * SLOT : (first + GP) * SLOT, :], r.x)
    thirds = [slice(n * D, (n + 1) * D) for n in range(3)]
    got_in = [moves.start(r.w_in.at[:, cols], r.win.at[:, cols]) for cols in thirds]
    zero_rows(r.qkv, GR)
    moves.wait(got_x)
    for p in range(GP):
        r.xp[p * PR : (p + 1) * PR, :] = r.x[p * SLOT : p * SLOT + PR, :]
    moves.wait(got_in[0])
    got_out = moves.start(r.w_out, r.wout)
    got_q = moves.start(r.w_q, r.wq)
    got_up = moves.start(r.w_up, r.wup)
    got_down = moves.start(r.w_down, r.wdown)

    for n, cols in enumerate(thirds):
        if n:
            moves.wait(got_in[n])
        r.qkv[0:GR, cols] = dot(r.xp[...], r.win[:, cols]).astype(BF)

    moves.start(r.xp, r.xp_out)
    moves.start(r.qkv.at[0:GR, :], r.qkv_out)
    attend_forward(lambda p: r.lengths[first + p], r.qkv, 0, r.qkv, 512, r.qkv, 1024, r.mix)
    moves.start(r.mix, r.mix_out)
    moves.wait(got_out)
    unit, scale = norm_of(r.xp[...].astype(F32) + dot(r.mix[...], r.wout[...]))
    r.unit0[...] = unit.astype(BF)
    r.sc0[...] = scale
    r.h[...] = unit * r.gains[0:1, :] + r.biases[0:1, :]
    moves.start(r.unit0, r.unit0_out)
    moves.start(r.sc0, r.sc0_out)
    moves.start(r.h, r.h_out)
    moves.wait(got_up, got_down, got_q)
    first_used = moves.used

    @pl.when(jnp.logical_not(is_encoder))
    def _():
        own = Moves(r.sems)
        own.used = first_used
        r.hb[...] = r.h[...].astype(BF)
        r.q[...] = dot(r.hb[...], r.wq[...]).astype(BF)
        own.start(r.hb, r.hb_out)
        own.start(r.q, r.q_out)
        own.finish()

    @pl.when(is_encoder)
    def _():
        own = Moves(r.sems)
        own.used = first_used

        def leave(cols):
            own.start(r.hid.at[:, cols], r.hid_out.at[:, cols])
            own.start(r.act.at[:, cols], r.act_out.at[:, cols])

        summed = feed_forward(r.wup, r.wdown, r.h, r.hb, r.hid, r.act, lambda: None, leave)
        own.start(r.hb, r.hb_out)
        unit, scale = norm_of(summed)
        r.unit1[...] = unit.astype(BF)
        r.sc1[...] = scale
        unit, scale = norm_of(unit * r.gains[1:2, :] + r.biases[1:2, :])
        r.unit2[...] = unit.astype(BF)
        r.sc2[...] = scale
        memory = unit * r.gains[2:3, :] + r.biases[2:3, :]
        r.mem[...] = memory.astype(BF)
        r.state[...] = memory
        row = lax.broadcasted_iota(jnp.int32, (16, D), 0)
        place = lax.broadcasted_iota(jnp.int32, (PR, D), 0)
        for p in range(GP):
            length = r.lengths[first + p]
            last = r.mem[(p + 1) * PR - 16 : (p + 1) * PR, :].astype(F32)
            r.mem[(p + 1) * PR - 16 : (p + 1) * PR, :] = jnp.where(
                row < 8, last, length.astype(F32)
            ).astype(BF)
            r.states[p * SLOT : p * SLOT + PR, :] = jnp.where(
                place < length, r.state[p * PR : (p + 1) * PR, :], 0.0
            )
            r.states[p * SLOT + PR : (p + 1) * SLOT, :] = jnp.zeros((SLOT - PR, D), F32)
        own.start(r.mem, r.mem_out)
        for name in ("unit1", "sc1", "unit2", "sc2"):
            own.start(getattr(r, name), getattr(r, name + "_out"))
        own.start(r.states, r.states_out.at[first * SLOT : (first + GP) * SLOT, :])
        own.finish()

    moves.finish()


def decode_body(group, r):
    first = group * GP

    @pl.when(r.role[0] == 1)
    def _():
        moves = Moves(r.sems)
        core = r.role[1]
        got_mine = moves.start(r.mine_in, r.wkv.at[pl.ds(pl.multiple_of(core * D, D), D), :])
        got_other = moves.start(r.other_in, r.wkv.at[pl.ds(pl.multiple_of((1 - core) * D, D), D), :])
        got_q = moves.start(r.q_in, r.q.at[0:GR, :])
        zero_rows(r.q, GR)
        zero_rows(r.gm, GR)
        r.gb[...] = jnp.zeros_like(r.gb)
        moves.wait(got_mine, got_other)
        got_h = moves.start(r.h_in, r.h)
        got_o = moves.start(r.wo_in, r.wo)
        got_up = moves.start(r.w_up, r.wup)
        got_down = moves.start(r.w_down, r.wdown)
        got_cot = moves.start(r.cot_in.at[first * SLOT : (first + GP) * SLOT, :], r.cot)
        r.k[...] = dot(r.mem[...], r.wkv[0:D, :]).astype(BF)
        r.v[...] = dot(r.mem[...], r.wkv[D : 2 * D, :]).astype(BF)
        moves.wait(got_q)

        def length_of(p):
            last = r.mem[rows_at(p * PR + PR - 16, 16), :].astype(F32)
            return last[15:16, :].astype(jnp.int32)

        attend_forward(length_of, r.q, 0, r.k, 0, r.v, 0, r.mix, r.kept)
        moves.start(r.mix, r.mix_out)
        moves.wait(got_h, got_o)
        unit, scale = norm_of(r.h[...] + dot(r.mix[...], r.wo[...]))
        r.unit1[...] = unit.astype(BF)
        r.sc1[...] = scale
        r.h[...] = unit * r.gains[1:2, :] + r.biases[1:2, :]
        moves.wait(got_up, got_cot)
        for p in range(GP):
            place = lax.broadcasted_iota(jnp.int32, (PR, 1), 0)
            valid = jnp.where(place < r.lengths[first + p], 1.0, 0.0)
            r.valid[p * PR : (p + 1) * PR, :] = valid
            r.ds[p * PR : (p + 1) * PR, :] = r.cot[p * SLOT : p * SLOT + PR, :].astype(F32) * valid
        summed = feed_forward(
            r.wup, r.wdown, r.h, r.hb, r.hid, r.act, lambda: moves.wait(got_down),
            lambda cols: moves.start(r.act.at[:, cols], r.act_out.at[:, cols]),
        )
        moves.start(r.hb, r.hb_out)
        unit, scale = norm_of(summed)
        grad = r.ds[...]
        decoded = (unit * r.gains[2:3, :] + r.biases[2:3, :]) * r.valid[...]
        for p in range(GP):
            r.states[p * SLOT : p * SLOT + PR, :] = decoded[p * PR : (p + 1) * PR, :]
            r.states[p * SLOT + PR : (p + 1) * SLOT, :] = jnp.zeros((SLOT - PR, D), F32)
        moves.start(r.states, r.states_out.at[first * SLOT : (first + GP) * SLOT, :])
        count_norm(r.gb, 2, grad, unit)
        grad_sum = norm_back(grad, unit, scale, r.gains[2:3, :])
        r.bg2[...] = grad_sum.astype(BF)
        r.ds[...] = grad_sum
        moves.start(r.bg2, r.bg2_out)
        grad = feed_back(r.wup, r.wdown, r.ds, r.bg2, r.hid, r.dhid)
        moves.start(r.dhid, r.dhid_out)
        unit = r.unit1[...].astype(F32)
        count_norm(r.gb, 1, grad, unit)
        grad_sum = norm_back(grad, unit, r.sc1[...], r.gains[1:2, :])
        r.bg1[...] = grad_sum.astype(BF)
        r.h[...] = grad_sum
        moves.start(r.h, r.dh_out)
        moves.start(r.bg1, r.bg1_out)
        moves.start(r.gb, r.gb_out)
        r.gm[0:GR, :] = dot_t(r.bg1[...], r.wo[...]).astype(BF)
        attend_backward(
            length_of, r.q, 0, r.k, 0, r.v, 0, r.gm, r.dq, 0, r.dk, 0, r.dv, 0, r.kept
        )
        moves.start(r.dq, r.dq_out)
        moves.start(r.dk, r.dk_out)
        moves.start(r.dv, r.dv_out)
        r.gmem[...] = (
            dot_t(r.dk[...], r.wkv[0:D, :]) + dot_t(r.dv[...], r.wkv[D : 2 * D, :])
        ).astype(BF)
        moves.start(r.gmem, r.gmem_out)
        moves.finish()


def self_back_part(r, moves, got, first, outs):
    zero_rows(r.gm, GR)
    zero_rows(r.qkv, GR)
    moves.wait(*got[:-1])
    grad = r.dh[...]
    unit = r.unit0[...].astype(F32)
    count_norm(r.gb, 0, grad, unit)
    grad = norm_back(grad, unit, r.sc0[...], r.gains[0:1, :])
    r.bg[...] = grad.astype(BF)
    r.dh[...] = grad
    moves.start(r.dh, outs[0])
    moves.start(r.bg, outs[1])
    r.gm[0:GR, :] = dot_t(r.bg[...], r.wout[...]).astype(BF)
    moves.wait(got[-1])
    attend_backward(
        lambda p: r.lengths[first + p],
        r.qkv, 0, r.qkv, 512, r.qkv, 1024, r.gm, r.dqkv, 0, r.dqkv, 512, r.dqkv, 1024,
    )
    moves.start(r.dqkv, outs[2])


def self_back_loads(r, moves, group):
    return [
        moves.start(getattr(r, f"unit0_{group}"), r.unit0),
        moves.start(getattr(r, f"sc0_{group}"), r.sc0),
        moves.start(r.w_out, r.wout),
        moves.start(getattr(r, f"qkv_{group}"), r.qkv.at[0:GR, :]),
    ]


def feed_back_loads(r, moves, group):
    return [
        moves.start(getattr(r, f"{name}_{group}"), getattr(r, name))
        for name in ("unit2", "sc2", "unit1", "sc1")
    ] + [
        moves.start(r.w_down, r.wdown),
        moves.start(getattr(r, f"hid_{group}"), r.hid),
        moves.start(r.w_up, r.wup),
    ]


def feed_back_part(r, moves, got, bg, dhid, then=lambda: None):
    moves.wait(*got[:4])
    then()
    grad = r.gmem[...].astype(F32)
    unit = r.unit2[...].astype(F32)
    count_norm(r.gb, 2, grad, unit)
    grad = norm_back(grad, unit, r.sc2[...], r.gains[2:3, :])
    unit = r.unit1[...].astype(F32)
    count_norm(r.gb, 1, grad, unit)
    grad = norm_back(grad, unit, r.sc1[...], r.gains[1:2, :])
    bg[...] = grad.astype(BF)
    r.dh[...] = grad
    moves.wait(*got[4:])
    r.dh[...] = feed_back(r.wup, r.wdown, r.dh, bg, r.hid, dhid)


def stacked_loads(r, moves, name, held):
    zero_rows(held, 2 * GR)
    return [
        moves.start(getattr(r, f"{name}_{g}"), held.at[g * GR : (g + 1) * GR, :]) for g in range(2)
    ]


def cross_body(r):
    @pl.when(r.role[0] == 0)
    def _():
        moves = Moves(r.sems)
        got = feed_back_loads(r, moves, 0)
        got_self = self_back_loads(r, moves, 0)
        got_grads = [group_loads(r, moves, "hb", 0, r.hb), group_loads(r, moves, "act", 0, r.act)]
        r.gb[...] = jnp.zeros_like(r.gb)
        zero_rows(r.dhid, GR)
        zero_rows(r.fbg, GR)
        feed_back_part(r, moves, got, r.fbg.at[0:GR, :], r.dhid.at[0:GR, :])
        first_feed_grads(r, moves, got_grads)
        self_back_part(r, moves, got_self, 0, (r.ds_out, r.bg_out, r.dqkv_out))
        moves.start(r.gb, r.gb_out)
        moves.finish()

    @pl.when(r.role[0] == 1)
    def _():
        moves = Moves(r.sems)
        names = ("hb2", "dhid2", "act2", "bg2")
        got = [c for name in names for c in stacked_loads(r, moves, name, getattr(r, "all_" + name))]
        moves.wait(*got)
        feed_weight_grads(r.all_hb2, r.all_dhid2, r.all_act2, r.all_bg2, r.gf)
        moves.start(r.gf, r.gf_out)
        moves.finish()


def first_feed_grads(r, moves, got):
    moves.wait(*got)
    feed_weight_grads(r.hb, r.dhid, r.act, r.fbg, r.gf)
    moves.start(r.gf, r.gf_out)


def group_loads(r, moves, name, group, held):
    zero_rows(held, GR)
    return moves.start(getattr(r, f"{name}_{group}"), held.at[0:GR, :])


def cross_grads_body(r):
    @pl.when(r.role[0] == 1)
    def _():
        moves = Moves(r.sems)
        names = ("mem", "dk", "dv", "fb", "dq", "mixc", "bg1")
        got = {name: stacked_loads(r, moves, name, getattr(r, "all_" + name)) for name in names}
        moves.wait(*got["mem"], *got["dk"], *got["dv"])
        r.gx[0:D, :] = dot_l(r.all_mem[...], r.all_dk[...]).astype(BF)
        r.gx[D : 2 * D, :] = dot_l(r.all_mem[...], r.all_dv[...]).astype(BF)
        start_halves(moves, r.role[1], r.gx, r.keep_out.at[0:D, :], r.send_out.at[0:D, :])
        moves.wait(*got["fb"], *got["dq"], *got["mixc"], *got["bg1"])
        r.gc[0:D, :] = dot_l(r.all_fb[...], r.all_dq[...]).astype(BF)
        r.gc[D : 2 * D, :] = dot_l(r.all_mixc[...], r.all_bg1[...]).astype(BF)
        start_halves(
            moves, r.role[1], r.gc, r.keep_out.at[D : 2 * D, :], r.send_out.at[D : 2 * D, :]
        )
        moves.finish()


def feed_body(r):
    @pl.when(r.role[0] == 0)
    def _():
        moves = Moves(r.sems)
        got = feed_back_loads(r, moves, 1)
        r.gb[...] = jnp.zeros_like(r.gb)
        zero_rows(r.dhid, GR)
        zero_rows(r.fbg, GR)
        got_grads = []

        def load():
            got_grads.append(group_loads(r, moves, "hb", 1, r.hb))
            got_grads.append(group_loads(r, moves, "act", 1, r.act))
            got_grads.append(moves.start(r.gf_in, r.gf))

        feed_back_part(r, moves, got, r.fbg.at[0:GR, :], r.dhid.at[0:GR, :], load)
        moves.start(r.dh, r.dh_out)
        moves.start(r.gb, r.gb_out)
        moves.wait(*got_grads)
        for n in range(4):
            cols = slice(n * D, (n + 1) * D)
            rows = slice(FF + n * D, FF + (n + 1) * D)
            grad = r.gf[cols, :].astype(F32) + dot_l(r.hb[...], r.dhid[:, cols])
            r.gf[cols, :] = grad.astype(BF)
            moves.start(r.gf.at[cols, :], r.gf_out.at[cols, :])
            grad = r.gf[rows, :].astype(F32) + dot_l(r.act[:, cols], r.fbg[...])
            r.gf[rows, :] = grad.astype(BF)
            moves.start(r.gf.at[rows, :], r.gf_out.at[rows, :])
        moves.finish()


def self_body(r):
    r.gb[...] = jnp.zeros_like(r.gb)
    moves = Moves(r.sems)
    got_dh = moves.start(r.dh_1, r.dh)
    got = self_back_loads(r, moves, 1)

    @pl.when(r.role[0] == 1)
    def _():
        own = Moves(r.sems)
        own.used = 20
        held = ("dh", "unit0", "sc0", "wout", "qkv", "bg", "gm", "dqkv")
        names = (*held, "gains", "lengths", "gb", "unit0_0", "sc0_0", "qkv_0", "w_out")
        first = Refs(names, [getattr(r, n + "_first" if n in held else n) for n in names])
        got_first = own.start(r.dh_0, first.dh)
        got_loads = self_back_loads(first, own, 0)
        got_dq = own.start(r.dq_0, r.dq_first)
        got_dq1 = own.start(r.dq_1, r.dq)
        got_wq = own.start(r.w_q, r.wq)
        own.wait(got_first, got_dq, got_wq)
        first.dh[...] += dot_t(r.dq_first[...], r.wq[...])
        self_back_part(first, own, got_loads, 0, (r.ds0_out, r.bg0_out, r.dqkv0_out))
        own.wait(got_dq1)
        got_dh.wait()
        r.dh[...] += dot_t(r.dq[...], r.wq[...])
        own.finish()

    @pl.when(r.role[0] == 0)
    def _():
        got_dh.wait()

    moves.open = [c for c in moves.open if c is not got_dh]
    self_back_part(r, moves, got, GP, (r.ds_out, r.bg_out, r.dqkv_out))
    moves.start(r.gb, r.gb_out)
    moves.finish()


EXTRA = 64


def chosen_loads(r, moves, name, held):
    zero_rows(held, 2 * GR)
    target = held.at[0:GR, :]
    sem = moves.sems.at[moves.used]
    moves.used += 1
    ours, theirs = (
        pltpu.make_async_copy(getattr(r, f"{name}{which}"), target, sem) for which in ("_enc", "_dec")
    )

    @pl.when(r.role[0] == 0)
    def _():
        ours.start()

    @pl.when(r.role[0] == 1)
    def _():
        theirs.start()

    moves.open.append(ours)
    return [ours, moves.start(getattr(r, f"{name}_1"), held.at[GR : 2 * GR, :])]


def self_weights_body(r):
    moves = Moves(r.sems)
    got_x = stacked_loads(r, moves, "xp", r.xp)
    got_qkv = chosen_loads(r, moves, "dqkv", r.dqkv)
    got_mix = stacked_loads(r, moves, "mix", r.mix)
    got_bg = chosen_loads(r, moves, "bg", r.bg)
    part = 2 * D + EXTRA
    enc = r.gb_cross[...] + r.gb_feed[...]
    dec = r.gb_dec0[...] + r.gb_dec1[...]
    picked = jnp.where(r.role[0] == 0, enc, dec) + r.gb_self[...]
    small = jnp.concatenate(
        [jnp.sum(picked[8 * i : 8 * i + 8, :], axis=0, keepdims=True) for i in range(6)]
        + [jnp.zeros((EXTRA - 6, D), F32)],
        axis=0,
    ).astype(BF)
    r.ga[2 * D : part, :] = small
    r.ga[part + 2 * D : 2 * part, :] = small
    moves.wait(*got_x, *got_qkv)
    r.ga[0:D, :] = dot_l(r.xp[...], r.dqkv[:, 0:D]).astype(BF)
    r.ga[D : 2 * D, :] = dot_l(r.xp[...], r.dqkv[:, D : 2 * D]).astype(BF)
    r.ga[part : part + D, :] = dot_l(r.xp[...], r.dqkv[:, 2 * D : 3 * D]).astype(BF)
    moves.wait(*got_mix, *got_bg)
    r.ga[part + D : part + 2 * D, :] = dot_l(r.mix[...], r.bg[...]).astype(BF)
    start_halves(moves, r.role[1], r.ga, r.keep_out, r.send_out)
    moves.finish()


def self_inputs_body(r):
    moves = Moves(r.sems)
    got = chosen_loads(r, moves, "dqkv", r.dqkv)
    got.append(moves.start(r.w_in, r.win))
    got += chosen_loads(r, moves, "ds", r.ds)
    moves.wait(*got)

    def leave(p):
        at = rows_at(p * PR, PR)
        to = rows_at(p * SLOT, PR)
        r.dx[to, :] = r.ds[at, :] + dot_t(r.dqkv[at, :], r.win[...])
        r.dx[rows_at(p * SLOT + PR, SLOT - PR), :] = jnp.zeros((SLOT - PR, D), F32)

    loop(2 * GP, leave)
    moves.start(r.dx, r.grads_out)
    moves.finish()


def start_halves(moves, core, held, keep, send):
    half = held.shape[0] // 2
    for target, shift in ((keep, 0), (send, 1)):
        start = pl.multiple_of(((core + shift) & 1) * half, 16)
        moves.start(held.at[pl.ds(start, half), :], target)


def place_blocks(core, moves, own, other, held, firsts):
    got = []
    for group, shift in ((own, 0), (other, 1)):
        start = 0
        for ref in group:
            size = ref.shape[0]
            place = pl.multiple_of(((core + shift) & 1) * firsts + start, 16)
            got.append(moves.start(ref, held.at[pl.ds(place, size), :]))
            start += size
    return got


def place_feed_body(r):
    moves = Moves(r.sems)
    got = [
        moves.start(r.gf.at[i * D : (i + 1) * D, :], r.held.at[i * D : (i + 1) * D, :])
        for i in range(8)
    ]
    for i in range(4):
        moves.wait(got[4 + i])
        at = slice(i * D, (i + 1) * D)
        r.down[at, :] = r.held[FF + i * D : FF + (i + 1) * D, :].astype(F32)
        moves.start(r.down.at[at, :], r.down_out.at[at, :])
    moves.wait(*got[:4])
    for i in range(4):
        at = slice(i * 128, (i + 1) * 128)
        for n in range(4):
            r.up[at, n * D : (n + 1) * D] = r.held[
                n * D + i * 128 : n * D + (i + 1) * 128, :
            ].astype(F32)
        moves.start(r.up.at[at, :], r.up_out.at[at, :])
    moves.finish()


def place_rest_body(r):
    moves = Moves(r.sems)
    part = 2 * D + EXTRA
    core = r.role[1]
    got_c = place_blocks(core, moves, [r.c], [r.c_other], r.held_c, D)
    got = place_blocks(core, moves, [r.da, r.db], [r.da_other, r.db_other], r.held, part)
    moves.wait(*got_c)
    r.ca[...] = r.held_c[0:D, :].astype(F32)
    r.cb[...] = r.held_c[D : 2 * D, :].astype(F32)
    moves.start(r.ca, r.ca_out)
    moves.start(r.cb, r.cb_out)
    moves.wait(*got)
    r.wout[...] = r.held[part + D : part + 2 * D, :].astype(F32)
    moves.start(r.wout, r.out_out)
    for n, start in enumerate((0, D, part)):
        r.win[:, n * D : (n + 1) * D] = r.held[start : start + D, :].astype(F32)
    moves.start(r.win, r.in_out)
    small = r.held[2 * D : 2 * D + 16, :].astype(F32)
    for i in range(3):
        r.gains[i] = small[i : i + 1, :]
        r.biases[i] = small[3 + i : 4 + i, :]
    moves.start(r.gains, r.gains_out)
    moves.start(r.biases, r.biases_out)
    moves.finish()


ANY = pl.BlockSpec(memory_space=pl.ANY)
WHOLE = pl.BlockSpec(memory_space=pltpu.VMEM)
SCALARS = pl.BlockSpec(memory_space=pltpu.SMEM)


def in_vmem(array):
    return pltpu.with_memory_space_constraint(array, pltpu.VMEM)


class Refs:
    def __init__(self, names, refs):
        for name, ref in zip(names, refs):
            setattr(self, name, ref)


def call(body, name, flops, ins, outs, scratch, copies, aliases=None, whole=()):
    scalars = ("role", "lengths")
    specs = [SCALARS if n in scalars else WHOLE if n in whole else ANY for n in ins]
    names = [*ins, *outs, *scratch, "sems"]
    position = list(ins).index
    results = list(outs).index

    def kernel(*refs):
        body(Refs(names, refs))

    found = pl.pallas_call(
        kernel,
        out_shape=[jax.ShapeDtypeStruct(s, t) for s, t in outs.values()],
        in_specs=specs,
        out_specs=[ANY] * len(outs),
        scratch_shapes=[pltpu.VMEM(s, t) for s, t in scratch.values()]
        + [pltpu.SemaphoreType.DMA((copies,))],
        input_output_aliases={position(i): results(o) for i, o in (aliases or {}).items()},
        compiler_params=pltpu.CompilerParams(vmem_limit_bytes=60 * 1024 * 1024),
        cost_estimate=pl.CostEstimate(
            flops=flops, bytes_accessed=flops // 1000, transcendentals=0
        ),
        name=name,
    )(*ins.values())
    return dict(zip(outs, found))


def swapped(x, mask, decoders=False):
    size = lax.axis_size("dp")
    if decoders:
        pairs = [(size + i, size + (i ^ mask)) for i in range(size)]
        return lax.ppermute(x, ("pipe", "dp"), pairs)
    return lax.ppermute(x, "dp", [(i, i ^ mask) for i in range(size)])


def added(keep, recv):
    return (keep.astype(F32) + recv.astype(F32)).astype(BF)


def lowered(cur, mask, bit):
    half = cur.shape[0] // 2
    recv = swapped(lax.dynamic_slice_in_dim(cur, (1 - bit) * half, half, 0), mask)
    return added(lax.dynamic_slice_in_dim(cur, bit * half, half, 0), recv)


def raised(cur, mask, bit):
    other = swapped(cur, mask)
    return jnp.where(
        bit == 0, jnp.concatenate([cur, other], 0), jnp.concatenate([other, cur], 0)
    )


class Sums:
    def __init__(self):
        size = lax.axis_size("dp")
        place = lax.axis_index("dp")
        self.masks = [1 << i for i in range(1, size.bit_length() - 1)]
        self.bits = {mask: (place >> (mask.bit_length() - 1)) & 1 for mask in self.masks}

    def order(self, turn):
        masks = self.masks
        return masks if turn == 0 else masks[1:] + masks[:1]

    def down(self, parts, turns, first, last):
        for step in range(first, last):
            parts = [
                lowered(p, self.order(t)[step], self.bits[self.order(t)[step]])
                for p, t in zip(parts, turns)
            ]
        return parts

    def up(self, parts, turns):
        for step in reversed(range(len(self.masks))):
            parts = [
                raised(p, self.order(t)[step], self.bits[self.order(t)[step]])
                for p, t in zip(parts, turns)
            ]
        return parts


def on_device(
    embeds, lengths, attn_in, attn_out, cross_a, cross_b, ffn_up, ffn_down,
    norm_gains, norm_biases, cotangent,
):
    x, own = embeds[0], lengths[0]
    win, wout, wa, wb, wup, wdown = (
        attn_in[0], attn_out[0], cross_a[0], cross_b[0], ffn_up[0], ffn_down[0],
    )
    gains, biases = norm_gains[0], norm_biases[0]
    slots = 2 * GP * SLOT
    pipe = lax.axis_index("pipe")
    is_encoder = pipe == 0
    odd = lax.axis_index("dp") & 1
    role = jnp.stack([pipe, odd]).astype(jnp.int32)
    onward, back = [(0, 1)], [(1, 0)]

    def bf(*shape):
        return (shape, BF)

    def f32(*shape):
        return (shape, F32)

    flat, flat_f, wide, one, triple = bf(GR, D), f32(GR, D), bf(GR, FF), f32(GR, 1), bf(GR, 3 * D)
    full, slot, slot_f = f32(slots, D), bf(GP * SLOT, D), f32(GP * SLOT, D)
    square, up_w, down_w, in_w = bf(D, D), bf(D, FF), bf(FF, D), bf(D, 3 * D)
    tall, counts = bf(TALL, D), f32(48, D)
    base = dict(role=role, lengths=own, gains=gains, biases=biases)
    whole = ("gains", "biases")

    mine = lax.ppermute(jnp.where(odd == 0, wa, wb), "pipe", onward)

    fwd, mem_in, states = [], [], None
    for g in range(2):
        ins = dict(base, x_in=x, w_in=win, w_out=wout, w_up=wup, w_down=wdown, w_q=wa)
        if g:
            ins["states_in"] = states
        fwd.append(
            call(
                functools.partial(forward_body, g), f"forward_{g}", 4_000_000_000, ins,
                dict(
                    h_out=flat_f, xp_out=flat, qkv_out=triple, mix_out=flat, unit0_out=flat, sc0_out=one,
                    mem_out=flat, hb_out=flat, hid_out=wide, act_out=wide, unit1_out=flat, sc1_out=one,
                    unit2_out=flat, sc2_out=one, q_out=flat, states_out=full,
                ),
                dict(
                    q=flat, wq=square, x=slot, win=in_w, wout=square, wup=up_w, wdown=down_w, h=flat_f, xp=flat,
                    qkv=bf(TALL, 3 * D), mix=flat, unit0=flat, sc0=one, mem=flat, hb=flat, hid=wide,
                    act=wide, unit1=flat, sc1=one, unit2=flat, sc2=one, state=flat_f, states=slot_f,
                ),
                36, aliases={"states_in": "states_out"} if g else None, whole=whole,
            )
        )
        states = fwd[g]["states_out"]
        memory = fwd[g]["mem_out"]
        if g == 0:
            mine, memory = lax.optimization_barrier((mine, memory))
            other = swapped(mine, 1)
        mem_in.append(lax.ppermute(memory, "pipe", onward))

    dec, gmem_in = [], []
    for g in range(2):
        dec.append(
            call(
                functools.partial(decode_body, g), f"decode_{g}", 8_000_000_000,
                dict(
                    base, h_in=fwd[g]["h_out"], q_in=fwd[g]["q_out"], mem=in_vmem(mem_in[g]), cot_in=cotangent, wo_in=wb,
                    mine_in=in_vmem(mine), other_in=in_vmem(other), w_up=wup, w_down=wdown, states_in=states,
                ),
                dict(
                    states_out=full, gmem_out=flat, dh_out=flat_f, dq_out=flat, mix_out=flat,
                    bg1_out=flat, dk_out=flat, dv_out=flat, hb_out=flat, dhid_out=wide, act_out=wide,
                    bg2_out=flat, gb_out=counts,
                ),
                dict(
                    kept=bf(GP * 4 * PR, 2 * SLOT), h=flat_f, cot=slot, wo=square, wkv=bf(2 * D, D), wup=up_w,
                    wdown=down_w, states=slot_f, gmem=flat, q=tall, k=flat, v=flat, mix=flat,
                    dq=flat, dk=flat, dv=flat, bg1=flat, hb=flat, hid=wide, dhid=wide, act=wide, bg2=flat,
                    unit1=flat, sc1=one, valid=one, ds=flat_f, gm=tall, gb=counts,
                ),
                36, aliases={"states_in": "states_out"}, whole=whole + ("mem", "mine_in", "other_in"),
            )
        )
        states = dec[g]["states_out"]
        gmem_in.append(lax.ppermute(dec[g]["gmem_out"], "pipe", back))

    def of(group, results, **names):
        return {f"{k}_{group}": results[v] for k, v in names.items()}

    enc_names = dict(
        unit2="unit2_out", sc2="sc2_out", unit1="unit1_out", sc1="sc1_out", hid="hid_out",
    )
    self_names = dict(unit0="unit0_out", sc0="sc0_out", qkv="qkv_out")
    back_scratch = dict(
        unit2=flat, sc2=one, unit1=flat, sc1=one, wdown=down_w, hid=wide, wup=up_w, dh=flat_f,
    )
    self_scratch = dict(
        unit0=flat, sc0=one, wout=square, qkv=bf(TALL, 3 * D), bg=flat, gm=tall, dqkv=triple, gb=counts,
    )
    dec_names = dict(
        dk="dk_out", dv="dv_out", dq="dq_out", mixc="mix_out", bg1="bg1_out", hb2="hb_out",
        dhid2="dhid_out", act2="act_out", bg2="bg2_out",
    )
    all_flat, all_wide = bf(ALL, D), bf(ALL, FF)
    cross_names = {k: v for k, v in dec_names.items() if k in ("dk", "dv", "dq", "mixc", "bg1")}
    feed_names = {k: v for k, v in dec_names.items() if k not in cross_names}
    ins = dict(
        base, w_up=wup, w_down=wdown, w_out=wout, gmem=in_vmem(gmem_in[0]),
        hb_0=fwd[0]["hb_out"], act_0=fwd[0]["act_out"],
    )
    ins.update(of(0, fwd[0], **enc_names, **self_names))
    for g in range(2):
        ins.update(of(g, dec[g], **feed_names))
    feed_scratch = dict(
        gf=bf(2 * FF, D), hb=tall, act=bf(TALL, FF), fbg=tall, dhid=bf(TALL, FF),
    )
    feed_outs = dict(gf_out=bf(2 * FF, D))
    cross = call(
        cross_body, "cross_back", 1_000, ins,
        dict(
            ds_out=flat_f, bg_out=flat, dqkv_out=triple, gb_out=counts, **feed_outs,
        ),
        dict(
            **back_scratch, **self_scratch, **feed_scratch,
            all_hb2=all_flat, all_dhid2=all_wide, all_act2=all_wide, all_bg2=all_flat,
        ),
        40, whole=whole + ("gmem",),
    )
    ins = dict(role=role)
    for g in range(2):
        ins.update(of(g, dec[g], **cross_names))
        ins[f"fb_{g}"] = fwd[g]["hb_out"]
        ins[f"mem_{g}"] = mem_in[g]
    ins["dk_1"], gf = lax.optimization_barrier((ins["dk_1"], cross["gf_out"]))
    crossed = call(
        cross_grads_body, "cross_grads", 1_000, ins,
        dict(keep_out=bf(2 * D, D), send_out=bf(2 * D, D)),
        dict(
            **{"all_" + n: all_flat for n in ("mem", "fb", *cross_names)}, gx=bf(2 * D, D), gc=bf(2 * D, D),
        ),
        32,
    )
    crossed_keep, crossed_send, gf = lax.optimization_barrier(
        (crossed["keep_out"], crossed["send_out"], gf)
    )
    crossed_sent = swapped(crossed_send, 1, True)

    ins = dict(
        base, w_up=wup, w_down=wdown, w_out=wout, gmem=in_vmem(gmem_in[1]), hb_1=fwd[1]["hb_out"],
        act_1=fwd[1]["act_out"], dh_in=dec[1]["dh_out"], gf_in=gf,
    )
    ins.update(of(1, fwd[1], **enc_names))
    feed = call(
        feed_body, "feed_back", 1_000, ins,
        dict(dh_out=flat_f, gb_out=counts, **feed_outs),
        dict(**back_scratch, **feed_scratch, gb=counts),
        32, aliases={name + "_in": name + "_out" for name in ("dh", "gf")}, whole=whole + ("gmem",),
    )
    gf = lax.psum(feed["gf_out"], "dp")
    crossed_x = added(crossed_keep[:D], crossed_sent[:D])
    crossed_c = added(crossed_keep[D:], crossed_sent[D:])
    sums = Sums()
    depth = len(sums.masks)
    part = 2 * D + EXTRA

    def tail():
        last = call(
            self_body, "self_back", 3_000_000_000,
            dict(
                base, dh_0=dec[0]["dh_out"], dh_1=feed["dh_out"], w_out=wout, w_q=wa,
                **of(0, dec[0], dq="dq_out"), **of(1, dec[1], dq="dq_out"),
                **of(0, fwd[0], **self_names), **of(1, fwd[1], **self_names),
            ),
            dict(
                ds_out=flat_f, bg_out=flat, dqkv_out=triple, gb_out=counts,
                ds0_out=flat_f, bg0_out=flat, dqkv0_out=triple,
            ),
            dict(
                **self_scratch, dh=flat_f, dq=flat, wq=square, dh_first=flat_f, dq_first=flat,
                **{n + "_first": self_scratch[n] for n in self_scratch if n != "gb"},
            ),
            48, whole=whole,
        )
        gx_in = lax.ppermute(crossed_x, "pipe", back)
        gx_in, last["bg_out"] = lax.optimization_barrier((gx_in, last["bg_out"]))
        ds = last["ds_out"]
        c_keep = jnp.where(is_encoder, gx_in, crossed_c)
        early = sums.down([c_keep], (0,), 0, 1)
        dqkv = dict(dqkv_enc=cross["dqkv_out"], dqkv_dec=last["dqkv0_out"], dqkv_1=last["dqkv_out"])
        ins = dict(
            role=role, gb_cross=cross["gb_out"], gb_dec0=dec[0]["gb_out"], gb_dec1=dec[1]["gb_out"],
            gb_feed=feed["gb_out"], gb_self=last["gb_out"], bg_enc=cross["bg_out"],
            bg_dec=last["bg0_out"], bg_1=last["bg_out"], **dqkv,
        )
        for g in range(2):
            ins.update(of(g, fwd[g], xp="xp_out", mix="mix_out"))
        found = call(
            self_weights_body, "self_weights", 4_000_000_000, ins,
            dict(keep_out=bf(part, D), send_out=bf(part, D)),
            dict(bg=all_flat, dqkv=bf(ALL, 3 * D), xp=all_flat, mix=all_flat, ga=bf(2 * part, D)),
            20, whole=("gb_cross", "gb_dec0", "gb_dec1", "gb_feed", "gb_self"),
        )
        found |= call(
            self_inputs_body, "self_inputs", 6_000_000_000,
            dict(
                role=role, w_in=win, ds_enc=cross["ds_out"], ds_dec=last["ds0_out"], ds_1=ds, **dqkv,
            ),
            dict(grads_out=full),
            dict(ds=f32(ALL, D), dqkv=bf(ALL, 3 * D), win=in_w, dx=full),
            12,
        )
        a_keep = added(found["keep_out"], swapped(found["send_out"], 1))
        early = sums.down(early, (0,), 1, depth)
        late = sums.down([a_keep[:D], a_keep[D:]], (0, 1), 0, 1)
        late, grads = lax.optimization_barrier((late, found["grads_out"]))
        late = sums.down(late, (0, 1), 1, depth)
        parts = sums.up(early + late, (0, 0, 1))
        return grads, parts, [swapped(p, 1) for p in parts]

    shapes = jax.eval_shape(tail)
    input_grads, parts, others = lax.cond(
        own[0] >= 0,
        tail,
        lambda: jax.tree.map(lambda leaf: jnp.zeros(leaf.shape, leaf.dtype), shapes),
    )
    placed = call(
        place_rest_body, "place_rest", 1_000_000_000,
        dict(
            role=role, c=parts[0], da=parts[1], db=parts[2],
            c_other=others[0], da_other=others[1], db_other=others[2],
        ),
        dict(
            in_out=f32(D, 3 * D), out_out=f32(D, D), gains_out=f32(3, 1, D), biases_out=f32(3, 1, D),
            ca_out=f32(D, D), cb_out=f32(D, D),
        ),
        dict(
            held=bf(2 * part, D), win=f32(D, 3 * D), wout=f32(D, D), gains=f32(3, 1, D), biases=f32(3, 1, D),
            held_c=bf(2 * D, D), ca=f32(D, D), cb=f32(D, D),
        ),
        16,
    )
    placed |= call(
        place_feed_body, "place_feed", 1_000_000_000,
        dict(gf=gf),
        dict(up_out=f32(D, FF), down_out=f32(FF, D)),
        dict(held=bf(2 * FF, D), up=f32(D, FF), down=f32(FF, D)),
        16,
    )
    outs = (
        states, input_grads, placed["in_out"], placed["out_out"], placed["ca_out"], placed["cb_out"],
        placed["up_out"], placed["down_out"],
    )
    small = (placed["gains_out"], placed["biases_out"])
    return tuple(out[None] for out in outs) + tuple(out.transpose(1, 0, 2) for out in small)


def solution(mesh):
    cut = P("pipe", "dp", None)
    held = P("pipe", None, None)
    return jax.shard_map(
        on_device,
        mesh=mesh,
        in_specs=(cut, P("pipe", "dp")) + (held,) * 8 + (P("dp", None),),
        out_specs=(cut, cut) + (held,) * 8,
        check_vma=False,
    )
```
